32 devices in a mesh: section: 2 (over x), row: 4 (over y, core), mp: 4 (over z).
Axes of the slice: x: 2, y: 2, z: 4, core: 2. Of those that a mesh axis runs over, the one named last changes fastest.
Arguments:
- layer_input: bfloat16 [5, 3136, 512], P(None, ('row', 'mp')), may hold values from -6 to 6
- out_cotangent: bfloat16 [5, 3136, 512], P(None, ('row', 'mp')), may hold values from -6 to 6
- norm_one_gain: float32 [2, 512], P('section'), may hold values from 0.5 to 1.5
- norm_one_bias: float32 [2, 512], P('section'), may hold values from -3 to 3
- attend_weight: bfloat16 [2, 512, 16, 96], P('section', None, 'mp'), may hold values from -0.25 to 0.25
- attend_bias: float32 [2, 16, 64], P('section', 'mp'), may hold values from -3 to 3
- position_table: float32 [2, 16, 169], P('section', 'mp'), may hold values from -4 to 4
- output_weight: bfloat16 [2, 16, 32, 512], P('section', 'mp'), may hold values from -2 to 2
- output_bias: float32 [2, 512], P('section'), may hold values from -3 to 3
- norm_two_gain: float32 [2, 512], P('section'), may hold values from 0.5 to 1.5
- norm_two_bias: float32 [2, 512], P('section'), may hold values from -3 to 3
- expand_weight: bfloat16 [2, 512, 2048], P('section', None, 'mp'), may hold values from -0.25 to 0.25
- expand_bias: float32 [2, 2048], P('section', 'mp'), may hold values from -3 to 3
- reduce_weight: bfloat16 [2, 2048, 512], P('section', 'mp'), may hold values from -0.1875 to 0.1875
- reduce_bias: float32 [2, 512], P('section'), may hold values from -3 to 3
Outputs:
- layer_outputs: bfloat16 [2, 5, 3136, 512], P('section', None, ('row', 'mp'))
- input_grads: float32 [2, 5, 3136, 512], P('section', None, ('row', 'mp'))
- grad_norm_one_gain: float32 [2, 512], P('section')
- grad_norm_one_bias: float32 [2, 512], P('section')
- grad_attend_weight: float32 [2, 512, 16, 96], P('section', None, 'mp')
- grad_attend_bias: float32 [2, 16, 64], P('section', 'mp')
- grad_position_table: float32 [2, 16, 169], P('section', 'mp')
- grad_output_weight: float32 [2, 16, 32, 512], P('section', 'mp')
- grad_output_bias: float32 [2, 512], P('section')
- grad_norm_two_gain: float32 [2, 512], P('section')
- grad_norm_two_bias: float32 [2, 512], P('section')
- grad_expand_weight: float32 [2, 512, 2048], P('section', None, 'mp')
- grad_expand_bias: float32 [2, 2048], P('section', 'mp')
- grad_reduce_weight: float32 [2, 2048, 512], P('section', 'mp')
- grad_reduce_bias: float32 [2, 512], P('section')
The draws below stay inside these ranges and needn't reach their ends.
All inputs are finite; a program needn't handle non-finite values.
Results may differ from the reference program's by a relative error of at most 0.039.
Values may be sent and summed in bfloat16 or wider, within the bound.
No kernel may reach another device: no remote copies, remote signals or barrier semaphores. Data moves between devices by JAX's collectives and lax.ppermute only.
A program may use at most 192 MiB of HBM per device.

```python
import jax
import jax.numpy as jnp
from jax import lax

D = 512
HEADS = 16
HEAD_DIM = 32
FF = 2048
WIN = 7
SHIFT = 3
IMGS = 1
MB = 5
HEIGHT = 56
WIDTH = 56
TOK_MB = 3136
TABLE = 169


def steps_of(own_key, shape, cuts, least, largest):
    def one(axis_at, parts):
        steps = jax.random.uniform(jax.random.fold_in(jax.random.fold_in(own_key, 6), axis_at), (parts,), jnp.float32, least / len(cuts), largest / len(cuts))
        return jnp.repeat(jnp.exp(steps), shape[axis_at] // parts).reshape((-1,) + (1,) * (len(shape) - axis_at - 1))

    factor_of = one(*cuts[0])
    for cut in cuts[1:]:
        factor_of = factor_of * one(*cut)
    return factor_of


def normal_values(rng, extent, scale, reach, shards=(), kind=jnp.bfloat16):
    result = jax.random.normal(rng, extent, jnp.float32) * scale
    if len(shards) > 0:
        result = steps_of(rng, extent, shards, -0.22, 0.18) * result
    return jnp.clip(result, min=-reach, max=reach).astype(kind)


def setup_inputs(seed: int = 0) -> dict:
    key_of = jax.random.split(jax.random.key(seed), 16)
    return {
        "layer_input": normal_values(key_of[0], (MB, TOK_MB, D), 1.0, 6.0, ((1, 16),)),
        "out_cotangent": normal_values(key_of[1], (MB, TOK_MB, D), 1.0, 6.0, ((1, 16),)),
        "norm_one_gain": jnp.clip(1.0 + 0.1 * jax.random.normal(key_of[2], (2, D), jnp.float32), 0.5, 1.5),
        "norm_one_bias": normal_values(key_of[3], (2, D), 0.5, 3.0, ((0, 2),), jnp.float32),
        "attend_weight": normal_values(key_of[4], (2, D, HEADS, 3 * HEAD_DIM), D ** -0.5, 0.25, ((0, 2), (2, 4))),
        "attend_bias": normal_values(key_of[5], (2, HEADS, 2 * HEAD_DIM), 0.5, 3.0, ((0, 2), (1, 4)), jnp.float32),
        "position_table": normal_values(key_of[6], (2, HEADS, TABLE), 1.0, 4.0, ((0, 2), (1, 4)), jnp.float32),
        "output_weight": normal_values(key_of[7], (2, HEADS, HEAD_DIM, D), (max(D // (WIN * WIN), 1)) ** -0.5, 2.0, ((0, 2), (1, 4))),
        "output_bias": normal_values(key_of[8], (2, D), 0.5, 3.0, ((0, 2),), jnp.float32),
        "norm_two_gain": jnp.clip(1.0 + 0.1 * jax.random.normal(key_of[9], (2, D), jnp.float32), 0.5, 1.5),
        "norm_two_bias": normal_values(key_of[10], (2, D), 0.5, 3.0, ((0, 2),), jnp.float32),
        "expand_weight": normal_values(key_of[11], (2, D, FF), D ** -0.5, 0.25, ((0, 2), (2, 4))),
        "expand_bias": normal_values(key_of[12], (2, FF), 0.5, 3.0, ((0, 2), (1, 4)), jnp.float32),
        "reduce_weight": normal_values(key_of[13], (2, FF, D), (FF // 2) ** -0.5, 0.1875, ((0, 2), (1, 4))),
        "reduce_bias": normal_values(key_of[14], (2, D), 0.5, 3.0, ((0, 2),), jnp.float32),
    }


@jax.custom_vjp
def low(v):
    return lax.optimization_barrier(v.astype(jnp.bfloat16)).astype(jnp.float32)

@jax.custom_vjp
def low_back(v):
    return v

def low_keep(v):
    return (low(v), None)

def low_pass(kept, grad):
    return (grad,)

def back_keep(v):
    return (v, None)

def back_low(kept, grad):
    return (low(grad),)
low.defvjp(low_keep, low_pass)
low_back.defvjp(back_keep, back_low)
precise = lax.Precision.HIGHEST
layer_eps = 1e-05

def normalize(values, norm_gain, norm_shift):
    middle = lax.optimization_barrier(jnp.mean(values, axis=-1, keepdims=True))
    centred = values - middle
    spread = lax.optimization_barrier(jnp.mean(centred * centred, axis=-1, keepdims=True))
    return centred * lax.rsqrt(spread + layer_eps) * norm_gain + norm_shift

def table_index():
    places = jnp.arange(WIN * WIN, dtype=jnp.int32)
    row_place = places // WIN
    col_place = places % WIN
    return (row_place[:, None] - row_place[None, :] + WIN - 1) * (2 * WIN - 1) + col_place[:, None] - col_place[None, :] + WIN - 1

def region_term():
    heights = jnp.arange(HEIGHT, dtype=jnp.int32)
    widths = jnp.arange(WIDTH, dtype=jnp.int32)
    row_ids = (heights >= HEIGHT - WIN).astype(jnp.int32) + (heights >= HEIGHT - SHIFT).astype(jnp.int32)
    col_ids = (widths >= WIDTH - WIN).astype(jnp.int32) + (widths >= WIDTH - SHIFT).astype(jnp.int32)
    labels = row_ids[:, None] * 3 + col_ids[None, :]
    labels = labels.reshape(HEIGHT // WIN, WIN, WIDTH // WIN, WIN).transpose(0, 2, 1, 3).reshape(-1, WIN * WIN)
    return jnp.where(labels[:, :, None] == labels[:, None, :], 0.0, -100.0).astype(jnp.float32)

def swin_layer(image, params, shifted):
    gain_one, bias_one, attend_matrix, attend_shift, table_bias, output_matrix, output_shift, gain_two, bias_two, expand_matrix, expand_shift, reduce_matrix, reduce_shift = params
    normed = low(normalize(image, gain_one, bias_one))
    if shifted:
        normed = jnp.roll(normed, (-SHIFT, -SHIFT), (0, 1))
    windows = normed.reshape(HEIGHT // WIN, WIN, WIDTH // WIN, WIN, D).transpose(0, 2, 1, 3, 4).reshape(-1, WIN * WIN, D)
    projected = jnp.einsum('wtd,dhe->wthe', windows, attend_matrix, precision=precise)
    queries = low(low_back(projected[..., :HEAD_DIM] + attend_shift[:, :HEAD_DIM]) * HEAD_DIM ** (-0.5))
    key_part = low(low_back(projected[..., HEAD_DIM:2 * HEAD_DIM]))
    value_part = low(low_back(projected[..., 2 * HEAD_DIM:] + attend_shift[:, HEAD_DIM:]))
    scores = jnp.einsum('wqhe,wkhe->whqk', queries, key_part, precision=precise) + table_bias[:, table_index()][None]
    if shifted:
        scores = scores + region_term()[:, None]
    soft_weights = jax.nn.softmax(low_back(scores), axis=-1)
    context = low(low_back(jnp.einsum('whqk,wkhe->wqhe', low(soft_weights), value_part, precision=precise)))
    context = context.reshape(HEIGHT // WIN, WIDTH // WIN, WIN, WIN, D).transpose(0, 2, 1, 3, 4).reshape(HEIGHT, WIDTH, D)
    if shifted:
        context = jnp.roll(context, (SHIFT, SHIFT), (0, 1))
    attended = low_back(jnp.dot(context, output_matrix.reshape(D, D), precision=precise) + output_shift)
    middle = image + attended
    normed_two = low(normalize(middle, gain_two, bias_two))
    hidden = low_back(jnp.dot(normed_two, expand_matrix, precision=precise) + expand_shift)
    active = low(jax.nn.gelu(hidden, approximate=False))
    return middle + low_back(jnp.dot(active, reduce_matrix, precision=precise) + reduce_shift)

def to_images(values):
    return values.reshape(MB, HEIGHT, IMGS, WIDTH, D).transpose(0, 2, 1, 3, 4).reshape(MB * IMGS, HEIGHT, WIDTH, D)

def from_images(values):
    return values.reshape(MB, IMGS, HEIGHT, WIDTH, D).transpose(0, 2, 1, 3, 4).reshape(MB, TOK_MB, D)

def reference(layer_input, out_cotangent, norm_one_gain, norm_one_bias, attend_weight, attend_bias, position_table, output_weight, output_bias, norm_two_gain, norm_two_bias, expand_weight, expand_bias, reduce_weight, reduce_bias):
    stacked = (norm_one_gain, norm_one_bias, attend_weight, attend_bias, position_table, output_weight, output_bias, norm_two_gain, norm_two_bias, expand_weight, expand_bias, reduce_weight, reduce_bias)
    params_first = tuple((member[0].astype(jnp.float32) for member in stacked))
    params_second = tuple((member[1].astype(jnp.float32) for member in stacked))
    images = to_images(layer_input.astype(jnp.float32))
    cotangent_images = to_images(out_cotangent.astype(jnp.float32))

    def run_layers(inputs, offsets, layer_first, layer_second):

        def one_image(image_pair):
            image_in, offset_in = image_pair
            first_out = low_back(low(swin_layer(image_in, layer_first, False)) + offset_in)
            return (first_out, swin_layer(first_out, layer_second, True))
        firsts, seconds = lax.map(jax.checkpoint(one_image), (inputs, offsets))
        return (seconds, firsts)
    seconds, backward_fn, firsts = jax.vjp(run_layers, images, jnp.zeros_like(images), params_first, params_second, has_aux=True)
    grad_input, grad_middle, grads_first, grads_second = backward_fn(cotangent_images)
    layer_outputs = jnp.stack([from_images(firsts), from_images(seconds)]).astype(jnp.bfloat16)
    input_grads = jnp.stack([from_images(grad_input), from_images(grad_middle)])
    weight_grads = tuple((jnp.stack([grads_first[number], grads_second[number]]) for number in range(13)))
    return (layer_outputs, input_grads, weight_grads[0], weight_grads[1], weight_grads[2], weight_grads[3], weight_grads[4], weight_grads[5], weight_grads[6], weight_grads[7], weight_grads[8], weight_grads[9], weight_grads[10], weight_grads[11], weight_grads[12])
```

```python
import functools

import jax
import jax.numpy as jnp
import numpy as np
from jax import lax
from jax.experimental import pallas as pl
from jax.experimental.pallas import tpu as pltpu
from jax.sharding import PartitionSpec as P

WIN = 7
SHIFT = 3
WCOLS = 8
WROWS = 2
TOKENS = WIN * WIN
SLOT = 64
GROUP = 4
AXES = ("section", "row", "mp")
EPS = 1e-05
BF = jnp.bfloat16
F32 = jnp.float32
NN = (((1,), (0,)), ((), ()))
NT = (((1,), (1,)), ((), ()))
TN = (((0,), (0,)), ((), ()))
VMEM_LIMIT = 56 * 1024 * 1024
highest = lax.Precision.HIGHEST


def mm(left, right, dims=NN):
    return lax.dot_general(left, right, dims, preferred_element_type=F32)


def up16(count):
    return -(-count // 16) * 16


def patch_place(row, col):
    return (col // WIN) * SLOT + row * WIN + col % WIN


class Tables:
    def __init__(self, wins):
        self.wins = wins
        self.rows = wins * SLOT
        cols = wins * WIN
        wide = range(SHIFT, cols)
        thin = range(SHIFT)
        low, high = range(SHIFT, WIN), range(SHIFT)
        pieces = [(low, wide), (high, wide), (low, thin), (high, thin)]
        self.sizes = [up16(len(a) * len(b)) for a, b in pieces]
        self.total = sum(self.sizes)
        pick = np.zeros((self.total, self.rows), np.float32)
        put = np.zeros((self.rows, self.total), np.float32)
        at = 0
        for (rows, columns), size in zip(pieces, self.sizes):
            spot = at
            for row in rows:
                for col in columns:
                    pick[spot, patch_place(row, col)] = 1
                    put[patch_place((row - SHIFT) % WIN, (col - SHIFT) % cols), spot] = 1
                    spot += 1
            at += size
        self.pick, self.put = pick, put


def pair_tables(wins):
    cols = wins * WIN
    tokens = WIN * cols
    keep = np.zeros((2, wins * SLOT, tokens), np.float32)
    take = np.zeros((2, wins * SLOT, up16(SHIFT * cols)), np.float32)
    send = np.zeros((up16(SHIFT * cols), tokens), np.float32)
    for seg in range(SHIFT):
        for col in range(cols):
            send[seg * cols + col, (2 * seg + 1) * cols + col] = 1
    for side in range(2):
        for row in range(WIN):
            for col in range(cols):
                place = patch_place(row, col)
                own = row <= SHIFT if side == 0 else row >= SHIFT
                if own:
                    seg = row if side == 0 else row - SHIFT
                    keep[side, place, 2 * seg * cols + col] = 1
                else:
                    seg = row - SHIFT - 1 if side == 0 else row
                    take[side, place, seg * cols + col] = 1
    return keep, take, send


class Layout:
    def __init__(self, row_count, mp_count):
        self.row_count, self.mp_count = row_count, mp_count
        self.across = mp_count // WROWS
        self.wins = WCOLS // self.across
        self.high = row_count * WROWS

    def device(self, section, window_row, place):
        window_row, place = window_row % self.high, place % self.across
        row = window_row // WROWS
        return (section * self.row_count + row) * self.mp_count + (window_row % WROWS) * self.across + place

    def route(self, source, target, up, back):
        return [
            (self.device(source, window_row, place), self.device(target, window_row - up, place - back))
            for window_row in range(self.high)
            for place in range(self.across)
        ]


HALO = ((0, 0), (1, 0), (0, 1), (1, 1))


def forward_halo(layout, parts, source):
    return [lax.ppermute(part, AXES, layout.route(source, 1, *by)) if (source, by) != (1, (0, 0)) else part for part, by in zip(parts, HALO)]


def backward_halo(layout, parts, target):
    result = []
    for part, by in zip(parts, HALO):
        if (target, by) == (1, (0, 0)):
            result.append(part)
        else:
            result.append(lax.ppermute(part, AXES, [(b, a) for a, b in layout.route(target, 1, *by)]))
    return result


def head_masks(dtype):
    lane = lax.broadcasted_iota(jnp.int32, (1, GROUP * 32), 1)
    return [jnp.where(lane // 32 == h, 1.0, 0.0).astype(dtype) for h in range(GROUP)]


def spread_heads(block, masks):
    return jnp.concatenate([block * mask for mask in masks], axis=0)


def fold_heads(tall, masks):
    total = tall[:SLOT] * masks[0]
    for h in range(1, GROUP):
        total = total + tall[h * SLOT : (h + 1) * SLOT] * masks[h]
    return total


def centre(values):
    middle = jnp.mean(values, axis=-1, keepdims=True)
    centred = values - middle
    scale = lax.rsqrt(jnp.mean(centred * centred, axis=-1, keepdims=True) + EPS)
    return centred * scale, scale


def forward_kernel(
    wins, sec, pin, p_main, p_row, p_col, p_cor, put, pick, wq_h, wo_h, w1_h, w2_h, vec, bq, b1, bias, region,
    y, s_main, s_row, s_col, s_cor, x_o, a_o, qkv_o, prob_o, ctx_o, mid_o, n2_o, act_o, gp_o,
    wq, wo, w1, w2, sems,
):
    copies = [pltpu.make_async_copy(src, dst, sems.at[i]) for i, (src, dst) in enumerate(((wq_h, wq), (wo_h, wo), (w1_h, w1), (w2_h, w2)))]
    for copy in copies:
        copy.start()

    @pl.when(sec[0] == 0)
    def _():
        x_o[...] = pin[0]

    @pl.when(sec[0] == 1)
    def _():
        joined = jnp.concatenate([p_main[...], p_row[...], p_col[...], p_cor[...]], axis=0)
        x_o[...] = mm(put[...], joined).astype(BF)

    def norm_one(w, carry):
        rows = pl.ds(pl.multiple_of(w * SLOT, SLOT), SLOT)
        hat, _ = centre(x_o[rows, :].astype(F32))
        a_o[rows, :] = (hat * vec[0:1, :] + vec[1:2, :]).astype(BF)
        return carry

    lax.fori_loop(0, wins, norm_one, 0)
    copies[0].wait()
    lane = lax.broadcasted_iota(jnp.int32, (1, 3 * GROUP * 32), 1)
    factor = jnp.where(lane < GROUP * 32, 32 ** (-0.5), 1.0)
    for g in range(4):
        cols = slice(g * 384, (g + 1) * 384)
        pr = mm(a_o[...], wq[g]) + bq[g : g + 1, :]
        qkv_o[:, cols] = (pr * factor).astype(BF)

    masks, masks_f = head_masks(BF), head_masks(F32)

    def attend(w, carry):
        rows = pl.ds(pl.multiple_of(w * SLOT, SLOT), SLOT)
        for g in range(4):
            q = qkv_o[rows, g * 384 : g * 384 + 128]
            k = qkv_o[rows, g * 384 + 128 : g * 384 + 256]
            v = qkv_o[rows, g * 384 + 256 : g * 384 + 384]
            scores = mm(k, spread_heads(q, masks), NT) + bias[g] + region[w]
            top = jnp.max(scores, axis=0, keepdims=True)
            e = jnp.exp(scores - top)
            prob = (e * (1.0 / jnp.sum(e, axis=0, keepdims=True))).astype(BF)
            prob_o[rows, g * 256 : (g + 1) * 256] = prob
            ctx_o[rows, g * 128 : (g + 1) * 128] = fold_heads(mm(prob, v, TN), masks_f).astype(BF)
        return carry

    lax.fori_loop(0, wins, attend, 0)
    copies[1].wait()
    mid_o[...] = x_o[...].astype(F32) + (mm(ctx_o[...], wo[...]) + vec[2:3, :])

    def norm_two(w, carry):
        rows = pl.ds(pl.multiple_of(w * SLOT, SLOT), SLOT)
        hat, _ = centre(mid_o[rows, :])
        n2_o[rows, :] = (hat * vec[3:4, :] + vec[4:5, :]).astype(BF)
        return carry

    lax.fori_loop(0, wins, norm_two, 0)
    copies[2].wait()
    copies[3].wait()
    parts, _, width = w1.shape
    total = mid_o[...] + vec[5:6, :]
    for j in range(parts):
        cols = slice(j * width, (j + 1) * width)
        hidden = mm(n2_o[...], w1[j]) + b1[j : j + 1, :]
        phi = 0.5 + 0.5 * lax.erf(hidden * 0.7071067811865476)
        act = (hidden * phi).astype(BF)
        act_o[:, cols] = act
        gp_o[:, cols] = (phi + hidden * (jnp.exp(hidden * hidden * -0.5) * 0.3989422804014327)).astype(BF)
        total = total + mm(act, w2[j])
    out = total.astype(BF)
    y[...] = out
    picked = mm(pick[...], out).astype(BF)
    at = 0
    for ref in (s_main, s_row, s_col, s_cor):
        ref[...] = picked[at : at + ref.shape[0]]
        at += ref.shape[0]


def norm_back(grad, hat, scale, gain):
    inner = grad * gain
    return scale * (inner - jnp.mean(inner, axis=-1, keepdims=True) - hat * jnp.mean(inner * hat, axis=-1, keepdims=True))


def backward_kernel(
    wins, sec, g_main, g_row, g_col, g_cor, c_main, c_row, c_col, c_cor, put, pick, wq_h, wo_h, w1_h, w2_h, vec,
    x0, qkv0, prob0, mid0, gp0, x1, qkv1, prob1, mid1, gp1,
    dx_o, s_main, s_row, s_col, s_cor, g_o, dh_o, gm_o, dqkv_o, small, dbias,
    wq, wo, w1, w2, x, qkv, prob, mid, gp, dmid, dn, dctx, sems,
):
    weights = [pltpu.make_async_copy(src, dst, sems.at[i]) for i, (src, dst) in enumerate(((w2_h, w2), (w1_h, w1), (wo_h, wo), (wq_h, wq)))]
    for copy in weights:
        copy.start()
    kept = (gp, mid, qkv, prob, x)
    olds = [pltpu.make_async_copy(src, dst, sems.at[4 + i]) for i, (src, dst) in enumerate(zip((gp0, mid0, qkv0, prob0, x0), kept))]
    news = [pltpu.make_async_copy(src, dst, sems.at[4 + i]) for i, (src, dst) in enumerate(zip((gp1, mid1, qkv1, prob1, x1), kept))]

    @pl.when(sec[0] == 0)
    def _():
        for copy in olds:
            copy.start()
        joined = jnp.concatenate([g_main[...], g_row[...], g_col[...], g_cor[...]], axis=0)
        g_o[...] = mm(pick[...], joined, TN).astype(BF)

    @pl.when(sec[0] == 1)
    def _():
        for copy in news:
            copy.start()
        joined = jnp.concatenate([c_main[0], c_row[0], c_col[0], c_cor[0]], axis=0)
        g_o[...] = mm(put[...], joined).astype(BF)

    small[...] = jnp.zeros_like(small)
    parts, _, width = w1.shape
    weights[0].wait()
    weights[1].wait()
    olds[0].wait()
    for j in range(parts):
        cols = slice(j * width, (j + 1) * width)
        dh = (mm(g_o[...], w2[j], NT) * gp[:, cols].astype(F32)).astype(BF)
        dh_o[:, cols] = dh
        small[0:1, cols] = jnp.sum(dh.astype(F32), axis=0, keepdims=True)
        part = mm(dh, w1[j], NT)
        if j == 0:
            dn[...] = part
        else:
            dn[...] += part
    olds[1].wait()

    def middle(w, carry):
        rows = pl.ds(pl.multiple_of(w * SLOT, SLOT), SLOT)
        grad = dn[rows, :]
        out = g_o[rows, :].astype(F32)
        hat, scale = centre(mid[rows, :])
        result = out + norm_back(grad, hat, scale, vec[3:4, :])
        dmid[rows, :] = result
        low = result.astype(BF)
        gm_o[rows, :] = low
        small[1:2, 0:512] += jnp.sum(out, axis=0, keepdims=True)
        small[1:2, 512:1024] += jnp.sum(low.astype(F32), axis=0, keepdims=True)
        small[2:3, 0:512] += jnp.sum(grad * hat, axis=0, keepdims=True)
        small[2:3, 512:1024] += jnp.sum(grad, axis=0, keepdims=True)
        return carry

    lax.fori_loop(0, wins, middle, 0)
    weights[2].wait()
    dctx[...] = mm(gm_o[...], wo[...], NT).astype(BF)
    olds[2].wait()
    olds[3].wait()
    dbias[...] = jnp.zeros_like(dbias)
    masks, masks_f = head_masks(BF), head_masks(F32)

    def attend(w, carry):
        rows = pl.ds(pl.multiple_of(w * SLOT, SLOT), SLOT)
        for g in range(4):
            q = qkv[rows, g * 384 : g * 384 + 128]
            k = qkv[rows, g * 384 + 128 : g * 384 + 256]
            v = qkv[rows, g * 384 + 256 : g * 384 + 384]
            do = spread_heads(dctx[rows, g * 128 : (g + 1) * 128], masks)
            low = prob[rows, g * 256 : (g + 1) * 256]
            p = low.astype(F32)
            dp = mm(v, do, NT)
            ds = (p * (dp - jnp.sum(p * dp, axis=0, keepdims=True))).astype(BF)
            dbias[:, g * 256 : (g + 1) * 256] += ds.astype(F32)
            dv = mm(low, do).astype(BF)
            dk = mm(ds, spread_heads(q, masks)).astype(BF)
            dq = (fold_heads(mm(ds, k, TN), masks_f) * 32 ** (-0.5)).astype(BF)
            dqkv_o[rows, g * 384 : g * 384 + 128] = dq
            dqkv_o[rows, g * 384 + 128 : g * 384 + 256] = dk
            dqkv_o[rows, g * 384 + 256 : g * 384 + 384] = dv
            small[3:4, g * 384 : g * 384 + 128] += jnp.sum(dq.astype(F32), axis=0, keepdims=True)
            small[3:4, g * 384 + 256 : g * 384 + 384] += jnp.sum(dv.astype(F32), axis=0, keepdims=True)
        return carry

    lax.fori_loop(0, wins, attend, 0)
    weights[3].wait()
    for g in range(4):
        part = mm(dqkv_o[:, g * 384 : (g + 1) * 384], wq[g], NT)
        if g == 0:
            dn[...] = part
        else:
            dn[...] += part
    olds[4].wait()

    def first(w, carry):
        rows = pl.ds(pl.multiple_of(w * SLOT, SLOT), SLOT)
        grad = dn[rows, :]
        hat, scale = centre(x[rows, :].astype(F32))
        dx_o[rows, :] = (dmid[rows, :] + norm_back(grad, hat, scale, vec[0:1, :])).astype(BF)
        small[1:2, 1024:1536] += jnp.sum(grad * hat, axis=0, keepdims=True)
        small[1:2, 1536:2048] += jnp.sum(grad, axis=0, keepdims=True)
        return carry

    lax.fori_loop(0, wins, first, 0)
    picked = mm(put[...], dx_o[...], TN).astype(BF)
    at = 0
    for ref in (s_main, s_row, s_col, s_cor):
        ref[...] = picked[at : at + ref.shape[0]]
        at += ref.shape[0]


def weight_grad_kernel(slots, batches, cut, sec, *refs):
    lists = [refs[i * slots : (i + 1) * slots] for i in range(4)]
    out1, out2, l1, r1, l2, r2, sems = refs[4 * slots :]
    rows = lists[0][0].shape[0]

    def copies(shift):
        result = []
        for kind, (slot_list, target) in enumerate(zip(lists, (l1, r1, l2, r2))):
            for batch in range(batches):
                result.append(
                    pltpu.make_async_copy(slot_list[batch + shift[kind % 2]], target.at[pl.ds(batch * rows, rows), :], sems.at[kind])
                )
        return result

    first, second = copies((0, 1)), copies((1, 0))

    @pl.when(sec[0] == 0)
    def _():
        for copy in first:
            copy.start()

    @pl.when(sec[0] == 1)
    def _():
        for copy in second:
            copy.start()

    for copy in first[: 2 * batches]:
        copy.wait()
    for part in range(out1.shape[0]):
        if cut[0] == "left":
            width = out1.shape[1]
            out1[part] = mm(l1[:, part * width : (part + 1) * width], r1[...], TN).astype(BF)
        else:
            width = out1.shape[2]
            out1[part] = mm(l1[...], r1[:, part * width : (part + 1) * width], TN).astype(BF)
    for copy in first[2 * batches :]:
        copy.wait()
    for part in range(out2.shape[0]):
        if cut[1] == "left":
            width = out2.shape[1]
            out2[part] = mm(l2[:, part * width : (part + 1) * width], r2[...], TN).astype(BF)
        else:
            width = out2.shape[2]
            out2[part] = mm(l2[...], r2[:, part * width : (part + 1) * width], TN).astype(BF)


SMEM_SPEC = pl.BlockSpec(memory_space=pltpu.SMEM)
HBM_SPEC = pl.BlockSpec(memory_space=pl.ANY)
VMEM_SPEC = pl.BlockSpec(memory_space=pltpu.VMEM)


def batch_spec(array, index):
    return pl.BlockSpec((1,) + array.shape[1:], lambda i: (index, 0, 0))


def shape_of(rows, cols, dtype=BF):
    return jax.ShapeDtypeStruct((rows, cols), dtype)


def run_forward(tables, sec, pin, index, pieces, put, pick, weights, vec, bq, b1, bias, region):
    rows = tables.rows
    wide = weights[2].shape[0] * weights[2].shape[2]
    outs = (
        [shape_of(rows, 512)]
        + [shape_of(size, 512) for size in tables.sizes]
        + [shape_of(rows, 512), shape_of(rows, 512), shape_of(rows, 1536), shape_of(rows, 1024), shape_of(rows, 512)]
        + [shape_of(rows, 512, F32), shape_of(rows, 512), shape_of(rows, wide), shape_of(rows, wide)]
    )
    flops = 2 * rows * 3145728 * 2
    result = pl.pallas_call(
        functools.partial(forward_kernel, tables.wins),
        grid=(1,),
        out_shape=outs,
        in_specs=[SMEM_SPEC, batch_spec(pin, index)] + [VMEM_SPEC] * 6 + [HBM_SPEC] * 4 + [VMEM_SPEC] * 5,
        out_specs=[VMEM_SPEC] * len(outs),
        scratch_shapes=[pltpu.VMEM(w.shape, BF) for w in weights] + [pltpu.SemaphoreType.DMA((4,))],
        compiler_params=pltpu.CompilerParams(vmem_limit_bytes=VMEM_LIMIT),
        cost_estimate=pl.CostEstimate(flops=flops, bytes_accessed=12_000_000, transcendentals=0),
        name="layer_forward",
    )(sec, pin, *pieces, put, pick, *weights, vec, bq, b1, bias, region)
    return result[0], result[1:5], result[5:]


def run_backward(tables, sec, pieces, targets, index, put, pick, weights, vec, old, new):
    rows = tables.rows
    wide = weights[2].shape[0] * weights[2].shape[2]
    outs = (
        [shape_of(rows, 512)]
        + [shape_of(size, 512) for size in tables.sizes]
        + [shape_of(rows, 512), shape_of(rows, wide), shape_of(rows, 512), shape_of(rows, 1536)]
        + [shape_of(8, 2048, F32), shape_of(SLOT, 1024, F32)]
    )
    kept = [pltpu.VMEM(a.shape, a.dtype) for a in old]
    result = pl.pallas_call(
        functools.partial(backward_kernel, tables.wins),
        grid=(1,),
        out_shape=outs,
        in_specs=[SMEM_SPEC] + [VMEM_SPEC] * 4 + [batch_spec(t, index) for t in targets] + [VMEM_SPEC] * 2
        + [HBM_SPEC] * 4 + [VMEM_SPEC] + [HBM_SPEC] * 10,
        out_specs=[VMEM_SPEC] * len(outs),
        scratch_shapes=[pltpu.VMEM(w.shape, BF) for w in weights]
        + kept
        + [pltpu.VMEM((rows, 512), F32), pltpu.VMEM((rows, 512), F32), pltpu.VMEM((rows, 512), BF)]
        + [pltpu.SemaphoreType.DMA((9,))],
        compiler_params=pltpu.CompilerParams(vmem_limit_bytes=VMEM_LIMIT),
        cost_estimate=pl.CostEstimate(flops=2 * rows * 3145728 * 2, bytes_accessed=16_000_000, transcendentals=0),
        name="layer_backward",
    )(sec, *pieces, *targets, put, pick, *weights, vec, *old, *new)
    return result[0], result[1:5], result[5:9], result[9], result[10]


def run_weight_grad(sec, batches, lists, outs, cut):
    slots = len(lists[0])
    rows = lists[0][0].shape[0]
    scratch = [pltpu.VMEM((batches * rows, members[0].shape[1]), BF) for members in lists]
    flops = sum(2 * batches * rows * int(np.prod(out)) for out in outs)
    return pl.pallas_call(
        functools.partial(weight_grad_kernel, slots, batches, cut),
        out_shape=[jax.ShapeDtypeStruct(out, BF) for out in outs],
        in_specs=[SMEM_SPEC] + [HBM_SPEC] * (4 * slots),
        out_specs=[VMEM_SPEC] * 2,
        scratch_shapes=scratch + [pltpu.SemaphoreType.DMA((4,))],
        compiler_params=pltpu.CompilerParams(vmem_limit_bytes=VMEM_LIMIT),
        cost_estimate=pl.CostEstimate(flops=flops, bytes_accessed=20_000_000, transcendentals=0),
        name="weight_grad",
    )(sec, *[member for members in lists for member in members])


def table_onehot():
    code = np.full((SLOT, SLOT), -1, np.int32)
    for u in range(TOKENS):
        for t in range(TOKENS):
            code[u, t] = (t // WIN - u // WIN + WIN - 1) * (2 * WIN - 1) + t % WIN - u % WIN + WIN - 1
    side = (2 * WIN - 1) ** 2
    return (jnp.arange(side, dtype=jnp.int32)[:, None] == jnp.asarray(code.reshape(1, -1))).astype(F32)


def region_mask(layout, section):
    row, mp = lax.axis_index("row"), lax.axis_index("mp")
    window_row = row * WROWS + mp // layout.across
    window_col = (mp % layout.across) * layout.wins + jnp.arange(layout.wins)
    place = jnp.arange(SLOT)
    row_label = jnp.where(window_row == layout.high - 1, 1 + (place // WIN >= WIN - SHIFT).astype(jnp.int32), 0)
    col_label = jnp.where(
        (window_col == WCOLS - 1)[:, None], 1 + (place % WIN >= WIN - SHIFT).astype(jnp.int32)[None], 0
    )
    labels = 3 * row_label[None] + col_label
    differs = labels[:, :, None] != labels[:, None, :]
    term = jnp.where(differs & (section == 1), -100.0, 0.0).astype(F32)
    return jnp.tile(term, (1, 1, GROUP))


def full_patches(layout, mp, tokens):
    wins = layout.wins
    place = jnp.arange(wins * SLOT)
    window, inner = place // SLOT, place % SLOT
    row = (mp // layout.across) * WIN + inner // WIN
    col = ((mp % layout.across) * wins + window) * WIN + inner % WIN
    token = jnp.where(inner < TOKENS, row * (WCOLS * WIN) + col, -1)
    return (token[:, None] == jnp.arange(tokens)[None]).astype(BF)


def whole_patches(layout, mp, tokens_here):
    token = mp * tokens_here + jnp.arange(tokens_here)
    row, col = token // (WCOLS * WIN), token % (WCOLS * WIN)
    window = col // WIN
    owner = (row // WIN) * layout.across + window // layout.wins
    place = owner * layout.wins * SLOT + (window % layout.wins) * SLOT + (row % WIN) * WIN + col % WIN
    return (place[:, None] == jnp.arange(layout.mp_count * layout.wins * SLOT)[None]).astype(BF)


def low_dot(matrix, stack):
    return jnp.einsum("pr,nrd->npd", matrix, stack, preferred_element_type=F32).astype(BF)


def body(
    layer_input,
    out_cotangent,
    norm_one_gain,
    norm_one_bias,
    attend_weight,
    attend_bias,
    position_table,
    output_weight,
    output_bias,
    norm_two_gain,
    norm_two_bias,
    expand_weight,
    expand_bias,
    reduce_weight,
    reduce_bias,
):
    row_count, mp_count = lax.axis_size("row"), lax.axis_size("mp")
    section, mp = lax.axis_index("section"), lax.axis_index("mp")
    layout = Layout(row_count, mp_count)
    tables = Tables(layout.wins)
    put = jnp.asarray(tables.put, BF)
    pick = jnp.asarray(tables.pick, BF)
    batches, tokens_here, width = layer_input.shape
    heads_here = attend_weight.shape[2]
    hidden_here = expand_weight.shape[2]
    sec = section.astype(jnp.int32).reshape(1)
    paired = layout.across == 2
    first = section == 0

    wq_here = attend_weight[0]
    if mp_count == 4:
        wq_here = wq_here.reshape(width, GROUP, 3, 32).transpose(0, 2, 1, 3).reshape(width, GROUP * 96)
    wq_all = lax.all_gather(wq_here, "mp", axis=0)
    if mp_count != 4:
        wq_all = wq_all.transpose(1, 0, 2, 3).reshape(width, 4, GROUP, 3, 32).transpose(1, 0, 3, 2, 4).reshape(4, width, GROUP * 96)
    wo_all = lax.all_gather(output_weight[0], "mp", axis=0).reshape(-1, width)
    w1_all = lax.all_gather(expand_weight[0], "mp", axis=0)
    w2_all = lax.all_gather(reduce_weight[0], "mp", axis=0)
    weights = (wq_all, wo_all, w1_all, w2_all)
    flat = jnp.concatenate([attend_bias[0].reshape(-1), position_table[0].reshape(-1), expand_bias[0].reshape(-1)])
    flat_all = lax.all_gather(flat, "mp", axis=0)
    cut_one = heads_here * 64
    cut_two = cut_one + heads_here * position_table.shape[2]
    bias_all = flat_all[:, :cut_one].reshape(4, GROUP, 2, 32)
    table_all = flat_all[:, cut_one:cut_two].reshape(-1, position_table.shape[2])
    b1 = flat_all[:, cut_two:]
    bq = jnp.stack([bias_all[:, :, 0], jnp.zeros_like(bias_all[:, :, 0]), bias_all[:, :, 1]], axis=1).reshape(4, -1)
    onehot = table_onehot()
    bias = jnp.dot(table_all, onehot, precision=highest).reshape(4, GROUP, SLOT, SLOT).transpose(0, 2, 1, 3)
    bias = bias.reshape(4, SLOT, GROUP * SLOT) + jnp.where(jnp.arange(SLOT) < TOKENS, 0.0, -1e30)[None, :, None]
    vec = jnp.concatenate(
        [norm_one_gain, norm_one_bias, output_bias, norm_two_gain, norm_two_bias, reduce_bias, jnp.zeros((2, width), F32)]
    )
    region = region_mask(layout, section)

    taken = jnp.where(first, layer_input, out_cotangent)
    if paired:
        keep, take, send = pair_tables(layout.wins)
        side = mp % 2
        keep = lax.dynamic_index_in_dim(jnp.asarray(keep, BF), side, 0, keepdims=False)
        take = lax.dynamic_index_in_dim(jnp.asarray(take, BF), side, 0, keepdims=False)
        send = jnp.asarray(send, BF)
        swap = [(i, i ^ 1) for i in range(mp_count)]
        arrived = lax.ppermute(low_dot(send, taken), "mp", swap)
        pin = low_dot(jnp.concatenate([keep, take], axis=1), jnp.concatenate([taken, arrived], axis=1))
    else:
        everything = lax.all_gather(taken, "mp", axis=1, tiled=True)
        pin = low_dot(full_patches(layout, mp, everything.shape[1]), everything)
    cuts = np.cumsum(tables.sizes)[:-1].tolist()
    targets = forward_halo(layout, jnp.split(low_dot(pick, pin), cuts, axis=1), 1)

    zero_pieces = [jnp.zeros((size, width), BF) for size in tables.sizes]
    forward_pieces, backward_pieces = zero_pieces, zero_pieces
    kept, outputs, grads, back_kept, smalls, biases = [], [], [], [], [], []
    for step in range(batches + 2):
        if step <= batches:
            out, sends, saved = run_forward(
                tables, sec, pin, min(step, batches - 1), forward_pieces, put, pick, weights, vec, bq, b1, bias, region
            )
            outputs.append(out)
            kept.append(saved)
            forward_pieces = forward_halo(layout, sends, 0)
        if step >= 1:
            chosen = [[kept[min(max(at, 0), batches)][i] for i in (0, 2, 3, 5, 8)] for at in (step - 2, step)]
            grad, sends, saved, small, table = run_backward(
                tables, sec, backward_pieces, targets, min(step - 1, batches - 1), put, pick, weights, vec, *chosen
            )
            grads.append(grad)
            back_kept.append(saved)
            smalls.append(small)
            biases.append(table)
            backward_pieces = backward_halo(layout, sends, 0)

    column = lambda rows, i: [row[i] for row in rows]
    d2, d1 = run_weight_grad(
        sec,
        batches,
        (column(kept, 7), column(back_kept, 0), column(kept, 6), column(back_kept, 1)),
        ((mp_count, hidden_here, width), (mp_count, width, hidden_here)),
        ("left", "right"),
    )
    do, dq = run_weight_grad(
        sec,
        batches,
        (column(kept, 4), column(back_kept, 2), column(kept, 1), column(back_kept, 3)),
        ((4, GROUP * 32, width), (4, width, GROUP * 96)),
        ("left", "right"),
    )
    do = do.reshape(mp_count, -1, width)
    if mp_count != 4:
        dq = dq.reshape(4, width, 3, GROUP, 32).transpose(0, 3, 1, 2, 4).reshape(mp_count, heads_here, width, 96)

    def shared(parts):
        part = lax.psum_scatter(parts, "mp", scatter_dimension=0, tiled=False)
        return lax.psum(part, "row").astype(F32)

    d2, d1, do, dq = shared(d2), shared(d1), shared(do), shared(dq)
    if mp_count == 4:
        dq = dq.reshape(width, 3, GROUP, 32).transpose(0, 2, 1, 3).reshape(width, GROUP, 96)
    else:
        dq = dq.transpose(1, 0, 2)
    pick_slots = lambda values: sum(jnp.where(first, values[i + 1], values[i]) for i in range(batches))
    small = pick_slots(smalls)
    table = pick_slots(biases).reshape(SLOT, 4 * GROUP, SLOT).transpose(1, 0, 2).reshape(4 * GROUP, -1)
    table = jnp.dot(table, onehot.T, precision=highest)
    small, table = lax.psum((small, table), ("row", "mp"))
    shift = small[3, :1536].reshape(4, 3, GROUP, 32)
    shift = jnp.concatenate([shift[:, 0], shift[:, 2]], axis=-1).reshape(4 * GROUP, 64)
    mine = lambda array: lax.dynamic_index_in_dim(array.reshape((mp_count, -1) + array.shape[1:]), mp, 0, keepdims=False)

    stack = jnp.stack(
        [jnp.where(first, outputs[i], outputs[i + 1]) for i in range(batches)]
        + [jnp.where(first, grads[i + 1], grads[i]) for i in range(batches)]
    )
    parts = jnp.split(low_dot(put.T, stack), cuts, axis=1)
    unrolled = low_dot(pick.T, jnp.concatenate(backward_halo(layout, parts, 1), axis=1))
    patches = jnp.where(first, stack, unrolled)
    if paired:
        arrived = lax.ppermute(low_dot(take.T, patches), "mp", swap)
        placed = low_dot(jnp.concatenate([keep.T, send.T], axis=1), jnp.concatenate([patches, arrived], axis=1))
    else:
        everything = lax.all_gather(patches, "mp", axis=1, tiled=True)
        placed = low_dot(whole_patches(layout, mp, tokens_here), everything)

    return (
        placed[:batches][None],
        placed[batches:].astype(F32)[None],
        small[1, 1024:1536][None],
        small[1, 1536:2048][None],
        dq[None],
        mine(shift)[None],
        mine(table)[None],
        do.reshape(output_weight.shape),
        small[1, 512:1024][None],
        small[2, 0:512][None],
        small[2, 512:1024][None],
        d1[None],
        mine(small[0])[None],
        d2[None],
        small[1, 0:512][None],
    )


def solution(mesh):
    return jax.shard_map(
        body,
        mesh=mesh,
        in_specs=(
            P(None, ("row", "mp"), None),
            P(None, ("row", "mp"), None),
            P("section", None),
            P("section", None),
            P("section", None, "mp", None),
            P("section", "mp", None),
            P("section", "mp", None),
            P("section", "mp", None, None),
            P("section", None),
            P("section", None),
            P("section", None),
            P("section", None, "mp"),
            P("section", "mp"),
            P("section", "mp", None),
            P("section", None),
        ),
        out_specs=(
            P("section", None, ("row", "mp"), None),
            P("section", None, ("row", "mp"), None),
            P("section", None),
            P("section", None),
            P("section", None, "mp", None),
            P("section", "mp", None),
            P("section", "mp", None),
            P("section", "mp", None, None),
            P("section", None),
            P("section", None),
            P("section", None),
            P("section", None, "mp"),
            P("section", "mp"),
            P("section", "mp", None),
            P("section", None),
        ),
        check_vma=False,
    )
```

```python
import functools

import jax
import jax.numpy as jnp
import numpy as np
from jax import lax
from jax.experimental import pallas as pl
from jax.experimental.pallas import tpu as pltpu
from jax.sharding import PartitionSpec as P

WIN = 7
SHIFT = 3
WCOLS = 8
WROWS = 2
TOKENS = WIN * WIN
SLOT = 64
GROUP = 4
AXES = ("section", "row", "mp")
EPS = 1e-05
BF = jnp.bfloat16
F32 = jnp.float32
NN = (((1,), (0,)), ((), ()))
NT = (((1,), (1,)), ((), ()))
TN = (((0,), (0,)), ((), ()))
VMEM_LIMIT = 56 * 1024 * 1024
highest = lax.Precision.HIGHEST


def mm(left, right, dims=NN):
    return lax.dot_general(left, right, dims, preferred_element_type=F32)


def up16(count):
    return -(-count // 16) * 16


def patch_place(row, col):
    return (col // WIN) * SLOT + row * WIN + col % WIN


class Tables:
    def __init__(self, wins):
        self.wins = wins
        self.rows = wins * SLOT
        cols = wins * WIN
        wide = range(SHIFT, cols)
        thin = range(SHIFT)
        low, high = range(SHIFT, WIN), range(SHIFT)
        pieces = [(low, wide), (high, wide), (low, thin), (high, thin)]
        self.sizes = [up16(len(a) * len(b)) for a, b in pieces]
        self.total = sum(self.sizes)
        pick = np.zeros((self.total, self.rows), np.float32)
        put = np.zeros((self.rows, self.total), np.float32)
        at = 0
        for (rows, columns), size in zip(pieces, self.sizes):
            spot = at
            for row in rows:
                for col in columns:
                    pick[spot, patch_place(row, col)] = 1
                    put[patch_place((row - SHIFT) % WIN, (col - SHIFT) % cols), spot] = 1
                    spot += 1
            at += size
        self.pick, self.put = pick, put


def pair_tables(wins):
    cols = wins * WIN
    tokens = WIN * cols
    keep = np.zeros((2, wins * SLOT, tokens), np.float32)
    take = np.zeros((2, wins * SLOT, up16(SHIFT * cols)), np.float32)
    send = np.zeros((up16(SHIFT * cols), tokens), np.float32)
    for seg in range(SHIFT):
        for col in range(cols):
            send[seg * cols + col, (2 * seg + 1) * cols + col] = 1
    for side in range(2):
        for row in range(WIN):
            for col in range(cols):
                place = patch_place(row, col)
                own = row <= SHIFT if side == 0 else row >= SHIFT
                if own:
                    seg = row if side == 0 else row - SHIFT
                    keep[side, place, 2 * seg * cols + col] = 1
                else:
                    seg = row - SHIFT - 1 if side == 0 else row
                    take[side, place, seg * cols + col] = 1
    return keep, take, send


class Layout:
    def __init__(self, row_count, mp_count):
        self.row_count, self.mp_count = row_count, mp_count
        self.across = mp_count // WROWS
        self.wins = WCOLS // self.across
        self.high = row_count * WROWS

    def device(self, section, window_row, place):
        window_row, place = window_row % self.high, place % self.across
        row = window_row // WROWS
        return (section * self.row_count + row) * self.mp_count + (window_row % WROWS) * self.across + place

    def route(self, source, target, up, back):
        return [
            (self.device(source, window_row, place), self.device(target, window_row - up, place - back))
            for window_row in range(self.high)
            for place in range(self.across)
        ]


HALO = ((0, 0), (1, 0), (0, 1), (1, 1))


def halo_swap(layout, parts):
    result = []
    for part, by in zip(parts, HALO):
        there = layout.route(0, 1, *by)
        result.append(lax.ppermute(part, AXES, there + [(b, a) for a, b in there]))
    return result


def halo_inside(layout, parts, back):
    result = [parts[0]]
    for part, by in zip(parts[1:], HALO[1:]):
        there = layout.route(1, 1, *by)
        result.append(lax.ppermute(part, AXES, [(b, a) for a, b in there] if back else there))
    return result


def ring(shard, axis, by=1):
    count = lax.axis_size(axis)
    return lax.ppermute(shard, axis, [(i, (i + by) % count) for i in range(count)])


def swap(shard, axis, bit):
    return lax.ppermute(shard, axis, [(i, i ^ bit) for i in range(lax.axis_size(axis))])


def natural_ring(shards, mp):
    stacked, count = jnp.stack(shards), len(shards)
    return jnp.stack([lax.dynamic_index_in_dim(stacked, (mp - j) % count, 0, keepdims=False) for j in range(count)])


def gather_quarter(quarter):
    held, crossed = [quarter], [swap(quarter, "row", 2)]
    for _ in range(lax.axis_size("mp") - 1):
        held.append(ring(held[-1], "mp"))
        crossed.append(swap(held[-1], "row", 2))
    mine = jnp.stack(held + crossed)
    return mine, swap(mine, "row", 1)


def take_at(array, index, axis=0):
    return lax.dynamic_index_in_dim(array, index, axis, keepdims=False)


def reduce_quarters(keep, send, row, mp):
    count = keep.shape[0]
    core, high = row % 2, row // 2
    part = keep + swap(send, "row", 1)
    part = take_at(part, high, 1) + swap(take_at(part, 1 - high, 1), "row", 2)
    total = take_at(part, (mp - 1) % count)
    for step in range(count - 1):
        total = ring(total, "mp") + take_at(part, (mp - 2 - step) % count)
    other = swap(total, "row", 2)
    pair = jnp.stack([jnp.where(high == 0, total, other), jnp.where(high == 0, other, total)])
    crossed = swap(pair, "row", 1)
    whole = jnp.stack([jnp.where(core == 0, pair, crossed), jnp.where(core == 0, crossed, pair)], axis=1)
    return whole.astype(F32).reshape((4,) + keep.shape[2:])


def sum_everywhere(array):
    for axis, bit in (("row", 1), ("row", 2), ("mp", 1), ("mp", 2)):
        array = array + swap(array, axis, bit)
    return array


def head_masks(dtype):
    lane = lax.broadcasted_iota(jnp.int32, (1, GROUP * 32), 1)
    return [jnp.where(lane // 32 == h, 1.0, 0.0).astype(dtype) for h in range(GROUP)]


def spread_heads(block, masks):
    return jnp.concatenate([block * mask for mask in masks], axis=0)


def fold_heads(tall, masks):
    total = tall[:SLOT] * masks[0]
    for h in range(1, GROUP):
        total = total + tall[h * SLOT : (h + 1) * SLOT] * masks[h]
    return total


def centre(values):
    middle = jnp.mean(values, axis=-1, keepdims=True)
    centred = values - middle
    scale = lax.rsqrt(jnp.mean(centred * centred, axis=-1, keepdims=True) + EPS)
    return centred * scale, scale


KEPT = ("gp", "mid", "qkv", "prob", "x")
WEIGHTS = ("wq", "wo", "w1", "w2")


class Refs:
    pass


class Copies:
    def __init__(self, sems):
        self.sems, self.used, self.sent = sems, 0, []

    def sem(self):
        self.used += 1
        return self.sems.at[self.used - 1]

    def ship(self, src, dst):
        copy = pltpu.make_async_copy(src, dst, self.sem())
        copy.start()
        self.sent.append(copy)

    def finish(self):
        for copy in self.sent:
            copy.wait()


def arrival(target, sem):
    return pltpu.make_async_copy(target, target, sem)


def load_weights(k, kinds, held, offsets):
    waits = {}
    shards = k.w1.shape[0]
    for name in kinds:
        kind, target, sem = WEIGHTS.index(name), getattr(k, name), k.copies.sem()
        waits[name] = arrival(target, sem)
        if held == 1:
            pltpu.make_async_copy(getattr(k, name + "_0"), target, sem).start()
            continue
        flat = len(target.shape) == 2
        high = target.shape[-2] // (4 * shards if flat else 4)
        for core in range(2):
            source = getattr(k, f"{name}_{core}")
            for piece in range(2 * shards):
                quarter = k.sec[1] ^ (core + 2 * (piece // shards))
                shard = lax.rem(k.sec[2] + (shards - piece % shards), shards)
                start = quarter * high
                if flat:
                    start = start + shard * (4 * high)
                rows = pl.ds(pl.multiple_of(start, high), high)
                place = target.at[rows, :] if flat else target.at[shard, rows, :]
                pltpu.make_async_copy(source.at[piece, pl.ds(offsets[kind], high), :], place, sem).start()
    return waits


def window_rows(w):
    return slice(w * SLOT, (w + 1) * SLOT)


def forward_part(k, wins, waits):
    x, qkv, prob, mid, gp = (k.x.at[0], k.qkv.at[0], k.prob.at[0], k.mid.at[0], k.gp.at[0])
    ship = k.copies.ship
    tables = []
    for name in ("bias", "region"):
        copy = pltpu.make_async_copy(getattr(k, name + "_h"), getattr(k, name), k.copies.sem())
        copy.start()
        tables.append(copy)

    @pl.when(k.sec[0] == 0)
    def _():
        x[...] = k.pin[0]

    @pl.when(k.sec[0] == 1)
    def _():
        joined = jnp.concatenate([k.p_main[...], k.p_row[...], k.p_col[...], k.p_cor[...]], axis=0)
        x[...] = mm(k.put[...], joined).astype(BF)

    for w in range(wins):
        rows = window_rows(w)
        hat, _ = centre(x[rows, :].astype(F32))
        k.a[rows, :] = (hat * k.vec[0:1, :] + k.vec[1:2, :]).astype(BF)
    ship(x, k.x_o)
    ship(k.a, k.a_o)
    waits["wq"].wait()
    lane = lax.broadcasted_iota(jnp.int32, (1, 3 * GROUP * 32), 1)
    factor = jnp.where(lane < GROUP * 32, 32 ** (-0.5), 1.0)
    for g in range(4):
        pr = mm(k.a[...], k.wq[g]) + k.bq[g : g + 1, :]
        qkv[:, g * 384 : (g + 1) * 384] = (pr * factor).astype(BF)
    ship(qkv, k.qkv_o)
    for copy in tables:
        copy.wait()
    masks, masks_f = head_masks(BF), head_masks(F32)
    for w in range(wins):
        rows = window_rows(w)
        for g in range(4):
            query = qkv[rows, g * 384 : g * 384 + 128]
            key = qkv[rows, g * 384 + 128 : g * 384 + 256]
            value = qkv[rows, g * 384 + 256 : g * 384 + 384]
            scores = mm(key, spread_heads(query, masks), NT) + k.bias[g] + k.region[w]
            top = jnp.max(scores, axis=0, keepdims=True)
            e = jnp.exp(scores - top)
            low = (e * (1.0 / jnp.sum(e, axis=0, keepdims=True))).astype(BF)
            prob[rows, g * 256 : (g + 1) * 256] = low
            k.ctx[rows, g * 128 : (g + 1) * 128] = fold_heads(mm(low, value, TN), masks_f).astype(BF)
    ship(prob, k.prob_o)
    ship(k.ctx, k.ctx_o)
    waits["wo"].wait()
    mid[...] = x[...].astype(F32) + (mm(k.ctx[...], k.wo[...]) + k.vec[2:3, :])
    ship(mid, k.mid_o)
    for w in range(wins):
        rows = window_rows(w)
        hat, _ = centre(mid[rows, :])
        k.n2[rows, :] = (hat * k.vec[3:4, :] + k.vec[4:5, :]).astype(BF)
    ship(k.n2, k.n2_o)
    waits["w1"].wait()
    waits["w2"].wait()
    parts, _, width = k.w1.shape
    total = mid[...] + k.vec[5:6, :]
    for j in range(parts):
        cols = slice(j * width, (j + 1) * width)
        hidden = mm(k.n2[...], k.w1[j]) + k.b1[j : j + 1, :]
        phi = 0.5 + 0.5 * lax.erf(hidden * 0.7071067811865476)
        act = (hidden * phi).astype(BF)
        k.act[:, cols] = act
        gp[:, cols] = (phi + hidden * (jnp.exp(hidden * hidden * -0.5) * 0.3989422804014327)).astype(BF)
        ship(k.act.at[:, cols], k.act_o.at[:, cols])
        ship(gp.at[:, cols], k.gp_o.at[:, cols])
        total = total + mm(act, k.w2[j])
    k.y[...] = total.astype(BF)
    ship(k.y, k.y_o)


def put_pieces(refs, joined):
    at = 0
    for ref in refs:
        ref[...] = joined[at : at + ref.shape[0]]
        at += ref.shape[0]


def norm_back(grad, hat, scale, gain):
    inner = grad * gain
    return scale * (inner - jnp.mean(inner, axis=-1, keepdims=True) - hat * jnp.mean(inner * hat, axis=-1, keepdims=True))


def column_sum(values):
    return jnp.sum(values, axis=0, keepdims=True)


def backward_start(k, names):
    waits = {}
    for name in names:
        copy = pltpu.make_async_copy(getattr(k, "old_" + name), getattr(k, name).at[1], k.copies.sem())
        pl.when(k.sec[0] == 0)(copy.start)
        waits[name] = lambda copy=copy: pl.when(k.sec[0] == 0)(copy.wait)
    return waits


def backward_mlp(k, wins, waits, olds):
    slot = 1 - k.sec[0]
    gp, mid = k.gp.at[slot], k.mid.at[slot]
    ship = k.copies.ship

    @pl.when(k.sec[0] == 0)
    def _():
        joined = jnp.concatenate([k.p_main[...], k.p_row[...], k.p_col[...], k.p_cor[...]], axis=0)
        k.g[...] = mm(k.pick[...], joined, TN).astype(BF)

    @pl.when(k.sec[0] == 1)
    def _():
        joined = jnp.concatenate([k.c_main[0], k.c_row[0], k.c_col[0], k.c_cor[0]], axis=0)
        k.g[...] = mm(k.put[...], joined).astype(BF)

    ship(k.g, k.g_o)
    parts, _, width = k.w1.shape
    waits["w2"].wait()
    waits["w1"].wait()
    olds["gp"]()
    total = None
    for j in range(parts):
        cols = slice(j * width, (j + 1) * width)
        dh = (mm(k.g[...], k.w2[j], NT) * gp[:, cols].astype(F32)).astype(BF)
        k.dh[:, cols] = dh
        k.small[0:1, cols] = column_sum(dh.astype(F32))
        ship(k.dh.at[:, cols], k.dh_o.at[:, cols])
        part = mm(dh, k.w1[j], NT)
        total = part if total is None else total + part
    k.dn[...] = total
    olds["mid"]()
    sums = [0.0] * 4
    for w in range(wins):
        rows = window_rows(w)
        grad = k.dn[rows, :]
        out = k.g[rows, :].astype(F32)
        hat, scale = centre(mid[rows, :])
        result = out + norm_back(grad, hat, scale, k.vec[3:4, :])
        k.dmid[rows, :] = result
        low = result.astype(BF)
        k.gm[rows, :] = low
        for i, term in enumerate((out, low.astype(F32), grad * hat, grad)):
            sums[i] = sums[i] + column_sum(term)
    ship(k.gm, k.gm_o)
    k.small[1:2, 0:512], k.small[1:2, 512:1024] = sums[0], sums[1]
    k.small[2:3, 0:512], k.small[2:3, 512:1024] = sums[2], sums[3]


def backward_attention(k, wins, waits, olds):
    slot = 1 - k.sec[0]
    qkv, prob, x = k.qkv.at[slot], k.prob.at[slot], k.x.at[slot]
    ship = k.copies.ship
    waits["wo"].wait()
    k.dctx[...] = mm(k.gm[...], k.wo[...], NT).astype(BF)
    olds["qkv"]()
    olds["prob"]()
    masks, masks_f = head_masks(BF), head_masks(F32)
    for w in range(wins):
        rows = window_rows(w)
        for g in range(4):
            at = g * 384
            query = qkv[rows, at : at + 128]
            key = qkv[rows, at + 128 : at + 256]
            value = qkv[rows, at + 256 : at + 384]
            do = spread_heads(k.dctx[rows, g * 128 : (g + 1) * 128], masks)
            low = prob[rows, g * 256 : (g + 1) * 256]
            p = low.astype(F32)
            dp = mm(value, do, NT)
            ds = (p * (dp - column_sum(p * dp))).astype(BF)
            if w == 0:
                k.dbias[:, g * 256 : (g + 1) * 256] = ds.astype(F32)
            else:
                k.dbias[:, g * 256 : (g + 1) * 256] += ds.astype(F32)
            dv = mm(low, do).astype(BF)
            dk = mm(ds, spread_heads(query, masks)).astype(BF)
            dq = (fold_heads(mm(ds, key, TN), masks_f) * 32 ** (-0.5)).astype(BF)
            k.dqkv[rows, at : at + 128] = dq
            k.dqkv[rows, at + 128 : at + 256] = dk
            k.dqkv[rows, at + 256 : at + 384] = dv
    ship(k.dqkv, k.dqkv_o)
    ship(k.dbias, k.dbias_o)
    waits["wq"].wait()
    total = None
    for g in range(4):
        part = k.dqkv[:, g * 384 : (g + 1) * 384]
        k.small[3:4, g * 384 : (g + 1) * 384] = column_sum(part.astype(F32))
        part = mm(part, k.wq[g], NT)
        total = part if total is None else total + part
    k.dn[...] = total
    olds["x"]()
    sums = [0.0] * 2
    for w in range(wins):
        rows = window_rows(w)
        grad = k.dn[rows, :]
        hat, scale = centre(x[rows, :].astype(F32))
        k.dx[rows, :] = (k.dmid[rows, :] + norm_back(grad, hat, scale, k.vec[0:1, :])).astype(BF)
        sums[0] = sums[0] + column_sum(grad * hat)
        sums[1] = sums[1] + column_sum(grad)
    ship(k.dx, k.dx_o)
    k.small[1:2, 1024:1536], k.small[1:2, 1536:2048] = sums


def step_kernel(wins, held, offsets, ahead, back, k):
    k.copies = Copies(k.sems)
    waits = load_weights(k, WEIGHTS if ahead else WEIGHTS[::-1], held, offsets)
    if back:
        olds = backward_start(k, KEPT)
    sends = [k.s_main, k.s_row, k.s_col, k.s_cor] if ahead else []
    if ahead:
        forward_part(k, wins, waits)

        @pl.when(k.sec[0] == 0)
        def _():
            put_pieces(sends, mm(k.pick[...], k.y[...]).astype(BF))

        @pl.when(k.sec[0] == 1)
        def _():
            k.unroll[...] = mm(k.put[...], k.y[...], TN).astype(BF)
            if not back:
                for ref in sends:
                    ref[...] = jnp.zeros_like(ref)

    if back:
        if ahead:
            waits = {name: Done() for name in WEIGHTS}
        k.small[...] = jnp.zeros_like(k.small)
        backward_mlp(k, wins, waits, olds)
        backward_attention(k, wins, waits, olds)
        if ahead:

            @pl.when(k.sec[0] == 1)
            def _():
                put_pieces(sends, mm(k.put[...], k.dx[...], TN).astype(BF))

    k.copies.finish()


class Done:
    def wait(self):
        pass


SMEM_SPEC = pl.BlockSpec(memory_space=pltpu.SMEM)
HBM_SPEC = pl.BlockSpec(memory_space=pl.ANY)
VMEM_SPEC = pl.BlockSpec(memory_space=pltpu.VMEM)


def shape_of(rows, cols, dtype=BF):
    return jax.ShapeDtypeStruct((rows, cols), dtype)


def call(kernel, name, ins, outs, scratch, flops, moved):
    names = list(ins) + list(outs) + list(scratch)

    def wrapped(*refs):
        k = Refs()
        for key, ref in zip(names, refs):
            setattr(k, key, ref)
        kernel(k)

    results = pl.pallas_call(
        wrapped,
        grid=(1,),
        out_shape=[shape for shape, _ in outs.values()],
        in_specs=[spec for _, spec in ins.values()],
        out_specs=[spec for _, spec in outs.values()],
        scratch_shapes=list(scratch.values()),
        compiler_params=pltpu.CompilerParams(vmem_limit_bytes=VMEM_LIMIT),
        cost_estimate=pl.CostEstimate(flops=flops, bytes_accessed=moved, transcendentals=0),
        name=name,
    )(*[array for array, _ in ins.values()])
    return dict(zip(outs, results))


PIECES = ("main", "row", "col", "cor")


def run_step(tables, static, landed, ahead=None, back=None):
    sources, offsets, shapes = static["weights"]
    rows, wide = tables.rows, shapes[2][0] * shapes[2][2]
    vmem = lambda array: (array, VMEM_SPEC)
    hbm = lambda array: (array, HBM_SPEC)
    one = lambda array, index: (array, pl.BlockSpec((1,) + array.shape[1:], lambda i: (index, 0, 0)))
    ins = {"sec": (static["sec"], SMEM_SPEC), "put": vmem(static["put"]), "pick": vmem(static["pick"]), "vec": vmem(static["vec"])}
    for name, piece in zip(PIECES, landed):
        ins["p_" + name] = vmem(piece)
    for core, source in enumerate(sources):
        for name, array in zip(WEIGHTS, source):
            ins[f"{name}_{core}"] = hbm(array)
    outs = {}
    scratch = {name: pltpu.VMEM(shape, BF) for name, shape in zip(WEIGHTS, shapes)}
    widths = {"gp": (wide, BF), "mid": (512, F32), "qkv": (1536, BF), "prob": (1024, BF), "x": (512, BF)}
    for name, (cols, dtype) in widths.items():
        scratch[name] = pltpu.VMEM((2, rows, cols), dtype)
    local = {}
    if ahead is not None:
        ins["pin"] = one(static["pin"], ahead)
        ins["bq"], ins["b1"] = vmem(static["bq"]), vmem(static["b1"])
        for name in ("bias", "region"):
            ins[name + "_h"] = hbm(static[name])
            scratch[name] = pltpu.VMEM(static[name].shape, F32)
        for name, size in zip(PIECES, tables.sizes):
            outs["s_" + name] = (shape_of(size, 512), VMEM_SPEC)
        outs["unroll"] = (shape_of(tables.total, 512), VMEM_SPEC)
        for name, (cols, dtype) in widths.items():
            outs[name + "_o"] = (shape_of(rows, cols, dtype), HBM_SPEC)
        local |= {"a": (512, BF), "ctx": (512, BF), "n2": (512, BF), "act": (wide, BF), "y": (512, BF)}
    if back is not None:
        index, old = back
        for name, target in zip(PIECES, static["targets"]):
            ins["c_" + name] = one(target, index)
        for name in KEPT:
            ins["old_" + name] = hbm(old[name + "_o"])
        outs["small"] = (shape_of(8, 2048, F32), VMEM_SPEC)
        local |= {"g": (512, BF), "dh": (wide, BF), "gm": (512, BF), "dqkv": (1536, BF), "dx": (512, BF)}
        for name, cols, dtype in (("dmid", 512, F32), ("dn", 512, F32), ("dctx", 512, BF)):
            scratch[name] = pltpu.VMEM((rows, cols), dtype)
        outs["dbias_o"] = (shape_of(SLOT, 1024, F32), HBM_SPEC)
        scratch["dbias"] = pltpu.VMEM((SLOT, 1024), F32)
    for name, (cols, dtype) in local.items():
        outs[name + "_o"] = (shape_of(rows, cols, dtype), HBM_SPEC)
        scratch[name] = pltpu.VMEM((rows, cols), dtype)
    scratch["sems"] = pltpu.SemaphoreType.DMA((96,))
    passes = 2 * (ahead is not None) + 4 * (back is not None)
    kernel = functools.partial(step_kernel, tables.wins, len(sources), offsets, ahead is not None, back is not None)
    return call(kernel, "layer_step", ins, outs, scratch, passes * rows * 3145728, 12_000_000)


def weight_grad_kernel(batches, first_slots, terms, quartered, k):
    k.copies = Copies(k.sems)
    waits = []
    for name in dict.fromkeys(name for term in terms for name in term[:2]):
        target, sem = getattr(k, name), k.copies.sem()
        rows = target.shape[0] // batches
        shift = first_slots[name]
        for section in range(2):
            for batch in range(batches):
                source = getattr(k, f"{name}_{batch + shift[section]}")
                copy = pltpu.make_async_copy(source, target.at[pl.ds(batch * rows, rows), :], sem)
                pl.when(k.sec[0] == section)(copy.start)
        waits.append((name, arrival(target, sem)))
    waits = dict(waits)
    for left, right, side, target, first, rows in terms:
        for name in (left, right):
            waits.pop(name, Done()).wait()
        l, r, t = getattr(k, left), getattr(k, right), getattr(k, target)
        parts = t.shape[0]
        for part in range(parts):
            if side == "left":
                width = l.shape[1] // parts
                value = mm(l[:, part * width : (part + 1) * width], r[...], TN)
            else:
                width = r.shape[1] // parts
                value = mm(l[...], r[:, part * width : (part + 1) * width], TN)
            t[part, first : first + rows, :] = value.astype(BF)
    targets = list(dict.fromkeys(term[3] for term in terms))
    if not quartered:
        for name in targets:
            k.copies.ship(getattr(k, name), getattr(k, name + "_o"))
        k.copies.finish()
        return
    sem = k.copies.sem()
    at = 0
    for name in targets:
        target = getattr(k, name)
        high = target.shape[1] // 4
        for quarter in range(4):
            source = target.at[:, pl.ds(quarter * high, high), :]
            for core in range(2):
                result = k.keep if quarter % 2 == core else k.send
                copy = pltpu.make_async_copy(source, result.at[:, quarter // 2, pl.ds(at, high), :], sem)
                pl.when(lax.rem(k.sec[1], 2) == core)(copy.start)
        at += high
    for result in (k.keep, k.send):
        arrival(result, sem).wait()


def run_weight_grad(static, batches, slots, first_slots, terms, shapes, quartered):
    ins = {"sec": (static["sec"], SMEM_SPEC)}
    scratch = {}
    for name, members in slots.items():
        for i, member in enumerate(members):
            ins[f"{name}_{i}"] = (member, HBM_SPEC)
        scratch[name] = pltpu.VMEM((batches * members[0].shape[0], members[0].shape[1]), BF)
    for name, shape in shapes.items():
        scratch[name] = pltpu.VMEM(shape, BF)
    if quartered:
        parts, cols = next(iter(shapes.values()))[::2]
        shape = jax.ShapeDtypeStruct((parts, 2, sum(shape[1] for shape in shapes.values()) // 4, cols), BF)
        outs = {"keep": (shape, HBM_SPEC), "send": (shape, HBM_SPEC)}
    else:
        outs = {name + "_o": (jax.ShapeDtypeStruct(shape, BF), HBM_SPEC) for name, shape in shapes.items()}
    scratch["sems"] = pltpu.SemaphoreType.DMA((16,))
    rows = batches * next(iter(slots.values()))[0].shape[0]
    flops = 2 * rows * sum(int(np.prod(shape)) for shape in shapes.values())
    kernel = functools.partial(weight_grad_kernel, batches, first_slots, terms, quartered)
    return call(kernel, "weight_grad", ins, outs, scratch, flops, 20_000_000)


def table_onehot():
    code = np.full((SLOT, SLOT), -1, np.int32)
    for u in range(TOKENS):
        for t in range(TOKENS):
            code[u, t] = (t // WIN - u // WIN + WIN - 1) * (2 * WIN - 1) + t % WIN - u % WIN + WIN - 1
    side = (2 * WIN - 1) ** 2
    return (jnp.arange(side, dtype=jnp.int32)[:, None] == jnp.asarray(code.reshape(1, -1))).astype(F32)


def region_mask(layout, section):
    row, mp = lax.axis_index("row"), lax.axis_index("mp")
    window_row = row * WROWS + mp // layout.across
    window_col = (mp % layout.across) * layout.wins + jnp.arange(layout.wins)
    place = jnp.arange(SLOT)
    row_label = jnp.where(window_row == layout.high - 1, 1 + (place // WIN >= WIN - SHIFT).astype(jnp.int32), 0)
    col_label = jnp.where(
        (window_col == WCOLS - 1)[:, None], 1 + (place % WIN >= WIN - SHIFT).astype(jnp.int32)[None], 0
    )
    labels = 3 * row_label[None] + col_label
    differs = labels[:, :, None] != labels[:, None, :]
    term = jnp.where(differs & (section == 1), -100.0, 0.0).astype(F32)
    return jnp.tile(term, (1, 1, GROUP))


def full_patches(layout, mp, tokens):
    wins = layout.wins
    place = jnp.arange(wins * SLOT)
    window, inner = place // SLOT, place % SLOT
    row = (mp // layout.across) * WIN + inner // WIN
    col = ((mp % layout.across) * wins + window) * WIN + inner % WIN
    token = jnp.where(inner < TOKENS, row * (WCOLS * WIN) + col, -1)
    return (token[:, None] == jnp.arange(tokens)[None]).astype(BF)


def whole_patches(layout, mp, tokens_here):
    token = mp * tokens_here + jnp.arange(tokens_here)
    row, col = token // (WCOLS * WIN), token % (WCOLS * WIN)
    window = col // WIN
    owner = (row // WIN) * layout.across + window // layout.wins
    place = owner * layout.wins * SLOT + (window % layout.wins) * SLOT + (row % WIN) * WIN + col % WIN
    return (place[:, None] == jnp.arange(layout.mp_count * layout.wins * SLOT)[None]).astype(BF)


def low_dot(matrix, stack):
    return jnp.einsum("pr,nrd->npd", matrix, stack, preferred_element_type=F32).astype(BF)


def body(
    layer_input,
    out_cotangent,
    norm_one_gain,
    norm_one_bias,
    attend_weight,
    attend_bias,
    position_table,
    output_weight,
    output_bias,
    norm_two_gain,
    norm_two_bias,
    expand_weight,
    expand_bias,
    reduce_weight,
    reduce_bias,
):
    row_count, mp_count = lax.axis_size("row"), lax.axis_size("mp")
    section, mp = lax.axis_index("section"), lax.axis_index("mp")
    layout = Layout(row_count, mp_count)
    tables = Tables(layout.wins)
    put = jnp.asarray(tables.put, BF)
    pick = jnp.asarray(tables.pick, BF)
    batches, tokens_here, width = layer_input.shape
    heads_here = attend_weight.shape[2]
    hidden_here = expand_weight.shape[2]
    row = lax.axis_index("row")
    sec = jnp.stack([section, row, mp]).astype(jnp.int32)
    paired = layout.across == 2 and row_count == 4
    first = section == 0

    flat = jnp.concatenate([attend_bias[0].reshape(-1), position_table[0].reshape(-1), expand_bias[0].reshape(-1)])
    if paired:
        quarter = lambda array: take_at(array.reshape((4, -1) + array.shape[1:]), row)
        one = quarter(attend_weight[0]).reshape(-1, GROUP, 3, 32).transpose(0, 2, 1, 3).reshape(-1, GROUP * 96)
        two = jnp.concatenate([quarter(output_weight[0].reshape(-1, width)), quarter(expand_weight[0]), quarter(reduce_weight[0])])
        held = [flat]
        for _ in range(mp_count - 1):
            held.append(ring(held[-1], "mp"))
        flat_all = natural_ring(held, mp)
        one, two = gather_quarter(one), gather_quarter(two)
        high_o, high_1 = heads_here * 8, width // 4
        weights = (
            [(one[i], two[i], two[i], two[i]) for i in range(2)],
            (0, 0, high_o, high_o + high_1),
            ((4, width, GROUP * 96), (4 * GROUP * 32, width), (mp_count, width, hidden_here), (mp_count, hidden_here, width)),
        )
    else:
        wq_all = lax.all_gather(attend_weight[0], "mp", axis=0)
        wq_all = wq_all.transpose(1, 0, 2, 3).reshape(width, 4, GROUP, 3, 32).transpose(1, 0, 3, 2, 4).reshape(4, width, GROUP * 96)
        wo_all = lax.all_gather(output_weight[0], "mp", axis=0).reshape(-1, width)
        w1_all = lax.all_gather(expand_weight[0], "mp", axis=0)
        w2_all = lax.all_gather(reduce_weight[0], "mp", axis=0)
        flat_all = lax.all_gather(flat, "mp", axis=0)
        whole = (wq_all, wo_all, w1_all, w2_all)
        weights = ([whole], (0, 0, 0, 0), tuple(array.shape for array in whole))
    cut_one = heads_here * 64
    cut_two = cut_one + heads_here * position_table.shape[2]
    bias_all = flat_all[:, :cut_one].reshape(4, GROUP, 2, 32)
    table_all = flat_all[:, cut_one:cut_two].reshape(-1, position_table.shape[2])
    b1 = flat_all[:, cut_two:]
    bq = jnp.stack([bias_all[:, :, 0], jnp.zeros_like(bias_all[:, :, 0]), bias_all[:, :, 1]], axis=1).reshape(4, -1)
    onehot = table_onehot()
    bias = jnp.dot(table_all, onehot, precision=highest).reshape(4, GROUP, SLOT, SLOT).transpose(0, 2, 1, 3)
    bias = bias.reshape(4, SLOT, GROUP * SLOT) + jnp.where(jnp.arange(SLOT) < TOKENS, 0.0, -1e30)[None, :, None]
    vec = jnp.concatenate(
        [norm_one_gain, norm_one_bias, output_bias, norm_two_gain, norm_two_bias, reduce_bias, jnp.zeros((2, width), F32)]
    )
    region = region_mask(layout, section)

    taken = jnp.where(first, layer_input, out_cotangent)
    if paired:
        keep, take, send = pair_tables(layout.wins)
        side = mp % 2
        keep = lax.dynamic_index_in_dim(jnp.asarray(keep, BF), side, 0, keepdims=False)
        take = lax.dynamic_index_in_dim(jnp.asarray(take, BF), side, 0, keepdims=False)
        send = jnp.asarray(send, BF)
        arrived = swap(low_dot(send, taken), "mp", 1)
        pin = low_dot(jnp.concatenate([keep, take], axis=1), jnp.concatenate([taken, arrived], axis=1))
    else:
        everything = lax.all_gather(taken, "mp", axis=1, tiled=True)
        pin = low_dot(full_patches(layout, mp, everything.shape[1]), everything)
    cuts = np.cumsum(tables.sizes)[:-1].tolist()
    targets = halo_inside(layout, jnp.split(low_dot(pick, pin), cuts, axis=1), False)

    static = dict(
        sec=sec, weights=weights, pin=pin, targets=targets, put=put, pick=pick, vec=vec, bq=bq, b1=b1, bias=bias, region=region
    )
    landed = [jnp.zeros((size, width), BF) for size in tables.sizes]
    steps = []
    for step in range(batches + 2):
        ahead = min(step, batches - 1) if step <= batches else None
        back = (min(step - 1, batches - 1), steps[max(step - 2, 0)]) if step else None
        done = run_step(tables, static, landed, ahead, back)
        steps.append(done)
        if step <= batches:
            landed = halo_swap(layout, [done["s_" + name] for name in PIECES])

    ahead_slots, back_slots = (0, 1), (1, 0)
    column = lambda name: [done[name + "_o"] for done in (steps[:-1] if name in ("act", "n2", "a", "ctx") else steps[1:])]
    where = {name: ahead_slots if name in ("act", "n2", "a", "ctx") else back_slots for name in ("act", "n2", "a", "ctx", "g", "dh", "gm", "dqkv")}
    gradient = lambda names, terms, shapes: run_weight_grad(
        static, batches, {name: column(name) for name in names}, where, terms, shapes, paired
    )
    mlp = gradient(
        ("act", "g", "n2", "dh"),
        (("act", "g", "left", "d2", 0, hidden_here), ("n2", "dh", "right", "d1", 0, width)),
        {"d2": (mp_count, hidden_here, width), "d1": (mp_count, width, hidden_here)},
    )
    heads = gradient(
        ("dqkv", "a", "ctx", "gm"),
        (("dqkv", "a", "left", "da", 0, GROUP * 96), ("ctx", "gm", "left", "da", GROUP * 96, GROUP * 32)),
        {"da": (4, GROUP * 128, width)},
    )
    if paired:
        both = reduce_quarters(mlp["keep"], mlp["send"], row, mp)
        d2 = both[:, : hidden_here // 4].reshape(hidden_here, width)
        d1 = both[:, hidden_here // 4 :].reshape(width, hidden_here)
        da = reduce_quarters(heads["keep"], heads["send"], row, mp).reshape(GROUP * 128, width)
        dq, do = da[: GROUP * 96].reshape(3, GROUP, 32, width), da[GROUP * 96 :]
        dq = dq.transpose(3, 1, 0, 2).reshape(attend_weight.shape[1:])
    else:

        def shared(parts):
            part = lax.psum_scatter(parts, "mp", scatter_dimension=0, tiled=False)
            return lax.psum(part, "row").astype(F32)

        da = heads["da_o"]
        dq = da[:, : GROUP * 96].reshape(4, 3, GROUP, 32, width).transpose(0, 2, 1, 3, 4).reshape(mp_count, heads_here * 96, width)
        d2, d1, do = shared(mlp["d2_o"]), shared(mlp["d1_o"]), shared(da[:, GROUP * 96 :].reshape(mp_count, heads_here * 32, width))
        dq = shared(dq).T.reshape(attend_weight.shape[1:])
    pick_slots = lambda values: sum(jnp.where(first, values[i + 1], values[i]) for i in range(batches))
    small = pick_slots([done["small"] for done in steps[1:]])
    table = pick_slots([done["dbias_o"] for done in steps[1:]]).reshape(SLOT, 4 * GROUP, SLOT).transpose(1, 0, 2).reshape(4 * GROUP, -1)
    table = jnp.dot(table, onehot.T, precision=highest)
    if paired:
        count = table.size
        table = jnp.pad(table.reshape(-1), (0, -count % 2048)).reshape(-1, 2048)
        both = sum_everywhere(jnp.concatenate([small, table]))
        small, table = both[: small.shape[0]], both[small.shape[0] :].reshape(-1)[:count].reshape(4 * GROUP, -1)
    else:
        small, table = lax.psum((small, table), ("row", "mp"))
    shift = small[3, :1536].reshape(4, 3, GROUP, 32)
    shift = jnp.concatenate([shift[:, 0], shift[:, 2]], axis=-1).reshape(4 * GROUP, 64)
    mine = lambda array: lax.dynamic_index_in_dim(array.reshape((mp_count, -1) + array.shape[1:]), mp, 0, keepdims=False)

    stack = jnp.stack([done["y_o"] for done in steps[:batches]] + [done["dx_o"] for done in steps[2:]])
    mine_y = [jnp.split(done["unroll"], cuts) for done in steps[1 : batches + 1]]
    mine_dx = [[done["s_" + name] for name in PIECES] for done in steps[1 : batches + 1]]
    parts = [jnp.stack([member[i] for member in mine_y + mine_dx]) for i in range(4)]
    unrolled = low_dot(pick.T, jnp.concatenate(halo_inside(layout, parts, True), axis=1))
    patches = jnp.where(first, stack, unrolled)
    if paired:
        arrived = swap(low_dot(take.T, patches), "mp", 1)
        placed = low_dot(jnp.concatenate([keep.T, send.T], axis=1), jnp.concatenate([patches, arrived], axis=1))
    else:
        everything = lax.all_gather(patches, "mp", axis=1, tiled=True)
        placed = low_dot(whole_patches(layout, mp, tokens_here), everything)

    return (
        placed[:batches][None],
        placed[batches:].astype(F32)[None],
        small[1, 1024:1536][None],
        small[1, 1536:2048][None],
        dq[None],
        mine(shift)[None],
        mine(table)[None],
        do.reshape(output_weight.shape),
        small[1, 512:1024][None],
        small[2, 0:512][None],
        small[2, 512:1024][None],
        d1[None],
        mine(small[0])[None],
        d2[None],
        small[1, 0:512][None],
    )


def solution(mesh):
    return jax.shard_map(
        body,
        mesh=mesh,
        in_specs=(
            P(None, ("row", "mp"), None),
            P(None, ("row", "mp"), None),
            P("section", None),
            P("section", None),
            P("section", None, "mp", None),
            P("section", "mp", None),
            P("section", "mp", None),
            P("section", "mp", None, None),
            P("section", None),
            P("section", None),
            P("section", None),
            P("section", None, "mp"),
            P("section", "mp"),
            P("section", "mp", None),
            P("section", None),
        ),
        out_specs=(
            P("section", None, ("row", "mp"), None),
            P("section", None, ("row", "mp"), None),
            P("section", None),
            P("section", None),
            P("section", None, "mp", None),
            P("section", "mp", None),
            P("section", "mp", None),
            P("section", "mp", None, None),
            P("section", None),
            P("section", None),
            P("section", None),
            P("section", None, "mp"),
            P("section", "mp"),
            P("section", "mp", None),
            P("section", None),
        ),
        check_vma=False,
    )
```

```python
import functools

import jax
import jax.numpy as jnp
import numpy as np
from jax import lax
from jax.experimental import pallas as pl
from jax.experimental.pallas import tpu as pltpu
from jax.sharding import PartitionSpec as P

WIN = 7
SHIFT = 3
WCOLS = 8
WROWS = 2
TOKENS = WIN * WIN
SLOT = 64
GROUP = 4
AXES = ("section", "row", "mp")
EPS = 1e-05
BF = jnp.bfloat16
F32 = jnp.float32
NN = (((1,), (0,)), ((), ()))
NT = (((1,), (1,)), ((), ()))
TN = (((0,), (0,)), ((), ()))
VMEM_LIMIT = 56 * 1024 * 1024
highest = lax.Precision.HIGHEST


def mm(left, right, dims=NN):
    return lax.dot_general(left, right, dims, preferred_element_type=F32)


def up16(count):
    return -(-count // 16) * 16


def patch_place(row, col):
    return (col // WIN) * SLOT + row * WIN + col % WIN


class Tables:
    def __init__(self, wins):
        self.wins = wins
        self.rows = wins * SLOT
        cols = wins * WIN
        wide = range(SHIFT, cols)
        thin = range(SHIFT)
        low, high = range(SHIFT, WIN), range(SHIFT)
        pieces = [(low, wide), (high, wide), (low, thin), (high, thin)]
        self.sizes = [up16(len(a) * len(b)) for a, b in pieces]
        self.total = sum(self.sizes)
        pick = np.zeros((self.total, self.rows), np.float32)
        put = np.zeros((self.rows, self.total), np.float32)
        at = 0
        for (rows, columns), size in zip(pieces, self.sizes):
            spot = at
            for row in rows:
                for col in columns:
                    pick[spot, patch_place(row, col)] = 1
                    put[patch_place((row - SHIFT) % WIN, (col - SHIFT) % cols), spot] = 1
                    spot += 1
            at += size
        self.pick, self.put = pick, put


def pair_tables(wins):
    cols = wins * WIN
    tokens = WIN * cols
    keep = np.zeros((2, wins * SLOT, tokens), np.float32)
    take = np.zeros((2, wins * SLOT, up16(SHIFT * cols)), np.float32)
    send = np.zeros((up16(SHIFT * cols), tokens), np.float32)
    for seg in range(SHIFT):
        for col in range(cols):
            send[seg * cols + col, (2 * seg + 1) * cols + col] = 1
    for side in range(2):
        for row in range(WIN):
            for col in range(cols):
                place = patch_place(row, col)
                own = row <= SHIFT if side == 0 else row >= SHIFT
                if own:
                    seg = row if side == 0 else row - SHIFT
                    keep[side, place, 2 * seg * cols + col] = 1
                else:
                    seg = row - SHIFT - 1 if side == 0 else row
                    take[side, place, seg * cols + col] = 1
    return keep, take, send


def placing_tables(wins):
    cols, tokens, most = wins * WIN, WIN * wins * WIN, up16(SHIFT * (wins * WIN + 1))
    own = np.zeros((2, 2, wins * SLOT, tokens), np.float32)
    give = np.zeros((2, 2, wins * SLOT, most), np.float32)
    take = np.zeros((2, 2, most, tokens), np.float32)
    up = np.zeros((wins * SLOT, most), np.float32)
    land = np.zeros((2, most, tokens), np.float32)
    half = SHIFT * 2 * cols + cols

    def holder(row, col):
        token = row * 2 * cols + col
        return (0, token) if token < half else (1, token - half)

    for section in range(2):
        for side in range(2):
            given, raised = 0, 0
            for row in range(WIN):
                for col in range(cols):
                    place = patch_place(row, col)
                    real_row = row + SHIFT * section
                    real_col = (side * cols + col + SHIFT * section) % (2 * cols)
                    if real_row >= WIN:
                        up[place, raised] = 1
                        land[side, raised, holder(real_row - WIN, real_col)[1]] = 1
                        raised += 1
                        continue
                    keeper, token = holder(real_row, real_col)
                    if keeper == side:
                        own[section, side, place, token] = 1
                    else:
                        give[section, side, place, given] = 1
                        take[section, keeper, given, token] = 1
                        given += 1
    return own, give, take, up, land


class Layout:
    def __init__(self, row_count, mp_count):
        self.row_count, self.mp_count = row_count, mp_count
        self.across = mp_count // WROWS
        self.wins = WCOLS // self.across
        self.high = row_count * WROWS

    def device(self, section, window_row, place):
        window_row, place = window_row % self.high, place % self.across
        row = window_row // WROWS
        return (section * self.row_count + row) * self.mp_count + (window_row % WROWS) * self.across + place

    def route(self, source, target, up, back):
        return [
            (self.device(source, window_row, place), self.device(target, window_row - up, place - back))
            for window_row in range(self.high)
            for place in range(self.across)
        ]


    def up_routes(self):
        return [
            [(self.device(1, window_row, side), self.device(1, window_row + 1, 0)) for window_row in range(self.high)] for side in range(2)
        ]


HALO = ((0, 0), (1, 0), (0, 1), (1, 1))


def halo_swap(layout, parts, back_only):
    result = []
    for part, by in zip(parts, HALO):
        there = layout.route(0, 1, *by)
        result.append(lax.ppermute(part, AXES, [(b, a) for a, b in there] + ([] if back_only else there)))
    return result


def halo_inside(layout, parts, back):
    result = [parts[0]]
    for part, by in zip(parts[1:], HALO[1:]):
        there = layout.route(1, 1, *by)
        result.append(lax.ppermute(part, AXES, [(b, a) for a, b in there] if back else there))
    return result


def ring(shard, axis, by=1):
    count = lax.axis_size(axis)
    return lax.ppermute(shard, axis, [(i, (i + by) % count) for i in range(count)])


def swap(shard, axis, bit):
    return lax.ppermute(shard, axis, [(i, i ^ bit) for i in range(lax.axis_size(axis))])


def natural_ring(shards, mp):
    stacked, count = jnp.stack(shards), len(shards)
    return jnp.stack([lax.dynamic_index_in_dim(stacked, (mp - j) % count, 0, keepdims=False) for j in range(count)])


def gather_quarter(quarter):
    near, far = ring(quarter, "mp"), ring(quarter, "mp", -1)
    further = ring(near, "mp")
    across = lambda piece: swap(piece, "row", 2)
    return (
        [(jnp.stack([quarter, near, across(quarter), across(near)]), ((0, 0), (0, 1), (2, 0), (2, 1)))]
        + [(jnp.stack([far, further, across(far), across(further)]), ((0, 3), (0, 2), (2, 3), (2, 2)))]
    ), further


def take_at(array, index, axis=0):
    return lax.dynamic_index_in_dim(array, index, axis, keepdims=False)


def head_masks(dtype):
    lane = lax.broadcasted_iota(jnp.int32, (1, GROUP * 32), 1)
    return [jnp.where(lane // 32 == h, 1.0, 0.0).astype(dtype) for h in range(GROUP)]


def spread_heads(block, masks):
    return jnp.concatenate([block * mask for mask in masks], axis=0)


def fold_heads(tall, masks):
    total = tall[:SLOT] * masks[0]
    for h in range(1, GROUP):
        total = total + tall[h * SLOT : (h + 1) * SLOT] * masks[h]
    return total


def centre(values):
    middle = jnp.mean(values, axis=-1, keepdims=True)
    centred = values - middle
    scale = lax.rsqrt(jnp.mean(centred * centred, axis=-1, keepdims=True) + EPS)
    return centred * scale, scale


KEPT = ("gp", "mid", "qkv", "prob", "x")
WEIGHTS = ("wq", "wo", "w1", "w2")
TOGETHER = 2


class Refs:
    pass


class Copies:
    def __init__(self, sems):
        self.sems, self.used, self.sent = sems, 0, []

    def sem(self, count=1):
        self.used += count
        return self.used - count

    def at(self, index):
        return self.sems.at[index]

    def ship(self, b, make):
        first = self.sem(TOGETHER)
        maker = lambda b: make(b, self.at(first + b))
        maker(b).start()
        self.sent.append(maker)

    def finish(self, count):
        for b in range(TOGETHER):

            @pl.when(b < count)
            def _(b=b):
                for maker in self.sent:
                    maker(b).wait()

        self.sent = []


def arrival(target, sem):
    return pltpu.make_async_copy(target, target, sem)


def load_weights(k, kinds, held, offsets):
    waits = {}
    for name in kinds:
        kind, target, sem = WEIGHTS.index(name), getattr(k, name), k.copies.at(k.copies.sem())
        waits[name] = arrival(target, sem)
        if held is None:
            pltpu.make_async_copy(getattr(k, name + "_whole"), target, sem).start()
            continue
        flat = len(target.shape) == 2
        shards = 4
        high = target.shape[-2] // (4 * shards if flat else 4)
        for number, places in enumerate(held):
            for piece, (bits, back) in enumerate(places):
                quarter = k.sec[1] ^ bits
                shard = lax.rem(k.sec[2] + (shards - back), shards)
                start = quarter * high
                if flat:
                    start = start + shard * (4 * high)
                rows = pl.ds(pl.multiple_of(start, high), high)
                place = target.at[rows, :] if flat else target.at[shard, rows, :]
                source = getattr(k, f"pieces_{number}").at[piece, pl.ds(offsets[kind], high), :]
                pltpu.make_async_copy(source, place, sem).start()
    return waits


def window_rows(w):
    return slice(w * SLOT, (w + 1) * SLOT)


def result(k, name, cols=None):
    def make(b, sem):
        src = getattr(k, name)
        src = src.at[0, b] if name in KEPT else src.at[b]
        dst = getattr(k, name + "_o").at[b]
        if cols is not None:
            src, dst = src.at[:, cols], dst.at[:, cols]
        return pltpu.make_async_copy(src, dst, sem)

    return make


def forward_part(k, wins, wait, b):
    x, qkv, prob, mid, gp = (getattr(k, name).at[0, b] for name in ("x", "qkv", "prob", "mid", "gp"))
    a, ctx, n2, act, y = (getattr(k, name).at[b] for name in ("a", "ctx", "n2", "act", "y"))
    ship = lambda name, cols=None: k.copies.ship(b, result(k, name, cols))

    @pl.when(k.sec[0] == 0)
    def _():
        x[...] = k.pin[b]

    if k.landed:

        @pl.when(k.sec[0] == 1)
        def _():
            joined = jnp.concatenate([k.p_main[b], k.p_row[b], k.p_col[b], k.p_cor[b]], axis=0)
            x[...] = mm(k.put[...], joined).astype(BF)

    for w in range(wins):
        rows = window_rows(w)
        hat, _ = centre(x[rows, :].astype(F32))
        a[rows, :] = (hat * k.vec[0:1, :] + k.vec[1:2, :]).astype(BF)
    ship("x")
    ship("a")
    wait("wq")
    lane = lax.broadcasted_iota(jnp.int32, (1, 3 * GROUP * 32), 1)
    factor = jnp.where(lane < GROUP * 32, 32 ** (-0.5), 1.0)
    for g in range(4):
        pr = mm(a[...], k.wq[g], NT) + k.bq[g : g + 1, :]
        qkv[:, g * 384 : (g + 1) * 384] = (pr * factor).astype(BF)
    ship("qkv")
    wait("bias")
    wait("region")
    masks, masks_f = head_masks(BF), head_masks(F32)
    for w in range(wins):
        rows = window_rows(w)
        for g in range(4):
            query = qkv[rows, g * 384 : g * 384 + 128]
            key = qkv[rows, g * 384 + 128 : g * 384 + 256]
            value = qkv[rows, g * 384 + 256 : g * 384 + 384]
            scores = mm(key, spread_heads(query, masks), NT) + k.bias[g] + k.region[w]
            top = jnp.max(scores, axis=0, keepdims=True)
            e = jnp.exp(scores - top)
            low = (e * (1.0 / jnp.sum(e, axis=0, keepdims=True))).astype(BF)
            prob[rows, g * 256 : (g + 1) * 256] = low
            ctx[rows, g * 128 : (g + 1) * 128] = fold_heads(mm(low, value, TN), masks_f).astype(BF)
    ship("prob")
    ship("ctx")
    wait("wo")
    mid[...] = x[...].astype(F32) + (mm(ctx[...], k.wo[...]) + k.vec[2:3, :])
    ship("mid")
    for w in range(wins):
        rows = window_rows(w)
        hat, _ = centre(mid[rows, :])
        n2[rows, :] = (hat * k.vec[3:4, :] + k.vec[4:5, :]).astype(BF)
    ship("n2")
    wait("w1")
    wait("w2")
    parts, _, width = k.w1.shape
    total = mid[...] + k.vec[5:6, :]
    for j in range(parts):
        cols = slice(j * width, (j + 1) * width)
        hidden = mm(n2[...], k.w1[j]) + k.b1[j : j + 1, :]
        phi = 0.5 + 0.5 * lax.erf(hidden * 0.7071067811865476)
        low = (hidden * phi).astype(BF)
        act[:, cols] = low
        gp[:, cols] = (phi + hidden * (jnp.exp(hidden * hidden * -0.5) * 0.3989422804014327)).astype(BF)
        ship("act", cols)
        ship("gp", cols)
        total = total + mm(low, k.w2[j])
    y[...] = total.astype(BF)
    ship("y")

    put_partner(k, 0, b, y)

    @pl.when(k.sec[0] == 0)
    def _():
        put_pieces(k, "s_", b, mm(k.pick[...], y[...]).astype(BF))

    @pl.when(k.sec[0] == 1)
    def _():
        put_neighbours(k, 0, b, y)


def put_pieces(k, first, b, joined):
    at = 0
    for name in PIECES:
        ref = getattr(k, first + name)
        ref[b] = joined[at : at + ref.shape[1]]
        at += ref.shape[1]


def put_partner(k, kind, b, result):
    if hasattr(k, "f_pair"):
        k.f_pair[kind, b] = mm(k.give[...], result[...], TN).astype(BF)


def put_neighbours(k, kind, b, result):
    if hasattr(k, "f_up"):
        k.f_up[kind, b] = mm(k.up[...], result[...], TN).astype(BF)
        return
    joined = mm(k.put[...], result[...], TN).astype(BF)
    at = 0
    for name in PIECES:
        ref = getattr(k, "h_" + name)
        ref[kind, b] = joined[at : at + ref.shape[2]]
        at += ref.shape[2]


def norm_back(grad, hat, scale, gain):
    inner = grad * gain
    return scale * (inner - jnp.mean(inner, axis=-1, keepdims=True) - hat * jnp.mean(inner * hat, axis=-1, keepdims=True))


def column_sum(values):
    return jnp.sum(values, axis=0, keepdims=True)


def backward_mlp(k, wins, wait, old, b):
    slot = 1 - k.sec[0]
    gp, mid = k.gp.at[slot, b], k.mid.at[slot, b]
    out_grad, dhs, gm, dmid = k.g.at[b], k.dh.at[b], k.gm.at[b], k.dmid.at[b]
    ship = lambda name, cols=None: k.copies.ship(b, result(k, name, cols))

    @pl.when(k.sec[0] == 0)
    def _():
        joined = jnp.concatenate([k.p_main[b], k.p_row[b], k.p_col[b], k.p_cor[b]], axis=0)
        out_grad[...] = mm(k.pick[...], joined, TN).astype(BF)

    @pl.when(k.sec[0] == 1)
    def _():
        joined = jnp.concatenate([k.c_main[b], k.c_row[b], k.c_col[b], k.c_cor[b]], axis=0)
        out_grad[...] = mm(k.put[...], joined).astype(BF)

    ship("g")
    parts, _, width = k.w1.shape
    wait("w2")
    wait("w1")
    old("gp", b)
    total = None
    for j in range(parts):
        cols = slice(j * width, (j + 1) * width)
        dh = (mm(out_grad[...], k.w2[j], NT) * gp[:, cols].astype(F32)).astype(BF)
        dhs[:, cols] = dh
        k.small[0:1, cols] += column_sum(dh.astype(F32))
        ship("dh", cols)
        part = mm(dh, k.w1[j], NT)
        total = part if total is None else total + part
    k.dn[...] = total
    old("mid", b)
    sums = [0.0] * 4
    for w in range(wins):
        rows = window_rows(w)
        grad = k.dn[rows, :]
        out = out_grad[rows, :].astype(F32)
        hat, scale = centre(mid[rows, :])
        whole = out + norm_back(grad, hat, scale, k.vec[3:4, :])
        dmid[rows, :] = whole
        low = whole.astype(BF)
        gm[rows, :] = low
        for i, term in enumerate((out, low.astype(F32), grad * hat, grad)):
            sums[i] = sums[i] + column_sum(term)
    ship("gm")
    if hasattr(k, "dmid_o"):
        ship("dmid")
    k.small[1:2, 0:512] += sums[0]
    k.small[1:2, 512:1024] += sums[1]
    k.small[2:3, 0:512] += sums[2]
    k.small[2:3, 512:1024] += sums[3]


def backward_attention(k, wins, wait, old, b, reload):
    slot = 1 - k.sec[0]
    qkv, prob, x = k.qkv.at[slot, b], k.prob.at[slot, b], k.x.at[slot, b]
    gm, dmid, dqkv, dx = k.gm.at[b], k.dmid.at[b], k.dqkv.at[b], k.dx.at[b]
    ship = lambda name, cols=None: k.copies.ship(b, result(k, name, cols))
    wait("wo")
    if reload:
        old("gm", b)
    k.dctx[...] = mm(gm[...], k.wo[...], NT).astype(BF)
    old("qkv", b)
    old("prob", b)
    masks, masks_f = head_masks(BF), head_masks(F32)
    for w in range(wins):
        rows = window_rows(w)
        for g in range(4):
            at = g * 384
            query = qkv[rows, at : at + 128]
            key = qkv[rows, at + 128 : at + 256]
            value = qkv[rows, at + 256 : at + 384]
            do = spread_heads(k.dctx[rows, g * 128 : (g + 1) * 128], masks)
            low = prob[rows, g * 256 : (g + 1) * 256]
            p = low.astype(F32)
            dp = mm(value, do, NT)
            ds = (p * (dp - column_sum(p * dp))).astype(BF)
            k.dbias[:, g * 256 : (g + 1) * 256] += ds.astype(F32)
            dv = mm(low, do).astype(BF)
            dk = mm(ds, spread_heads(query, masks)).astype(BF)
            dq = (fold_heads(mm(ds, key, TN), masks_f) * 32 ** (-0.5)).astype(BF)
            dqkv[rows, at : at + 128] = dq
            dqkv[rows, at + 128 : at + 256] = dk
            dqkv[rows, at + 256 : at + 384] = dv
    ship("dqkv")
    wait("wq")
    total = None
    for g in range(4):
        part = dqkv[:, g * 384 : (g + 1) * 384]
        k.small[3:4, g * 384 : (g + 1) * 384] += column_sum(part.astype(F32))
        part = mm(part, k.wq[g])
        total = part if total is None else total + part
    k.dn[...] = total
    old("x", b)
    if reload:
        old("dmid", b)
    sums = [0.0] * 2
    for w in range(wins):
        rows = window_rows(w)
        grad = k.dn[rows, :]
        hat, scale = centre(x[rows, :].astype(F32))
        dx[rows, :] = (dmid[rows, :] + norm_back(grad, hat, scale, k.vec[0:1, :])).astype(BF)
        sums[0] = sums[0] + column_sum(grad * hat)
        sums[1] = sums[1] + column_sum(grad)
    ship("dx")
    k.small[1:2, 1024:1536] += sums[0]
    k.small[1:2, 1536:2048] += sums[1]
    put_partner(k, 1, b, dx)
    if hasattr(k, "s_main"):

        @pl.when(k.sec[0] == 1)
        def _():
            put_pieces(k, "s_", b, mm(k.put[...], dx[...], TN).astype(BF))
            put_neighbours(k, 1, b, dx)


def loop(count, most, run):
    def once(b, carry):
        run(b)
        return carry

    if most:
        lax.fori_loop(0, count, once, 0)


def step_kernel(wins, held, offsets, counts, mlp, attention, k):
    k.copies = copies = Copies(k.sems)
    ahead, back = max(counts[:2]), max(counts[2:])
    number = lambda pair: jnp.where(k.sec[0] == 0, pair[0], pair[1])
    forwards, backwards = number(counts[:2]), number(counts[2:])
    kinds = WEIGHTS if ahead else (("w2", "w1") if mlp else ()) + (("wo", "wq") if attention else ())
    waits = load_weights(k, kinds[:1], held, offsets)
    if ahead:
        for name in ("bias", "region"):
            copy = pltpu.make_async_copy(getattr(k, name + "_h"), getattr(k, name), copies.at(copies.sem()))
            copy.start()
            waits[name] = copy
    fetched = {}
    if back:
        reload = attention and not mlp
        for name in (("gp", "mid") if mlp else ("gm", "dmid")) + (("qkv", "prob", "x") if attention else ()):
            first = copies.sem(TOGETHER)

            def fetch(b, name=name, first=first):
                target = getattr(k, name)
                target = target.at[1, b] if name in KEPT else target.at[b]
                return pltpu.make_async_copy(getattr(k, "old_" + name).at[b], target, copies.at(first + b))

            fetched[name] = fetch
            for b in range(back):
                pl.when((k.sec[0] == 0) & (b < backwards))(lambda b=b, fetch=fetch: fetch(b).start())
    waits |= load_weights(k, kinds[1:], held, offsets)

    def all_weights():
        for copy in waits.values():
            copy.wait()

    def old(name, b):
        if name in fetched:
            pl.when(k.sec[0] == 0)(lambda: fetched[name](b).wait())

    def forward(b):
        forward_part(k, wins, lambda name: pl.when(b == 0)(waits[name].wait), b)

    loop(forwards, ahead, forward)
    if ahead:
        pl.when(forwards == 0)(all_weights)
    sent_ahead, copies.sent = copies.sent, []
    if back:
        k.small[...] = jnp.zeros_like(k.small)
        if attention:
            k.dbias[...] = jnp.zeros_like(k.dbias)
        wait = lambda b: (lambda name: None) if ahead else (lambda name: pl.when(b == 0)(waits[name].wait))

        def backward(b):
            if mlp:
                backward_mlp(k, wins, wait(b), old, b)
            if attention:
                backward_attention(k, wins, wait(b), old, b, reload)

        loop(backwards, back, backward)
        if not ahead:
            pl.when(backwards == 0)(all_weights)
    copies.finish(backwards)
    copies.sent = sent_ahead
    copies.finish(forwards)


SMEM_SPEC = pl.BlockSpec(memory_space=pltpu.SMEM)
HBM_SPEC = pl.BlockSpec(memory_space=pl.ANY)
VMEM_SPEC = pl.BlockSpec(memory_space=pltpu.VMEM)


def shape_of(*shape, dtype=BF):
    return jax.ShapeDtypeStruct(shape, dtype)


def call(kernel, name, ins, outs, scratch, flops, moved):
    names = list(ins) + list(outs) + list(scratch)

    def wrapped(*refs):
        k = Refs()
        for key, ref in zip(names, refs):
            setattr(k, key, ref)
        kernel(k)

    results = pl.pallas_call(
        wrapped,
        grid=(1,),
        out_shape=[shape for shape, _ in outs.values()],
        in_specs=[spec for _, spec in ins.values()],
        out_specs=[spec for _, spec in outs.values()],
        scratch_shapes=list(scratch.values()),
        compiler_params=pltpu.CompilerParams(vmem_limit_bytes=VMEM_LIMIT),
        cost_estimate=pl.CostEstimate(flops=min(flops, 1), bytes_accessed=min(moved, 1), transcendentals=0),
        name=name,
    )(*[array for array, _ in ins.values()])
    return dict(zip(outs, results))


PIECES = ("main", "row", "col", "cor")


def vmem(array):
    return (array, VMEM_SPEC)


def hbm(array):
    return (array, HBM_SPEC)


def run_step(tables, static, landed, counts, groups, old, mlp=True, attention=True):
    sources, held, offsets, shapes = static["weights"]
    rows, wide = tables.rows, shapes[2][0] * shapes[2][2]
    ahead, back = max(counts[:2]), max(counts[2:])
    one = lambda array, index: (array, pl.BlockSpec((TOGETHER,) + array.shape[1:], lambda i: (index, 0, 0)))
    ins = {"sec": (static["sec"], SMEM_SPEC), "put": vmem(static["put"]), "pick": vmem(static["pick"]), "vec": vmem(static["vec"])}
    if landed is not None and (ahead or mlp):
        for name, piece in zip(PIECES, landed):
            ins["p_" + name] = vmem(piece)
    kinds = WEIGHTS if ahead else (("w1", "w2") if mlp else ()) + (("wq", "wo") if attention else ())
    outs, scratch = {}, {}
    for name, shape in zip(WEIGHTS, shapes):
        if name in kinds:
            scratch[name] = pltpu.VMEM(shape, BF)
            if held is None:
                ins[name + "_whole"] = hbm(sources[WEIGHTS.index(name)])
    if held is not None:
        for number, source in enumerate(sources):
            ins[f"pieces_{number}"] = hbm(source)
    widths = {"gp": (wide, BF), "mid": (512, F32), "qkv": (1536, BF), "prob": (1024, BF), "x": (512, BF)}
    for name, (cols, dtype) in widths.items():
        if ahead or (mlp if name in ("gp", "mid") else attention):
            scratch[name] = pltpu.VMEM((2, TOGETHER, rows, cols), dtype)
    local, passed = {}, {}
    if "give" in static and (ahead or attention):
        ins["give"] = vmem(static["give"])
        outs["f_pair"] = (shape_of(2, TOGETHER, static["give"].shape[1], 512), VMEM_SPEC)
        if ahead:
            ins["up"] = vmem(static["up"])
            outs["f_up"] = (shape_of(2, TOGETHER, static["up"].shape[1], 512), VMEM_SPEC)
    if ahead:
        ins["pin"] = one(static["pin"], groups[0])
        ins["bq"], ins["b1"] = vmem(static["bq"]), vmem(static["b1"])
        for name in ("bias", "region"):
            ins[name + "_h"] = hbm(static[name])
            scratch[name] = pltpu.VMEM(static[name].shape, F32)
        for name, size in zip(PIECES, tables.sizes):
            outs["s_" + name] = (shape_of(TOGETHER, size, 512), VMEM_SPEC)
            if "give" not in static:
                outs["h_" + name] = (shape_of(2, TOGETHER, size, 512), VMEM_SPEC)
        for name, (cols, dtype) in widths.items():
            outs[name + "_o"] = (shape_of(TOGETHER, rows, cols, dtype=dtype), HBM_SPEC)
        local |= {"a": (512, BF), "ctx": (512, BF), "n2": (512, BF), "act": (wide, BF), "y": (512, BF)}
    if back:
        if mlp:
            for name, target in zip(PIECES, static["targets"]):
                ins["c_" + name] = one(target, groups[1])
            local |= {"g": (512, BF), "dh": (wide, BF), "gm": (512, BF)}
            (passed if attention else local)["dmid"] = (512, F32)
        else:
            passed |= {"gm": (512, BF), "dmid": (512, F32)}
        for name in (("gp", "mid") if mlp else ("gm", "dmid")) + (("qkv", "prob", "x") if attention else ()):
            ins["old_" + name] = hbm(old[name + "_o"])
        if attention:
            local |= {"dqkv": (1536, BF), "dx": (512, BF)}
            scratch["dctx"] = pltpu.VMEM((rows, 512), BF)
            outs["dbias"] = (shape_of(SLOT, 1024, dtype=F32), VMEM_SPEC)
        scratch["dn"] = pltpu.VMEM((rows, 512), F32)
        outs["small"] = (shape_of(8, 2048, dtype=F32), VMEM_SPEC)
    for name, (cols, dtype) in local.items():
        outs[name + "_o"] = (shape_of(TOGETHER, rows, cols, dtype=dtype), HBM_SPEC)
        scratch[name] = pltpu.VMEM((TOGETHER, rows, cols), dtype)
    for name, (cols, dtype) in passed.items():
        scratch[name] = pltpu.VMEM((TOGETHER, rows, cols), dtype)
    scratch["sems"] = pltpu.SemaphoreType.DMA((192,))
    passes = 2 * ahead + 2 * back * (mlp + attention)
    kernel = functools.partial(step_kernel, tables.wins, held, offsets, counts, mlp, attention)

    def run(k):
        k.landed = landed is not None
        kernel(k)

    return call(run, "layer_step", ins, outs, scratch, 2 * passes * rows * TOGETHER * 3145728, 20_000_000)


def weight_grad_kernel(slots, terms, quartered, based, k):
    sems = iter(range(64))
    waits = {}
    for name in dict.fromkeys(name for term in terms for name in term[:2]):
        target, sem = getattr(k, name), k.sems.at[next(sems)]
        batches = len(slots[name][0])
        rows = target.shape[0] // batches
        for section in range(2):

            @pl.when(k.sec[0] == section)
            def _(name=name, section=section, target=target, sem=sem):
                for batch, (step, place) in enumerate(slots[name][section]):
                    source = getattr(k, f"{name}_{step}").at[place]
                    pltpu.make_async_copy(source, target.at[pl.ds(batch * rows, rows), :], sem).start()

        waits[name] = arrival(target, sem)
    for name in based:
        waits[name] = pltpu.make_async_copy(getattr(k, name + "_base"), getattr(k, name), k.sems.at[next(sems)])
        waits[name].start()
    leaving = []
    for number, (left, right, side, name, first, rows) in enumerate(terms):
        for needed in (left, right, name):
            if needed in waits:
                waits.pop(needed).wait()
        l, r, t = getattr(k, left), getattr(k, right), getattr(k, name)
        parts = t.shape[0]
        for part in range(parts):
            if side == "left":
                width = l.shape[1] // parts
                value = mm(l[:, part * width : (part + 1) * width], r[...], TN)
            else:
                width = r.shape[1] // parts
                value = mm(l[...], r[:, part * width : (part + 1) * width], TN)
            if name in based:
                value = value + t[part, first : first + rows, :].astype(F32)
            t[part, first : first + rows, :] = value.astype(BF)
        if any(name == term[3] for term in terms[number + 1 :]):
            continue
        sem = k.sems.at[next(sems)]
        if not quartered:
            copy = pltpu.make_async_copy(t, getattr(k, name + "_o"), sem)
            copy.start()
            leaving.append(copy)
            continue
        keep, send = getattr(k, name + "_keep"), getattr(k, name + "_send")
        high = t.shape[1] // 4
        for core in range(2):

            @pl.when(lax.rem(k.sec[1], 2) == core)
            def _(core=core, t=t, keep=keep, send=send, sem=sem, high=high):
                for quarter in range(4):
                    place = keep if quarter % 2 == core else send
                    pltpu.make_async_copy(t.at[:, pl.ds(quarter * high, high), :], place.at[:, quarter // 2], sem).start()

        leaving.append(arrival(t, sem))
    for copy in leaving:
        copy.wait()


def run_weight_grad(static, members, slots, terms, shapes, quartered, base):
    ins = {"sec": (static["sec"], SMEM_SPEC)}
    scratch, outs = {}, {}
    for name, arrays in members.items():
        for i, array in arrays.items():
            ins[f"{name}_{i}"] = hbm(array)
        scratch[name] = pltpu.VMEM((len(slots[name][0]) * array.shape[1], array.shape[2]), BF)
    for name, array in base.items():
        ins[name + "_base"] = hbm(array)
    for name, shape in shapes.items():
        scratch[name] = pltpu.VMEM(shape, BF)
        if quartered:
            for kind in ("_keep", "_send"):
                outs[name + kind] = (shape_of(shape[0], 2, shape[1] // 4, shape[2]), HBM_SPEC)
        else:
            outs[name + "_o"] = (shape_of(*shape), HBM_SPEC)
    scratch["sems"] = pltpu.SemaphoreType.DMA((64,))
    rows = scratch[next(iter(members))].shape[0]
    flops = 2 * rows * sum(int(np.prod(shape)) for shape in shapes.values())
    kernel = functools.partial(weight_grad_kernel, slots, terms, quartered, tuple(base))
    return call(kernel, "weight_grad", ins, outs, scratch, flops, 20_000_000)


def collect(arrays):
    ins = {f"{name}_{i}": vmem(array) for name, members in arrays.items() for i, array in enumerate(members)}
    outs = {name: (shape_of(len(members), *members[0].shape), VMEM_SPEC) for name, members in arrays.items()}

    def kernel(k):
        for name, members in arrays.items():
            for i in range(len(members)):
                getattr(k, name)[i] = getattr(k, f"{name}_{i}")[...]

    return call(kernel, "collect", ins, outs, {}, 0, 4_000_000)


def run_patches(static, plain, mains, halo, sizes):
    rows = plain[0][0].shape[1]
    batches = sum(sizes)
    ins = {"sec": (static["sec"], SMEM_SPEC), "pick": vmem(static["pick"])}
    for group, (pair, main) in enumerate(zip(plain, mains)):
        ins[f"plain_0_{group}"], ins[f"plain_1_{group}"], ins[f"main_{group}"] = vmem(pair[0]), vmem(pair[1]), vmem(main)
    for name, array in zip(PIECES[1:], halo):
        ins[name] = vmem(array)
    outs = {"patch": (shape_of(2 * batches, rows, 512), VMEM_SPEC)}

    def kernel(k):
        for kind in range(2):
            for group, size in enumerate(sizes):
                for b in range(size):
                    at = kind * batches + sum(sizes[:group]) + b

                    @pl.when(k.sec[0] == 0)
                    def _(at=at, kind=kind, group=group, b=b):
                        k.patch[at] = getattr(k, f"plain_{kind}_{group}")[b]

                    @pl.when(k.sec[0] == 1)
                    def _(at=at, kind=kind, group=group, b=b):
                        parts = [getattr(k, f"main_{group}")[kind, b]] + [getattr(k, name)[group, kind, b] for name in PIECES[1:]]
                        k.patch[at] = mm(k.pick[...], jnp.concatenate(parts, axis=0), TN).astype(BF)

    return call(kernel, "patches", ins, outs, {}, 0, 0)


def run_places(static, steps, pairs, ups, own, take, land, sizes, tokens):
    batches, groups = sum(sizes), len(sizes)
    ins = {"sec": (static["sec"], SMEM_SPEC), "own": vmem(own), "take": vmem(take), "land_0": vmem(land[0]), "land_1": vmem(land[1])}
    for step, done in enumerate(steps):
        for name in ("y_o", "dx_o"):
            if name in done:
                ins[f"{name}_{step}"] = vmem(done[name])
        ins[f"pair_{step}"] = vmem(pairs[step])
        for side, array in enumerate(ups[step]):
            ins[f"up_{side}_{step}"] = vmem(array)
    outs = {"first": (shape_of(batches, tokens, 512), VMEM_SPEC), "second": (shape_of(batches, tokens, 512, dtype=F32), VMEM_SPEC)}

    def kernel(k):
        for kind, name in enumerate(("y_o", "dx_o")):
            for group, size in enumerate(sizes):
                for b in range(size):
                    at = sum(sizes[:group]) + b

                    def put(value, at=at, kind=kind):
                        if kind == 0:
                            k.first[at] = value.astype(BF)
                        else:
                            k.second[at] = value

                    def here(step, kind=kind, name=name, b=b):
                        value = mm(k.own[...], getattr(k, f"{name}_{step}")[b], TN)
                        return value + mm(k.take[...], getattr(k, f"pair_{step}")[kind, b], TN)

                    @pl.when(k.sec[0] == 0)
                    def _(group=group, kind=kind, put=put, here=here):
                        put(here(group + 2 * kind))

                    @pl.when(k.sec[0] == 1)
                    def _(group=group, kind=kind, b=b, put=put, here=here):
                        value = here(group + 1)
                        for side in range(2):
                            value = value + mm(getattr(k, f"land_{side}")[...], getattr(k, f"up_{side}_{group + 1}")[kind, b], TN)
                        put(value)

    return call(kernel, "places", ins, outs, {}, 0, 0)


def table_onehot():
    code = np.full((SLOT, SLOT), -1, np.int32)
    for u in range(TOKENS):
        for t in range(TOKENS):
            code[u, t] = (t // WIN - u // WIN + WIN - 1) * (2 * WIN - 1) + t % WIN - u % WIN + WIN - 1
    side = (2 * WIN - 1) ** 2
    return (jnp.arange(side, dtype=jnp.int32)[:, None] == jnp.asarray(code.reshape(1, -1))).astype(F32)


def region_mask(layout, section):
    row, mp = lax.axis_index("row"), lax.axis_index("mp")
    window_row = row * WROWS + mp // layout.across
    window_col = (mp % layout.across) * layout.wins + jnp.arange(layout.wins)
    place = jnp.arange(SLOT)
    row_label = jnp.where(window_row == layout.high - 1, 1 + (place // WIN >= WIN - SHIFT).astype(jnp.int32), 0)
    col_label = jnp.where(
        (window_col == WCOLS - 1)[:, None], 1 + (place % WIN >= WIN - SHIFT).astype(jnp.int32)[None], 0
    )
    labels = 3 * row_label[None] + col_label
    differs = labels[:, :, None] != labels[:, None, :]
    term = jnp.where(differs & (section == 1), -100.0, 0.0).astype(F32)
    return jnp.tile(term, (1, 1, GROUP))


def full_patches(layout, mp, tokens):
    wins = layout.wins
    place = jnp.arange(wins * SLOT)
    window, inner = place // SLOT, place % SLOT
    row = (mp // layout.across) * WIN + inner // WIN
    col = ((mp % layout.across) * wins + window) * WIN + inner % WIN
    token = jnp.where(inner < TOKENS, row * (WCOLS * WIN) + col, -1)
    return (token[:, None] == jnp.arange(tokens)[None]).astype(BF)


def whole_patches(layout, mp, tokens_here):
    token = mp * tokens_here + jnp.arange(tokens_here)
    row, col = token // (WCOLS * WIN), token % (WCOLS * WIN)
    window = col // WIN
    owner = (row // WIN) * layout.across + window // layout.wins
    place = owner * layout.wins * SLOT + (window % layout.wins) * SLOT + (row % WIN) * WIN + col % WIN
    return (place[:, None] == jnp.arange(layout.mp_count * layout.wins * SLOT)[None]).astype(BF)


def low_dot(matrix, stack):
    return jnp.einsum("pr,nrd->npd", matrix, stack, preferred_element_type=F32).astype(BF)


def body(
    layer_input,
    out_cotangent,
    norm_one_gain,
    norm_one_bias,
    attend_weight,
    attend_bias,
    position_table,
    output_weight,
    output_bias,
    norm_two_gain,
    norm_two_bias,
    expand_weight,
    expand_bias,
    reduce_weight,
    reduce_bias,
):
    row_count, mp_count = lax.axis_size("row"), lax.axis_size("mp")
    section, mp = lax.axis_index("section"), lax.axis_index("mp")
    layout = Layout(row_count, mp_count)
    tables = Tables(layout.wins)
    put = jnp.asarray(tables.put, BF)
    pick = jnp.asarray(tables.pick, BF)
    batches, tokens_here, width = layer_input.shape
    heads_here = attend_weight.shape[2]
    hidden_here = expand_weight.shape[2]
    row = lax.axis_index("row")
    sec = jnp.stack([section, row, mp]).astype(jnp.int32)
    paired = layout.across == 2 and row_count == 4
    first = section == 0

    flat = jnp.concatenate([attend_bias[0].reshape(-1), position_table[0].reshape(-1), expand_bias[0].reshape(-1)])
    wq_rows = attend_weight[0].transpose(1, 2, 0).reshape(heads_here, 3, 32, width)
    if paired:
        quarter = lambda array: take_at(array.reshape(4, -1, width), row)
        shards = (wq_rows.transpose(1, 0, 2, 3), output_weight[0], expand_weight[0], reduce_weight[0])
        quarters = [quarter(array) for array in shards]
        offsets = np.cumsum([0] + [array.shape[0] for array in quarters])[:-1].tolist()
        pieces, last_in = gather_quarter(jnp.concatenate(quarters))
        last_in, flat, layer_input, out_cotangent = lax.optimization_barrier((last_in, flat, layer_input, out_cotangent))
        after = ring(flat, "mp")
        flat_all = natural_ring([flat, after, ring(after, "mp"), ring(flat, "mp", -1)], mp)
    else:
        wq_all = lax.all_gather(wq_rows, "mp", axis=0).reshape(4, GROUP, 3, 32, width).transpose(0, 2, 1, 3, 4)
        wq_all = wq_all.reshape(4, GROUP * 96, width)
        wo_all = lax.all_gather(output_weight[0], "mp", axis=0).reshape(-1, width)
        w1_all = lax.all_gather(expand_weight[0], "mp", axis=0)
        w2_all = lax.all_gather(reduce_weight[0], "mp", axis=0)
        flat_all = lax.all_gather(flat, "mp", axis=0)
        whole = (wq_all, wo_all, w1_all, w2_all)
        weights = (whole, None, None, tuple(array.shape for array in whole))
    cut_one = heads_here * 64
    cut_two = cut_one + heads_here * position_table.shape[2]
    bias_all = flat_all[:, :cut_one].reshape(4, GROUP, 2, 32)
    table_all = flat_all[:, cut_one:cut_two].reshape(-1, position_table.shape[2])
    b1 = flat_all[:, cut_two:]
    bq = jnp.stack([bias_all[:, :, 0], jnp.zeros_like(bias_all[:, :, 0]), bias_all[:, :, 1]], axis=1).reshape(4, -1)
    onehot = table_onehot()
    bias = jnp.dot(table_all, onehot, precision=highest).reshape(4, GROUP, SLOT, SLOT).transpose(0, 2, 1, 3)
    bias = bias.reshape(4, SLOT, GROUP * SLOT) + jnp.where(jnp.arange(SLOT) < TOKENS, 0.0, -1e30)[None, :, None]
    vec = jnp.concatenate(
        [norm_one_gain, norm_one_bias, output_bias, norm_two_gain, norm_two_bias, reduce_bias, jnp.zeros((2, width), F32)]
    )
    region = region_mask(layout, section)

    taken = jnp.where(first, layer_input, out_cotangent)
    if paired:
        keep, take, send = pair_tables(layout.wins)
        side = mp % 2
        keep = lax.dynamic_index_in_dim(jnp.asarray(keep, BF), side, 0, keepdims=False)
        take = lax.dynamic_index_in_dim(jnp.asarray(take, BF), side, 0, keepdims=False)
        send = jnp.asarray(send, BF)
        arrived = swap(low_dot(send, taken), "mp", 1)
        pin = low_dot(jnp.concatenate([keep, take], axis=1), jnp.concatenate([taken, arrived], axis=1))
        own, give, take, up, land = (jnp.asarray(table, BF) for table in placing_tables(layout.wins))
        own, give, take = (take_at(take_at(table, section), side) for table in (own, give, take))
        land = jnp.where((section == 1) & (side == 0), land, 0)
    else:
        everything = lax.all_gather(taken, "mp", axis=1, tiled=True)
        pin = low_dot(full_patches(layout, mp, everything.shape[1]), everything)
    groups = -(-batches // TOGETHER)
    sizes = [min(TOGETHER, batches - TOGETHER * group) for group in range(groups)]
    pin = jnp.pad(pin, ((0, TOGETHER * groups - batches), (0, 0), (0, 0)))
    cuts = np.cumsum(tables.sizes)[:-1].tolist()
    targets = halo_inside(layout, jnp.split(low_dot(pick, pin), cuts, axis=1), False)
    if paired:
        arrays = [array for array, _ in pieces]
        arrays[0], pin, targets, bias, region, bq, b1 = lax.optimization_barrier((arrays[0], pin, targets, bias, region, bq, b1))
        held = tuple(places for _, places in pieces)
        held += tuple(tuple((bits + 1, back) for bits, back in places) for places in held)
        weights = (
            arrays + [swap(array, "row", 1) for array in arrays],
            held,
            offsets,
            ((4, GROUP * 96, width), (4 * GROUP * 32, width), (mp_count, width, hidden_here), (mp_count, hidden_here, width)),
        )

    static = dict(
        sec=sec, weights=weights, pin=pin, targets=targets, put=put, pick=pick, vec=vec, bq=bq, b1=b1, bias=bias, region=region
    )
    if paired:
        static |= dict(give=give, up=up)
    size_of = lambda group: sizes[group] if 0 <= group < groups else 0
    landed = None
    steps, pairs, ups = [], [], []
    for step in range(groups + 1):
        counts = (size_of(step), size_of(step - 1), size_of(step - 2), size_of(step - 1))
        which = (min(step, groups - 1), max(step - 1, 0))
        done = run_step(tables, static, landed, counts, which, steps[max(step - 2, 0)] if step else None)
        steps.append(done)
        sends = [done["s_" + name] for name in PIECES]
        pair, up_piece = done.get("f_pair"), done.get("f_up")
        if step == groups:
            sends = [piece[: sizes[-1]] for piece in sends]
        if paired:
            sends, pairs, ups = lax.optimization_barrier((sends, pairs, ups))
        landed = halo_swap(layout, sends, step == groups)
        if paired:
            if step == groups:
                break
            landed, pair, up_piece = lax.optimization_barrier((landed, pair, up_piece))
            pairs = pairs + [swap(pair, "mp", 1)]
            ups = ups + [[lax.ppermute(up_piece, AXES, route) for route in layout.up_routes()] if step else []]

    if not paired:
        halo = collect({name: [done["h_" + name] for done in steps[1:]] for name in PIECES[1:]})
        halo = [halo[name] for name in PIECES[1:]]
        flat_halo = halo_inside(layout, [None] + [array.reshape((-1,) + array.shape[3:]) for array in halo], True)[1:]
        halo = [flat.reshape(array.shape) for flat, array in zip(flat_halo, halo)]

    ahead_names = ("act", "n2", "a", "ctx")
    early = TOGETHER * (groups - 1)

    def gradient(names, terms, shapes, within, quartered, base, after):
        members, slots = {}, {}
        for name in names:
            shifts = (0, 1) if name in ahead_names else (2, 1)
            slots[name] = [[(batch // TOGETHER + shift, batch % TOGETHER) for batch in within] for shift in shifts]
            used = sorted({step for places in slots[name] for step, _ in places})
            members[name] = {step: steps[step][name + "_o"] for step in used}
        return run_weight_grad(dict(static, sec=after), members, slots, terms, shapes, quartered, base)

    mlp_names = ("act", "g", "n2", "dh")
    mlp_terms = (("act", "g", "left", "d2", 0, hidden_here), ("n2", "dh", "right", "d1", 0, width))
    mlp_shapes = {"d2": (mp_count, hidden_here, width), "d1": (mp_count, width, hidden_here)}
    base = gradient(mlp_names, mlp_terms, mlp_shapes, range(early), False, {}, sec)
    base = {name: base[name + "_o"] for name in mlp_shapes}
    landed, base = lax.optimization_barrier((landed, base))
    after = sec
    if paired:
        base, pair, up_piece = lax.optimization_barrier((base, pair, up_piece[:, : sizes[-1]]))
        pairs = pairs + [swap(pair, "mp", 1)]
        ups = ups + [[lax.ppermute(up_piece, AXES, route) for route in layout.up_routes()]]
        after, pairs, ups = lax.optimization_barrier((sec, pairs, ups))

    counts = (0, 0, sizes[-1], 0)
    which = (groups - 1, groups - 1)
    last = run_step(tables, static, landed, counts, which, steps[-2], attention=False)
    steps.append(last)
    mlp = gradient(mlp_names, mlp_terms, mlp_shapes, range(early, batches), paired, base, after)
    end = run_step(tables, static, None, counts, which, {**steps[-3], **last}, mlp=False)
    smalls = [done["small"] for done in steps[1:]] + [end["small"]]
    biases = [done["dbias"] for done in steps[1:-1]] + [end["dbias"]]
    if paired:
        d2, d1 = (mlp[name + "_keep"] + swap(mlp[name + "_send"], "row", 1) for name in ("d2", "d1"))
        d2, d1, end_dqkv = lax.optimization_barrier((d2, d1, end["dqkv_o"]))
        end = {**end, "dqkv_o": end_dqkv}
    steps[-1] = {**last, **end}
    heads = gradient(
        ("dqkv", "a", "ctx", "gm"),
        (("dqkv", "a", "left", "da", 0, GROUP * 96), ("ctx", "gm", "left", "da", GROUP * 96, GROUP * 32)),
        {"da": (4, GROUP * 128, width)},
        range(batches),
        paired,
        {},
        sec,
    )
    smalls, biases, _ = lax.optimization_barrier((smalls, biases, heads))
    small, dbias = sum(smalls), sum(biases)
    table = dbias.reshape(SLOT, 4 * GROUP, SLOT).transpose(1, 0, 2).reshape(4 * GROUP, -1)
    table = jnp.dot(table, onehot.T, precision=highest)
    if paired:
        count = table.size
        table = jnp.pad(table.reshape(-1), (0, -count % 2048)).reshape(-1, 2048)
        sums = jnp.concatenate([small, table])
        high, core = row // 2, row % 2
        gate = lax.optimization_barrier
        term = lambda part, step: take_at(part, (mp - 2 - step) % mp_count)

        def joined(pair, crossed):
            whole = jnp.stack([jnp.where(core == 0, pair, crossed), jnp.where(core == 0, crossed, pair)], axis=1)
            return whole.astype(F32).reshape(-1, width)

        def ordered(mine, other):
            return jnp.stack([jnp.where(high == 0, mine, other), jnp.where(high == 0, other, mine)])

        da_came, pair_came, sums_came = swap(heads["da_send"], "row", 1), swap(end["f_pair"], "mp", 1), swap(sums, "row", 1)
        d2_came, d1_came = ring(take_at(d2, (mp - 1) % mp_count), "mp"), swap(take_at(d1, 1 - high, 1), "row", 2)
        da = heads["da_keep"] + da_came
        mine, other = take_at(da, high, 1), take_at(da, 1 - high, 1)
        da_came = swap(other, "row", 2)
        d2_came, d1_came, pair_came, sums_came, _ = gate((d2_came, d1_came, pair_came, sums_came, other))
        d2_total, d1, sums = d2_came + term(d2, 0), take_at(d1, high, 1) + d1_came, sums + sums_came
        d2_came, d1_came, sums_came = ring(d2_total, "mp"), ring(take_at(d1, (mp - 1) % mp_count), "mp"), swap(sums, "row", 2)
        placed = run_places(static, steps, pairs + [pair_came], ups + [[]], own, take, land, sizes, tokens_here)
        da_came, first_out, second_out = gate((da_came, placed["first"], placed["second"]))
        da = mine + da_came
        sending = take_at(da, (mp - 1) % mp_count)
        da_came = ring(sending, "mp")
        d2_came, d1_came, sums_came, _ = gate((d2_came, d1_came, sums_came, sending))
        d2_total, d1_total, sums = d2_came + term(d2, 1), d1_came + term(d1, 0), sums + sums_came
        d2_came, d1_came, sums_came = ring(d2_total, "mp"), ring(d1_total, "mp"), swap(sums, "mp", 1)
        sending = da_came + term(da, 0)
        da_came = ring(sending, "mp")
        d2_came, d1_came, sums_came, _ = gate((d2_came, d1_came, sums_came, sending))
        d2, d1_total, sums = d2_came + term(d2, 2), d1_came + term(d1, 1), sums + sums_came
        d2_came, d1_came, sums_came = swap(d2, "row", 2), ring(d1_total, "mp"), swap(sums, "mp", 2)
        sending = da_came + term(da, 1)
        da_came = ring(sending, "mp")
        d2_came, d1_came, sums_came, _ = gate((d2_came, d1_came, sums_came, sending))
        d2, d1, sums = d2 + d2_came, d1_came + term(d1, 2), sums + sums_came
        d2_came, d1_came = swap(d2, "row", 1), swap(d1, "row", 2)
        da = da_came + term(da, 2)
        da_came = swap(da, "row", 2)
        d2_came, d1_came, _ = gate((d2_came, d1_came, da))
        d2, d1 = joined(d2, d2_came), ordered(d1, d1_came)
        d1_came = swap(d1, "row", 1)
        da = ordered(da, da_came)
        d1 = joined(d1, d1_came)
        da = joined(da, swap(da, "row", 1))
        dq, do = da[: GROUP * 96].reshape(3, GROUP, 32, width), da[GROUP * 96 :]
        dq = dq.transpose(3, 1, 0, 2).reshape(attend_weight.shape[1:])
        small, table = sums[: small.shape[0]], sums[small.shape[0] :].reshape(-1)[:count].reshape(4 * GROUP, -1)
    else:

        def shared(parts):
            part = lax.psum_scatter(parts, "mp", scatter_dimension=0, tiled=False)
            return lax.psum(part, "row").astype(F32)

        da = heads["da_o"]
        dq = da[:, : GROUP * 96].reshape(4, 3, GROUP, 32, width).transpose(0, 2, 1, 3, 4).reshape(mp_count, heads_here * 96, width)
        d2, d1, do = shared(mlp["d2_o"]), shared(mlp["d1_o"]), shared(da[:, GROUP * 96 :].reshape(mp_count, heads_here * 32, width))
        dq = shared(dq).T.reshape(attend_weight.shape[1:])
        small, table = lax.psum((small, table), ("row", "mp"))
    shift = small[3, :1536].reshape(4, 3, GROUP, 32)
    shift = jnp.concatenate([shift[:, 0], shift[:, 2]], axis=-1).reshape(4 * GROUP, 64)
    mine = lambda array: lax.dynamic_index_in_dim(array.reshape((mp_count, -1) + array.shape[1:]), mp, 0, keepdims=False)

    if not paired:
        plain = [(steps[group]["y_o"], steps[group + 2]["dx_o"]) for group in range(groups)]
        mains = [steps[group + 1]["h_main"] for group in range(groups)]
        made = run_patches(static, plain, mains, halo, sizes)
        everything = lax.all_gather(made["patch"], "mp", axis=1, tiled=True)
        placed = low_dot(whole_patches(layout, mp, tokens_here), everything)
        first_out, second_out = placed[:batches], placed[batches:].astype(F32)

    return (
        first_out[None],
        second_out[None],
        small[1, 1024:1536][None],
        small[1, 1536:2048][None],
        dq[None],
        mine(shift)[None],
        mine(table)[None],
        do.reshape(output_weight.shape),
        small[1, 512:1024][None],
        small[2, 0:512][None],
        small[2, 512:1024][None],
        d1[None],
        mine(small[0])[None],
        d2[None],
        small[1, 0:512][None],
    )


def solution(mesh):
    return jax.shard_map(
        body,
        mesh=mesh,
        in_specs=(
            P(None, ("row", "mp"), None),
            P(None, ("row", "mp"), None),
            P("section", None),
            P("section", None),
            P("section", None, "mp", None),
            P("section", "mp", None),
            P("section", "mp", None),
            P("section", "mp", None, None),
            P("section", None),
            P("section", None),
            P("section", None),
            P("section", None, "mp"),
            P("section", "mp"),
            P("section", "mp", None),
            P("section", None),
        ),
        out_specs=(
            P("section", None, ("row", "mp"), None),
            P("section", None, ("row", "mp"), None),
            P("section", None),
            P("section", None),
            P("section", None, "mp", None),
            P("section", "mp", None),
            P("section", "mp", None),
            P("section", "mp", None, None),
            P("section", None),
            P("section", None),
            P("section", None),
            P("section", None, "mp"),
            P("section", "mp"),
            P("section", "mp", None),
            P("section", None),
        ),
        check_vma=False,
    )
```

```python
import functools

import jax
import jax.numpy as jnp
import numpy as np
from jax import lax
from jax.experimental import pallas as pl
from jax.experimental.pallas import tpu as pltpu
from jax.sharding import PartitionSpec as P

WIN = 7
SHIFT = 3
WCOLS = 8
WROWS = 2
TOKENS = WIN * WIN
SLOT = 64
GROUP = 4
SECTION, ROW, MP = AXES = ("section", "row", "mp")
EPS = 1e-05
BF = jnp.bfloat16
F32 = jnp.float32
NN = (((1,), (0,)), ((), ()))
NT = (((1,), (1,)), ((), ()))
TN = (((0,), (0,)), ((), ()))
VMEM_LIMIT = 56 * 1024 * 1024
highest = lax.Precision.HIGHEST


def mm(left, right, dims=NN):
    return lax.dot_general(left, right, dims, preferred_element_type=F32)


def up16(count):
    return -(-count // 16) * 16


def patch_place(row, col):
    return (col // WIN) * SLOT + row * WIN + col % WIN


class Tables:
    def __init__(self, wins):
        self.wins = wins
        self.rows = wins * SLOT
        cols = wins * WIN
        wide = range(SHIFT, cols)
        thin = range(SHIFT)
        low, high = range(SHIFT, WIN), range(SHIFT)
        pieces = [(low, wide), (high, wide), (low, thin), (high, thin)]
        self.sizes = [up16(len(a) * len(b)) for a, b in pieces]
        self.total = sum(self.sizes)
        pick = np.zeros((self.total, self.rows), np.float32)
        put = np.zeros((self.rows, self.total), np.float32)
        at = 0
        for (rows, columns), size in zip(pieces, self.sizes):
            spot = at
            for row in rows:
                for col in columns:
                    pick[spot, patch_place(row, col)] = 1
                    put[patch_place((row - SHIFT) % WIN, (col - SHIFT) % cols), spot] = 1
                    spot += 1
            at += size
        self.pick, self.put = pick, put


def pair_tables(wins):
    cols = wins * WIN
    tokens = WIN * cols
    keep = np.zeros((2, wins * SLOT, tokens), np.float32)
    take = np.zeros((2, wins * SLOT, up16(SHIFT * cols)), np.float32)
    send = np.zeros((up16(SHIFT * cols), tokens), np.float32)
    for seg in range(SHIFT):
        for col in range(cols):
            send[seg * cols + col, (2 * seg + 1) * cols + col] = 1
    for side in range(2):
        for row in range(WIN):
            for col in range(cols):
                place = patch_place(row, col)
                own = row <= SHIFT if side == 0 else row >= SHIFT
                if own:
                    seg = row if side == 0 else row - SHIFT
                    keep[side, place, 2 * seg * cols + col] = 1
                else:
                    seg = row - SHIFT - 1 if side == 0 else row
                    take[side, place, seg * cols + col] = 1
    return keep, take, send


def placing_tables(wins):
    cols, tokens, most = wins * WIN, WIN * wins * WIN, up16(SHIFT * (wins * WIN + 1))
    own = np.zeros((2, 2, wins * SLOT, tokens), np.float32)
    give = np.zeros((2, 2, wins * SLOT, most), np.float32)
    take = np.zeros((2, 2, most, tokens), np.float32)
    up = np.zeros((wins * SLOT, most), np.float32)
    land = np.zeros((2, most, tokens), np.float32)
    half = SHIFT * 2 * cols + cols

    def holder(row, col):
        token = row * 2 * cols + col
        return (0, token) if token < half else (1, token - half)

    for section in range(2):
        for side in range(2):
            given, raised = 0, 0
            for row in range(WIN):
                for col in range(cols):
                    place = patch_place(row, col)
                    real_row = row + SHIFT * section
                    real_col = (side * cols + col + SHIFT * section) % (2 * cols)
                    if real_row >= WIN:
                        up[place, raised] = 1
                        land[side, raised, holder(real_row - WIN, real_col)[1]] = 1
                        raised += 1
                        continue
                    keeper, token = holder(real_row, real_col)
                    if keeper == side:
                        own[section, side, place, token] = 1
                    else:
                        give[section, side, place, given] = 1
                        take[section, keeper, given, token] = 1
                        given += 1
    return own, give, take, up, land


class Layout:
    def __init__(self, row_count, mp_count):
        self.row_count, self.mp_count = row_count, mp_count
        self.across = mp_count // WROWS
        self.wins = WCOLS // self.across
        self.high = row_count * WROWS

    def device(self, section, window_row, place):
        window_row, place = window_row % self.high, place % self.across
        row = window_row // WROWS
        return (section * self.row_count + row) * self.mp_count + (window_row % WROWS) * self.across + place

    def route(self, source, target, up, back):
        return [
            (self.device(source, window_row, place), self.device(target, window_row - up, place - back))
            for window_row in range(self.high)
            for place in range(self.across)
        ]


    def pair_route(self, section):
        return [
            (self.device(section, window_row, side), self.device(section, window_row, 1 - side))
            for window_row in range(self.high)
            for side in range(2)
        ]

    def up_routes(self):
        return [
            [(self.device(1, window_row, side), self.device(1, window_row + 1, 0)) for window_row in range(self.high)] for side in range(2)
        ]


HALO = ((0, 0), (1, 0), (0, 1), (1, 1))


def halo_swap(layout, parts, back_only):
    result = []
    for part, by in zip(parts, HALO):
        there = layout.route(0, 1, *by)
        result.append(lax.ppermute(part, AXES, [(b, a) for a, b in there] + ([] if back_only else there)))
    return result


def halo_inside(layout, parts, back):
    result = [parts[0]]
    for part, by in zip(parts[1:], HALO[1:]):
        there = layout.route(1, 1, *by)
        result.append(lax.ppermute(part, AXES, [(b, a) for a, b in there] if back else there))
    return result


def ring(shard, axis, by=1):
    count = lax.axis_size(axis)
    return lax.ppermute(shard, axis, [(i, (i + by) % count) for i in range(count)])


def swap(shard, axis, bit):
    return lax.ppermute(shard, axis, [(i, i ^ bit) for i in range(lax.axis_size(axis))])


def natural_ring(shards, mp):
    stacked, count = jnp.stack(shards), len(shards)
    return jnp.stack([lax.dynamic_index_in_dim(stacked, (mp - j) % count, 0, keepdims=False) for j in range(count)])


def gather_quarter(quarter):
    near, far = ring(quarter, MP), ring(quarter, MP, -1)
    further = ring(near, MP)
    across = lambda piece: swap(piece, ROW, 2)
    return (
        [(jnp.stack([quarter, near, across(quarter), across(near)]), ((0, 0), (0, 1), (2, 0), (2, 1)))]
        + [(jnp.stack([far, further, across(far), across(further)]), ((0, 3), (0, 2), (2, 3), (2, 2)))]
    ), near, further


def take_at(array, index, axis=0):
    return lax.dynamic_index_in_dim(array, index, axis, keepdims=False)


def head_masks(dtype):
    lane = lax.broadcasted_iota(jnp.int32, (1, GROUP * 32), 1)
    return [jnp.where(lane // 32 == h, 1.0, 0.0).astype(dtype) for h in range(GROUP)]


def spread_heads(block, masks):
    return jnp.concatenate([block * mask for mask in masks], axis=0)


def fold_heads(tall, masks):
    total = tall[:SLOT] * masks[0]
    for h in range(1, GROUP):
        total = total + tall[h * SLOT : (h + 1) * SLOT] * masks[h]
    return total


def centre(values):
    middle = jnp.mean(values, axis=-1, keepdims=True)
    centred = values - middle
    scale = lax.rsqrt(jnp.mean(centred * centred, axis=-1, keepdims=True) + EPS)
    return centred * scale, scale


KEPT = ("gp", "mid", "qkv", "prob", "x")
WEIGHTS = ("wq", "wo", "w1", "w2")
AHEAD = ("act", "n2", "a", "ctx")
TOGETHER = 2


class Refs:
    pass


class Copies:
    def __init__(self, sems):
        self.sems, self.used, self.sent = sems, 0, []

    def sem(self, count=1):
        self.used += count
        return self.used - count

    def at(self, index):
        return self.sems.at[index]

    def ship(self, b, make):
        first = self.sem(TOGETHER)
        maker = lambda b: make(b, self.at(first + b))
        maker(b).start()
        self.sent.append(maker)

    def finish(self, count):
        for b in range(TOGETHER):

            @pl.when(b < count)
            def _(b=b):
                for maker in self.sent:
                    maker(b).wait()

        self.sent = []


def arrival(target, sem):
    return pltpu.make_async_copy(target, target, sem)


def load_weights(k, kinds, held, offsets):
    waits = {}
    for name in kinds:
        kind, target, sem = WEIGHTS.index(name), getattr(k, name), k.copies.at(k.copies.sem())
        waits[name] = arrival(target, sem)
        if held is None:
            pltpu.make_async_copy(getattr(k, name + "_whole"), target, sem).start()
            continue
        flat, shards = len(target.shape) == 2, 4
        high = target.shape[-2] // (4 * shards if flat else 4)
        for number, places in enumerate(held):
            for piece, (bits, back) in enumerate(places):
                quarter = k.sec[1] ^ bits
                shard = lax.rem(k.sec[2] + (shards - back), shards)
                start = quarter * high
                if flat:
                    start = start + shard * (4 * high)
                rows = pl.ds(pl.multiple_of(start, high), high)
                place = target.at[rows, :] if flat else target.at[shard, rows, :]
                source = getattr(k, f"pieces_{number}").at[piece, pl.ds(offsets[kind], high), :]
                pltpu.make_async_copy(source, place, sem).start()
    return waits


def window_rows(w):
    return slice(w * SLOT, (w + 1) * SLOT)


def result(k, name, cols=None):
    def make(b, sem):
        src = getattr(k, name)
        src = src.at[0, b] if name in KEPT else src.at[b]
        dst = getattr(k, name + "_o").at[b]
        if cols is not None:
            src, dst = src.at[:, cols], dst.at[:, cols]
        return pltpu.make_async_copy(src, dst, sem)

    return make


def forward_part(k, wins, wait, b):
    x, qkv, prob, mid, gp = (getattr(k, name).at[0, b] for name in ("x", "qkv", "prob", "mid", "gp"))
    a, ctx, n2, act, y = (getattr(k, name).at[b] for name in ("a", "ctx", "n2", "act", "y"))
    ship = lambda name, cols=None: k.copies.ship(b, result(k, name, cols))

    @pl.when(k.sec[0] == 0)
    def _():
        x[...] = k.pin[b]

    if k.landed:

        @pl.when(k.sec[0] == 1)
        def _():
            joined = jnp.concatenate([k.p_main[b], k.p_row[b], k.p_col[b], k.p_cor[b]], axis=0)
            x[...] = mm(k.put[...], joined).astype(BF)

    for w in range(wins):
        rows = window_rows(w)
        hat, _ = centre(x[rows, :].astype(F32))
        a[rows, :] = (hat * k.vec[0:1, :] + k.vec[1:2, :]).astype(BF)
    ship("x")
    ship("a")
    wait("wq")
    lane = lax.broadcasted_iota(jnp.int32, (1, 512), 1)
    for part in range(3):
        cols = slice(part * 512, (part + 1) * 512)
        factor = jnp.where(lax.rem(lane + part * 512, 384) < GROUP * 32, 32 ** (-0.5), 1.0)
        pr = mm(a[...], k.wq[cols, :], NT) + k.bq[0:1, cols]
        qkv[:, cols] = (pr * factor).astype(BF)
    ship("qkv")
    wait("bias")
    wait("region")
    masks, masks_f = head_masks(BF), head_masks(F32)
    for w in range(wins):
        rows = window_rows(w)
        for g in range(4):
            query = qkv[rows, g * 384 : g * 384 + 128]
            key = qkv[rows, g * 384 + 128 : g * 384 + 256]
            value = qkv[rows, g * 384 + 256 : g * 384 + 384]
            scores = mm(key, spread_heads(query, masks), NT) + k.bias[g] + k.region[w]
            top = jnp.max(scores, axis=0, keepdims=True)
            e = jnp.exp(scores - top)
            low = (e * (1.0 / jnp.sum(e, axis=0, keepdims=True))).astype(BF)
            prob[rows, g * 256 : (g + 1) * 256] = low
            ctx[rows, g * 128 : (g + 1) * 128] = fold_heads(mm(low, value, TN), masks_f).astype(BF)
    ship("prob")
    ship("ctx")
    wait("wo")
    mid[...] = x[...].astype(F32) + (mm(ctx[...], k.wo[...]) + k.vec[2:3, :])
    ship("mid")
    for w in range(wins):
        rows = window_rows(w)
        hat, _ = centre(mid[rows, :])
        n2[rows, :] = (hat * k.vec[3:4, :] + k.vec[4:5, :]).astype(BF)
    ship("n2")
    wait("w1")
    wait("w2")
    parts, _, width = k.w1.shape
    for j in range(parts):
        cols = slice(j * width, (j + 1) * width)
        hidden = mm(n2[...], k.w1[j]) + k.b1[j : j + 1, :]
        phi = 0.5 + 0.5 * lax.erf(hidden * 0.7071067811865476)
        low = (hidden * phi).astype(BF)
        act[:, cols] = low
        gp[:, cols] = (phi + hidden * (jnp.exp(hidden * hidden * -0.5) * 0.3989422804014327)).astype(BF)
        ship("act", cols)
        ship("gp", cols)
    y[...] = (mid[...] + k.vec[5:6, :] + mm(act[...], k.w2[...])).astype(BF)
    ship("y")

    put_partner(k, 0, b, y)

    @pl.when(k.sec[0] == 0)
    def _():
        put_pieces(k, "s_", b, mm(k.pick[...], y[...]).astype(BF))

    @pl.when(k.sec[0] == 1)
    def _():
        put_neighbours(k, 0, b, y)


def put_pieces(k, first, b, joined):
    at = 0
    for name in PIECES:
        ref = getattr(k, first + name)
        ref[b] = joined[at : at + ref.shape[1]]
        at += ref.shape[1]


def put_partner(k, kind, b, result):
    if hasattr(k, "f_pair"):
        k.f_pair[kind, b] = mm(k.give[...], result[...], TN).astype(BF)


def put_neighbours(k, kind, b, result):
    if hasattr(k, "f_up"):
        k.f_up[kind, b] = mm(k.up[...], result[...], TN).astype(BF)
        return
    joined = mm(k.put[...], result[...], TN).astype(BF)
    at = 0
    for name in PIECES:
        ref = getattr(k, "h_" + name)
        ref[kind, b] = joined[at : at + ref.shape[2]]
        at += ref.shape[2]


def norm_back(grad, hat, scale, gain):
    inner = grad * gain
    return scale * (inner - jnp.mean(inner, axis=-1, keepdims=True) - hat * jnp.mean(inner * hat, axis=-1, keepdims=True))


def column_sum(values):
    return jnp.sum(values, axis=0, keepdims=True)


def backward_mlp(k, wins, wait, old, b):
    slot = 1 - k.sec[0]
    gp, mid = k.gp.at[slot, b], k.mid.at[slot, b]
    out_grad, dhs, gm, dmid = k.g.at[b], k.dh.at[b], k.gm.at[b], k.dmid.at[b]
    ship = lambda name, cols=None: k.copies.ship(b, result(k, name, cols))

    @pl.when(k.sec[0] == 0)
    def _():
        joined = jnp.concatenate([k.p_main[b], k.p_row[b], k.p_col[b], k.p_cor[b]], axis=0)
        out_grad[...] = mm(k.pick[...], joined, TN).astype(BF)

    @pl.when(k.sec[0] == 1)
    def _():
        joined = jnp.concatenate([k.c_main[b], k.c_row[b], k.c_col[b], k.c_cor[b]], axis=0)
        out_grad[...] = mm(k.put[...], joined).astype(BF)

    ship("g")
    parts, _, width = k.w1.shape
    wait("w2")
    wait("w1")
    old("gp", b)
    total = None
    for j in range(parts):
        cols = slice(j * width, (j + 1) * width)
        dh = (mm(out_grad[...], k.w2[cols, :], NT) * gp[:, cols].astype(F32)).astype(BF)
        dhs[:, cols] = dh
        k.small[0:1, cols] += column_sum(dh.astype(F32))
        ship("dh", cols)
        part = mm(dh, k.w1[j], NT)
        total = part if total is None else total + part
    k.dn[...] = total
    old("mid", b)
    sums = [0.0] * 4
    for w in range(wins):
        rows = window_rows(w)
        grad = k.dn[rows, :]
        out = out_grad[rows, :].astype(F32)
        hat, scale = centre(mid[rows, :])
        whole = out + norm_back(grad, hat, scale, k.vec[3:4, :])
        dmid[rows, :] = whole
        low = whole.astype(BF)
        gm[rows, :] = low
        for i, term in enumerate((out, low.astype(F32), grad * hat, grad)):
            sums[i] = sums[i] + column_sum(term)
    ship("gm")
    if hasattr(k, "dmid_o"):
        ship("dmid")
    k.small[1:2, 0:512] += sums[0]
    k.small[1:2, 512:1024] += sums[1]
    k.small[2:3, 0:512] += sums[2]
    k.small[2:3, 512:1024] += sums[3]


def backward_attention(k, wins, wait, old, b, reload):
    slot = 1 - k.sec[0]
    qkv, prob, x = k.qkv.at[slot, b], k.prob.at[slot, b], k.x.at[slot, b]
    gm, dmid, dqkv, dx = k.gm.at[b], k.dmid.at[b], k.dqkv.at[b], k.dx.at[b]
    ship = lambda name, cols=None: k.copies.ship(b, result(k, name, cols))
    wait("wo")
    if reload:
        old("gm", b)
    k.dctx[...] = mm(gm[...], k.wo[...], NT).astype(BF)
    old("qkv", b)
    old("prob", b)
    masks, masks_f = head_masks(BF), head_masks(F32)
    for w in range(wins):
        rows = window_rows(w)
        for g in range(4):
            at = g * 384
            query = qkv[rows, at : at + 128]
            key = qkv[rows, at + 128 : at + 256]
            value = qkv[rows, at + 256 : at + 384]
            do = spread_heads(k.dctx[rows, g * 128 : (g + 1) * 128], masks)
            low = prob[rows, g * 256 : (g + 1) * 256]
            p = low.astype(F32)
            dp = mm(value, do, NT)
            ds = (p * (dp - column_sum(p * dp))).astype(BF)
            k.dbias[:, g * 256 : (g + 1) * 256] += ds.astype(F32)
            dv = mm(low, do).astype(BF)
            dk = mm(ds, spread_heads(query, masks)).astype(BF)
            dq = (fold_heads(mm(ds, key, TN), masks_f) * 32 ** (-0.5)).astype(BF)
            dqkv[rows, at : at + 128] = dq
            dqkv[rows, at + 128 : at + 256] = dk
            dqkv[rows, at + 256 : at + 384] = dv
    ship("dqkv")
    wait("wq")
    k.small[3:4, 0:1536] += column_sum(dqkv[...].astype(F32))
    k.dn[...] = mm(dqkv[...], k.wq[...])
    old("x", b)
    if reload:
        old("dmid", b)
    sums = [0.0] * 2
    for w in range(wins):
        rows = window_rows(w)
        grad = k.dn[rows, :]
        hat, scale = centre(x[rows, :].astype(F32))
        dx[rows, :] = (dmid[rows, :] + norm_back(grad, hat, scale, k.vec[0:1, :])).astype(BF)
        sums[0] = sums[0] + column_sum(grad * hat)
        sums[1] = sums[1] + column_sum(grad)
    ship("dx")
    k.small[1:2, 1024:1536] += sums[0]
    k.small[1:2, 1536:2048] += sums[1]
    put_partner(k, 1, b, dx)
    if hasattr(k, "s_main"):

        @pl.when(k.sec[0] == 1)
        def _():
            put_pieces(k, "s_", b, mm(k.put[...], dx[...], TN).astype(BF))
            put_neighbours(k, 1, b, dx)


def loop(count, most, run):
    def once(b, carry):
        run(b)
        return carry

    if most:
        lax.fori_loop(0, count, once, 0)


def step_kernel(wins, held, offsets, counts, mlp, attention, terms, quartered, k):
    k.copies = copies = Copies(k.sems)
    ahead, back = max(counts[:2]), max(counts[2:])
    number = lambda pair: jnp.where(k.sec[0] == 0, pair[0], pair[1])
    forwards, backwards = number(counts[:2]), number(counts[2:])
    kinds = WEIGHTS if ahead else (("w2", "w1") if mlp else ()) + (("wo", "wq") if attention else ())
    waits = load_weights(k, kinds[:1], held, offsets)
    if ahead:
        for name in ("bias", "region"):
            copy = pltpu.make_async_copy(getattr(k, name + "_h"), getattr(k, name), copies.at(copies.sem()))
            copy.start()
            waits[name] = copy
    fetched = {}
    if back:
        reload = attention and not mlp
        for name in k.needed:
            first = copies.sem(TOGETHER)

            def fetch(b, name=name, first=first):
                target = getattr(k, name)
                target = target.at[1, b] if name in KEPT else target.at[b]
                return pltpu.make_async_copy(getattr(k, "old_" + name).at[b], target, copies.at(first + b))

            fetched[name] = fetch
            for b in range(back):
                pl.when((k.sec[0] == 0) & (b < backwards))(lambda b=b, fetch=fetch: fetch(b).start())
    waits |= load_weights(k, kinds[1:], held, offsets)
    targets = tuple(dict.fromkeys(term[3] for term in terms))
    bases = [pltpu.make_async_copy(getattr(k, name + "_b"), getattr(k, name), copies.at(copies.sem())) for name in targets]
    for copy in bases:
        copy.start()

    def all_weights():
        for copy in waits.values():
            copy.wait()

    def old(name, b):
        if name in fetched:
            pl.when(k.sec[0] == 0)(lambda: fetched[name](b).wait())

    def forward(b):
        forward_part(k, wins, lambda name: pl.when(b == 0)(waits[name].wait), b)

    loop(forwards, ahead, forward)
    if ahead:
        pl.when(forwards == 0)(all_weights)
    sent_ahead, copies.sent = copies.sent, []
    if back:
        k.small[...] = jnp.zeros_like(k.small)
        if attention:
            k.dbias[...] = jnp.zeros_like(k.dbias)
        wait = lambda b: (lambda name: None) if ahead else (lambda name: pl.when(b == 0)(waits[name].wait))

        def backward(b):
            if mlp:
                backward_mlp(k, wins, wait(b), old, b)
            if attention:
                backward_attention(k, wins, wait(b), old, b, reload)
            if terms:
                for name in dict.fromkeys(name for term in terms for name in term[:2]):
                    if name in k.needed and name not in ("gm", "dmid"):
                        old(name, b)
                for copy in bases:
                    pl.when(b == 0)(copy.wait)
                add_products(k, terms, b, False)

        loop(backwards, back, backward)
        if not ahead:
            pl.when(backwards == 0)(all_weights)
        for copy in bases:
            pl.when(backwards == 0)(copy.wait)
        leaving = [leave(k, name, quartered, copies.at(copies.sem())) for name in targets]
        for copy in leaving:
            copy.wait()
    copies.finish(backwards)
    copies.sent = sent_ahead
    copies.finish(forwards)


SMEM_SPEC = pl.BlockSpec(memory_space=pltpu.SMEM)
HBM_SPEC = pl.BlockSpec(memory_space=pl.ANY)
VMEM_SPEC = pl.BlockSpec(memory_space=pltpu.VMEM)


def shape_of(*shape, dtype=BF):
    return jax.ShapeDtypeStruct(shape, dtype)


def call(kernel, name, ins, outs, scratch, flops, moved):
    names = list(ins) + list(outs) + list(scratch)

    def wrapped(*refs):
        k = Refs()
        for key, ref in zip(names, refs):
            setattr(k, key, ref)
        kernel(k)

    results = pl.pallas_call(
        wrapped,
        grid=(1,),
        out_shape=[shape for shape, _ in outs.values()],
        in_specs=[spec for _, spec in ins.values()],
        out_specs=[spec for _, spec in outs.values()],
        scratch_shapes=list(scratch.values()),
        compiler_params=pltpu.CompilerParams(vmem_limit_bytes=VMEM_LIMIT),
        cost_estimate=pl.CostEstimate(flops=min(flops, 1), bytes_accessed=min(moved, 1), transcendentals=0),
        name=name,
    )(*[array for array, _ in ins.values()])
    return dict(zip(outs, results))


PIECES = ("main", "row", "col", "cor")


def vmem(array):
    return (array, VMEM_SPEC)


def hbm(array):
    return (array, HBM_SPEC)


def run_step(tables, static, landed, counts, groups, old, mlp=True, attention=True, terms=(), base=None, quartered=False):
    sources, held, offsets, shapes = static["weights"]
    rows, wide = tables.rows, shapes[2][0] * shapes[2][2]
    ahead, back = max(counts[:2]), max(counts[2:])
    one = lambda array, index: (array, pl.BlockSpec((TOGETHER,) + array.shape[1:], lambda i: (index, 0, 0)))
    ins = {"sec": (static["sec"], SMEM_SPEC), "put": vmem(static["put"]), "pick": vmem(static["pick"]), "vec": vmem(static["vec"])}
    if landed is not None and (ahead or mlp):
        for name, piece in zip(PIECES, landed):
            ins["p_" + name] = vmem(piece)
    kinds = WEIGHTS if ahead else (("w1", "w2") if mlp else ()) + (("wq", "wo") if attention else ())
    outs, scratch = {}, {}
    for name, shape in zip(WEIGHTS, shapes):
        if name in kinds:
            scratch[name] = pltpu.VMEM(shape, BF)
            if held is None:
                ins[name + "_whole"] = hbm(sources[WEIGHTS.index(name)])
    if held is not None:
        for number, source in enumerate(sources):
            ins[f"pieces_{number}"] = hbm(source)
    widths = {"gp": (wide, BF), "mid": (512, F32), "qkv": (1536, BF), "prob": (1024, BF), "x": (512, BF)}
    for name, (cols, dtype) in widths.items():
        if ahead or (mlp if name in ("gp", "mid") else attention):
            scratch[name] = pltpu.VMEM((2, TOGETHER, rows, cols), dtype)
    local, passed = {}, {}
    if "give" in static and (ahead or attention):
        ins["give"] = vmem(static["give"])
        outs["f_pair"] = (shape_of(2, TOGETHER, static["give"].shape[1], 512), VMEM_SPEC)
        if ahead:
            ins["up"] = vmem(static["up"])
            outs["f_up"] = (shape_of(2, TOGETHER, static["up"].shape[1], 512), VMEM_SPEC)
    if ahead:
        ins["pin"] = one(static["pin"], groups[0])
        ins["bq"], ins["b1"] = vmem(static["bq"]), vmem(static["b1"])
        for name in ("bias", "region"):
            ins[name + "_h"] = hbm(static[name])
            scratch[name] = pltpu.VMEM(static[name].shape, F32)
        for name, size in zip(PIECES, tables.sizes):
            outs["s_" + name] = (shape_of(TOGETHER, size, 512), VMEM_SPEC)
            if "give" not in static:
                outs["h_" + name] = (shape_of(2, TOGETHER, size, 512), VMEM_SPEC)
        for name, (cols, dtype) in widths.items():
            outs[name + "_o"] = (shape_of(TOGETHER, rows, cols, dtype=dtype), HBM_SPEC)
        local |= {"a": (512, BF), "ctx": (512, BF), "n2": (512, BF), "act": (wide, BF), "y": (512, BF)}
    if back:
        if mlp:
            for name, target in zip(PIECES, static["targets"]):
                ins["c_" + name] = one(target, groups[1])
            local |= {"g": (512, BF), "dh": (wide, BF), "gm": (512, BF)}
            (passed if attention else local)["dmid"] = (512, F32)
        else:
            passed |= {"gm": (512, BF), "dmid": (512, F32)}
        needed = (("gp", "mid") if mlp else ("gm", "dmid")) + (("qkv", "prob", "x") if attention else ())
        for name in dict.fromkeys(name for term in terms for name in term[:2]):
            if name in AHEAD:
                needed += (name,)
                passed[name] = (old[name + "_o"].shape[2], BF)
        for name in needed:
            ins["old_" + name] = hbm(old[name + "_o"])
        for name, array in (base or {}).items():
            ins[name + "_b"] = hbm(array)
            scratch[name] = pltpu.VMEM(array.shape, BF)
        outs |= leaving_shapes({name: array.shape for name, array in (base or {}).items()}, quartered)
        if attention:
            local |= {"dqkv": (1536, BF), "dx": (512, BF)}
            scratch["dctx"] = pltpu.VMEM((rows, 512), BF)
            outs["dbias"] = (shape_of(SLOT, 1024, dtype=F32), VMEM_SPEC)
        scratch["dn"] = pltpu.VMEM((rows, 512), F32)
        outs["small"] = (shape_of(8, 2048, dtype=F32), VMEM_SPEC)
    for name, (cols, dtype) in local.items():
        outs[name + "_o"] = (shape_of(TOGETHER, rows, cols, dtype=dtype), HBM_SPEC)
        scratch[name] = pltpu.VMEM((TOGETHER, rows, cols), dtype)
    for name, (cols, dtype) in passed.items():
        scratch[name] = pltpu.VMEM((TOGETHER, rows, cols), dtype)
    scratch["sems"] = pltpu.SemaphoreType.DMA((192,))
    passes = 2 * ahead + 2 * back * (mlp + attention)
    kernel = functools.partial(step_kernel, tables.wins, held, offsets, counts, mlp, attention, terms, quartered)

    def run(k):
        k.landed = landed is not None
        k.needed = needed if back else ()
        kernel(k)

    return call(run, "layer_step", ins, outs, scratch, 2 * passes * rows * TOGETHER * 3145728, 20_000_000)


def add_products(k, terms, place, fresh):
    for left, right, cut_left, name, first, rows in terms:
        l, r, t = getattr(k, left).at[place], getattr(k, right).at[place], getattr(k, name)
        parts = t.shape[0]
        for part in range(parts):
            width = (l if cut_left else r).shape[1] // parts
            cols = slice(part * width, (part + 1) * width)
            value = mm(l[:, cols], r[...], TN) if cut_left else mm(l[...], r[:, cols], TN)
            if not fresh:
                value = value + t[part, first : first + rows, :].astype(F32)
            t[part, first : first + rows, :] = value.astype(BF)


def leave(k, name, quartered, sem):
    t = getattr(k, name)
    if not quartered:
        copy = pltpu.make_async_copy(t, getattr(k, name + "_o"), sem)
        copy.start()
        return copy
    keep, send = getattr(k, name + "_k"), getattr(k, name + "_s")
    high = t.shape[1] // 4
    for core in range(2):

        @pl.when(lax.rem(k.sec[1], 2) == core)
        def _(core=core):
            for quarter in range(4):
                place = keep if quarter % 2 == core else send
                pltpu.make_async_copy(t.at[:, pl.ds(quarter * high, high), :], place.at[:, quarter // 2], sem).start()

    return arrival(t, sem)


def leaving_shapes(shapes, quartered):
    outs = {}
    for name, shape in shapes.items():
        if quartered:
            for kind in "ks":
                outs[f"{name}_{kind}"] = (shape_of(shape[0], 2, shape[1] // 4, shape[2]), HBM_SPEC)
        else:
            outs[name + "_o"] = (shape_of(*shape), HBM_SPEC)
    return outs


def weight_grad_kernel(slots, terms, based, k):
    def run(section):
        sems = iter(range(64))
        waits = {}
        for name in dict.fromkeys(name for term in terms for name in term[:2]):
            places, target, sem = slots[name][section], getattr(k, name), k.sems.at[next(sems)]
            rows = getattr(k, f"{name}_{places[0][0]}").shape[1]
            for at, (step, place) in enumerate(places):
                source = getattr(k, f"{name}_{step}").at[place]
                pltpu.make_async_copy(source, target.at[pl.ds(at * rows, rows), :], sem).start()
            waits[name] = arrival(target.at[pl.ds(0, len(places) * rows), :], sem)
            all_rows = pl.ds(0, len(places) * rows)
        if section == 0:
            for name in based:
                waits[name] = pltpu.make_async_copy(getattr(k, name + "_b"), getattr(k, name), k.sems.at[next(sems)])
                waits[name].start()
        leaving = []
        for number, term in enumerate(terms):
            fresh = term[3] not in based or section == 1
            for needed in (term[0], term[1], term[3]):
                if needed in waits:
                    waits.pop(needed).wait()
            add_products(k, (term,), all_rows, fresh)
            if all(term[3] != later[3] for later in terms[number + 1 :]):
                leaving.append(leave(k, term[3], False, k.sems.at[next(sems)]))
        for copy in leaving:
            copy.wait()

    for section in range(2):
        if slots[terms[0][0]][section]:
            pl.when(k.sec[0] == section)(functools.partial(run, section))


def run_weight_grad(static, steps, counted, terms, shapes, base):
    ins = {"sec": (static["sec"], SMEM_SPEC)}
    scratch, slots = {}, {}
    for name in dict.fromkeys(name for term in terms for name in term[:2]):
        shifts = (0, 1) if name in AHEAD else (2, 1)
        slots[name] = [[(at // TOGETHER + shift, at % TOGETHER) for at in count] for count, shift in zip(counted, shifts)]
        for step in sorted({step for places in slots[name] for step, _ in places}):
            array = steps[step][name + "_o"]
            ins[f"{name}_{step}"] = hbm(array)
        most = max(len(places) for places in slots[name])
        scratch[name] = pltpu.VMEM((most * array.shape[1], array.shape[2]), BF)
    for name, shape in shapes.items():
        scratch[name] = pltpu.VMEM(shape, BF)
        if base:
            ins[name + "_b"] = hbm(base[name])
    scratch["sems"] = pltpu.SemaphoreType.DMA((64,))
    kernel = functools.partial(weight_grad_kernel, slots, terms, tuple(base))
    done = call(kernel, "weight_grad", ins, leaving_shapes(shapes, False), scratch, 0, 0)
    return {name: done[name + "_o"] for name in shapes}


def collect(arrays):
    ins = {f"{name}_{i}": vmem(array) for name, members in arrays.items() for i, array in enumerate(members)}
    outs = {name: (shape_of(len(members), *members[0].shape), VMEM_SPEC) for name, members in arrays.items()}

    def kernel(k):
        for name, members in arrays.items():
            for i in range(len(members)):
                getattr(k, name)[i] = getattr(k, f"{name}_{i}")[...]

    return call(kernel, "collect", ins, outs, {}, 0, 4_000_000)


def run_patches(static, plain, mains, halo, sizes):
    rows = plain[0][0].shape[1]
    batches = sum(sizes)
    ins = {"sec": (static["sec"], SMEM_SPEC), "pick": vmem(static["pick"])}
    for group, (pair, main) in enumerate(zip(plain, mains)):
        ins[f"plain_0_{group}"], ins[f"plain_1_{group}"], ins[f"main_{group}"] = vmem(pair[0]), vmem(pair[1]), vmem(main)
    for name, array in zip(PIECES[1:], halo):
        ins[name] = vmem(array)
    outs = {"patch": (shape_of(2 * batches, rows, 512), VMEM_SPEC)}

    def kernel(k):
        for kind in range(2):
            for group, size in enumerate(sizes):
                for b in range(size):
                    at = kind * batches + sum(sizes[:group]) + b

                    @pl.when(k.sec[0] == 0)
                    def _(at=at, kind=kind, group=group, b=b):
                        k.patch[at] = getattr(k, f"plain_{kind}_{group}")[b]

                    @pl.when(k.sec[0] == 1)
                    def _(at=at, kind=kind, group=group, b=b):
                        parts = [getattr(k, f"main_{group}")[kind, b]] + [getattr(k, name)[group, kind, b] for name in PIECES[1:]]
                        k.patch[at] = mm(k.pick[...], jnp.concatenate(parts, axis=0), TN).astype(BF)

    return call(kernel, "patches", ins, outs, {}, 0, 0)


def run_places(static, steps, pairs, ups, own, take, land, sizes, tokens):
    batches, groups = sum(sizes), len(sizes)
    ins = {"sec": (static["sec"], SMEM_SPEC), "own": vmem(own), "take": vmem(take), "land_0": vmem(land[0]), "land_1": vmem(land[1])}
    for step, done in enumerate(steps):
        for name in ("y_o", "dx_o"):
            if name in done:
                ins[f"{name}_{step}"] = vmem(done[name])
        ins[f"pair_{step}"] = vmem(pairs[step])
        for side, array in enumerate(ups[step]):
            ins[f"up_{side}_{step}"] = vmem(array)
    outs = {"first": (shape_of(batches, tokens, 512), VMEM_SPEC), "second": (shape_of(batches, tokens, 512, dtype=F32), VMEM_SPEC)}

    def kernel(k):
        for kind, name in enumerate(("y_o", "dx_o")):
            for group, size in enumerate(sizes):
                for b in range(size):
                    at = sum(sizes[:group]) + b

                    def put(value, at=at, kind=kind):
                        if kind == 0:
                            k.first[at] = value.astype(BF)
                        else:
                            k.second[at] = value

                    def here(step, kind=kind, name=name, b=b):
                        value = mm(k.own[...], getattr(k, f"{name}_{step}")[b], TN)
                        return value + mm(k.take[...], getattr(k, f"pair_{step}")[kind, b], TN)

                    @pl.when(k.sec[0] == 0)
                    def _(group=group, kind=kind, put=put, here=here):
                        put(here(group + 2 * kind))

                    @pl.when(k.sec[0] == 1)
                    def _(group=group, kind=kind, b=b, put=put, here=here):
                        value = here(group + 1)
                        for side in range(2):
                            value = value + mm(getattr(k, f"land_{side}")[...], getattr(k, f"up_{side}_{group + 1}")[kind, b], TN)
                        put(value)

    return call(kernel, "places", ins, outs, {}, 0, 0)


def table_onehot():
    code = np.full((SLOT, SLOT), -1, np.int32)
    for u in range(TOKENS):
        for t in range(TOKENS):
            code[u, t] = (t // WIN - u // WIN + WIN - 1) * (2 * WIN - 1) + t % WIN - u % WIN + WIN - 1
    side = (2 * WIN - 1) ** 2
    return (jnp.arange(side, dtype=jnp.int32)[:, None] == jnp.asarray(code.reshape(1, -1))).astype(F32)


def region_mask(layout, section):
    row, mp = lax.axis_index(ROW), lax.axis_index(MP)
    window_row = row * WROWS + mp // layout.across
    window_col = (mp % layout.across) * layout.wins + jnp.arange(layout.wins)
    place = jnp.arange(SLOT)
    row_label = jnp.where(window_row == layout.high - 1, 1 + (place // WIN >= WIN - SHIFT).astype(jnp.int32), 0)
    col_label = jnp.where(
        (window_col == WCOLS - 1)[:, None], 1 + (place % WIN >= WIN - SHIFT).astype(jnp.int32)[None], 0
    )
    labels = 3 * row_label[None] + col_label
    differs = labels[:, :, None] != labels[:, None, :]
    term = jnp.where(differs & (section == 1), -100.0, 0.0).astype(F32)
    return jnp.tile(term, (1, 1, GROUP))


def full_patches(layout, mp, tokens):
    wins = layout.wins
    place = jnp.arange(wins * SLOT)
    window, inner = place // SLOT, place % SLOT
    row = (mp // layout.across) * WIN + inner // WIN
    col = ((mp % layout.across) * wins + window) * WIN + inner % WIN
    token = jnp.where(inner < TOKENS, row * (WCOLS * WIN) + col, -1)
    return (token[:, None] == jnp.arange(tokens)[None]).astype(BF)


def whole_patches(layout, mp, tokens_here):
    token = mp * tokens_here + jnp.arange(tokens_here)
    row, col = token // (WCOLS * WIN), token % (WCOLS * WIN)
    window = col // WIN
    owner = (row // WIN) * layout.across + window // layout.wins
    place = owner * layout.wins * SLOT + (window % layout.wins) * SLOT + (row % WIN) * WIN + col % WIN
    return (place[:, None] == jnp.arange(layout.mp_count * layout.wins * SLOT)[None]).astype(BF)


def low_dot(matrix, stack):
    return jnp.einsum("pr,nrd->npd", matrix, stack, preferred_element_type=F32).astype(BF)


def body(
    layer_input,
    out_cotangent,
    norm_one_gain,
    norm_one_bias,
    attend_weight,
    attend_bias,
    position_table,
    output_weight,
    output_bias,
    norm_two_gain,
    norm_two_bias,
    expand_weight,
    expand_bias,
    reduce_weight,
    reduce_bias,
):
    row_count, mp_count = lax.axis_size(ROW), lax.axis_size(MP)
    section, mp = lax.axis_index(SECTION), lax.axis_index(MP)
    layout = Layout(row_count, mp_count)
    tables = Tables(layout.wins)
    put = jnp.asarray(tables.put, BF)
    pick = jnp.asarray(tables.pick, BF)
    batches, tokens_here, width = layer_input.shape
    heads_here = attend_weight.shape[2]
    hidden_here = expand_weight.shape[2]
    row = lax.axis_index(ROW)
    sec = jnp.stack([section, row, mp]).astype(jnp.int32)
    paired = layout.across == 2 and row_count == 4
    first = section == 0

    flat = jnp.concatenate([attend_bias[0].reshape(-1), position_table[0].reshape(-1), expand_bias[0].reshape(-1)])
    wq_rows = attend_weight[0].transpose(1, 2, 0).reshape(heads_here, 3, 32, width)
    if paired:
        quarter = lambda array: take_at(array.reshape(4, -1, width), row)
        shards = (wq_rows.transpose(1, 0, 2, 3), output_weight[0], expand_weight[0], reduce_weight[0])
        quarters = [quarter(array) for array in shards]
        offsets = np.cumsum([0] + [array.shape[0] for array in quarters])[:-1].tolist()
        pieces, first_in, last_in = gather_quarter(jnp.concatenate(quarters))
        _, layer_input, out_cotangent = lax.optimization_barrier((first_in, layer_input, out_cotangent))
        _, flat = lax.optimization_barrier((last_in, flat))
        after = ring(flat, MP)
        flat_all = natural_ring([flat, after, ring(after, MP), ring(flat, MP, -1)], mp)
    else:
        wq_all = lax.all_gather(wq_rows, MP, axis=0).reshape(4, GROUP, 3, 32, width).transpose(0, 2, 1, 3, 4)
        wq_all = wq_all.reshape(4 * GROUP * 96, width)
        wo_all = lax.all_gather(output_weight[0], MP, axis=0).reshape(-1, width)
        w1_all = lax.all_gather(expand_weight[0], MP, axis=0)
        w2_all = lax.all_gather(reduce_weight[0], MP, axis=0).reshape(-1, width)
        flat_all = lax.all_gather(flat, MP, axis=0)
        whole = (wq_all, wo_all, w1_all, w2_all)
        weights = (whole, None, None, tuple(array.shape for array in whole))
    cut_one = heads_here * 64
    cut_two = cut_one + heads_here * position_table.shape[2]
    bias_all = flat_all[:, :cut_one].reshape(4, GROUP, 2, 32)
    table_all = flat_all[:, cut_one:cut_two].reshape(-1, position_table.shape[2])
    b1 = flat_all[:, cut_two:]
    bq = jnp.stack([bias_all[:, :, 0], jnp.zeros_like(bias_all[:, :, 0]), bias_all[:, :, 1]], axis=1).reshape(1, -1)
    onehot = table_onehot()
    bias = jnp.dot(table_all, onehot, precision=highest).reshape(4, GROUP, SLOT, SLOT).transpose(0, 2, 1, 3)
    bias = bias.reshape(4, SLOT, GROUP * SLOT) + jnp.where(jnp.arange(SLOT) < TOKENS, 0.0, -1e30)[None, :, None]
    vec = jnp.concatenate(
        [norm_one_gain, norm_one_bias, output_bias, norm_two_gain, norm_two_bias, reduce_bias, jnp.zeros((2, width), F32)]
    )
    region = region_mask(layout, section)

    taken = jnp.where(first, layer_input, out_cotangent)
    if paired:
        keep, take, send = pair_tables(layout.wins)
        side = mp % 2
        keep = lax.dynamic_index_in_dim(jnp.asarray(keep, BF), side, 0, keepdims=False)
        take = lax.dynamic_index_in_dim(jnp.asarray(take, BF), side, 0, keepdims=False)
        send = jnp.asarray(send, BF)
        arrived = swap(low_dot(send, taken), MP, 1)
        pin = low_dot(jnp.concatenate([keep, take], axis=1), jnp.concatenate([taken, arrived], axis=1))
        own, give, take, up, land = (jnp.asarray(table, BF) for table in placing_tables(layout.wins))
        own, give, take = (take_at(take_at(table, section), side) for table in (own, give, take))
        land = jnp.where((section == 1) & (side == 0), land, 0)
    else:
        everything = lax.all_gather(taken, MP, axis=1, tiled=True)
        pin = low_dot(full_patches(layout, mp, everything.shape[1]), everything)
    groups = -(-batches // TOGETHER)
    sizes = [min(TOGETHER, batches - TOGETHER * group) for group in range(groups)]
    pin = jnp.pad(pin, ((0, TOGETHER * groups - batches), (0, 0), (0, 0)))
    cuts = np.cumsum(tables.sizes)[:-1].tolist()
    targets = halo_inside(layout, jnp.split(low_dot(pick, pin), cuts, axis=1), False)
    if paired:
        arrays = [array for array, _ in pieces]
        arrays[0], pin, targets, bias, region, bq, b1 = lax.optimization_barrier((arrays[0], pin, targets, bias, region, bq, b1))
        held = tuple(places for _, places in pieces)
        held += tuple(tuple((bits + 1, back) for bits, back in places) for places in held)
        weights = (
            arrays + [swap(array, ROW, 1) for array in arrays],
            held,
            offsets,
            ((4 * GROUP * 96, width), (4 * GROUP * 32, width), (mp_count, width, hidden_here), (mp_count * hidden_here, width)),
        )

    static = dict(
        sec=sec, weights=weights, pin=pin, targets=targets, put=put, pick=pick, vec=vec, bq=bq, b1=b1, bias=bias, region=region
    )
    if paired:
        static |= dict(give=give, up=up)
    size_of = lambda group: sizes[group] if 0 <= group < groups else 0
    landed = None
    steps, pairs, ups = [], [], []
    mlp_terms = (("act", "g", True, "d2", 0, hidden_here), ("n2", "dh", False, "d1", 0, width))
    heads_terms = (("dqkv", "a", True, "da", 0, GROUP * 96), ("ctx", "gm", True, "da", GROUP * 96, GROUP * 32))
    terms = mlp_terms + heads_terms
    shapes = {"d2": (mp_count, hidden_here, width), "d1": (mp_count, width, hidden_here), "da": (4, GROUP * 128, width)}
    early, ready = TOGETHER * (groups - 1), max(TOGETHER * (groups - 2), 0)
    grads_base = {}
    for step in range(groups + 1):
        counts = (size_of(step), size_of(step - 1), size_of(step - 2), size_of(step - 1))
        which = (min(step, groups - 1), max(step - 1, 0))
        done = run_step(tables, static, landed, counts, which, steps[max(step - 2, 0)] if step else None)
        steps.append(done)
        sends = [done["s_" + name] for name in PIECES]
        pair, up_piece = done.get("f_pair"), done.get("f_up")
        if step == groups:
            sends = [piece[: sizes[-1]] for piece in sends]
        if paired:
            sends, pairs, ups = lax.optimization_barrier((sends, pairs, ups))
        if step == groups - 1 and ready:
            grads_base = run_weight_grad(static, steps, (range(ready), ()), terms, shapes, {})
            sends, grads_base = lax.optimization_barrier((sends, grads_base))
        landed = halo_swap(layout, sends, step == groups)
        if paired:
            if step == groups:
                break
            landed, pair, up_piece = lax.optimization_barrier((landed, pair, up_piece))
            pairs = pairs + [swap(pair, MP, 1)]
            ups = ups + [[lax.ppermute(up_piece, AXES, route) for route in layout.up_routes()] if step else []]

    if not paired:
        halo = collect({name: [done["h_" + name] for done in steps[1:]] for name in PIECES[1:]})
        halo = [halo[name] for name in PIECES[1:]]
        flat_halo = halo_inside(layout, [None] + [array.reshape((-1,) + array.shape[3:]) for array in halo], True)[1:]
        halo = [flat.reshape(array.shape) for flat, array in zip(flat_halo, halo)]

    grads_base = run_weight_grad(static, steps, (range(ready, early), range(batches)), terms, shapes, grads_base)
    landed, grads_base = lax.optimization_barrier((landed, grads_base))
    after = sec
    if paired:
        grads_base, pair, up_piece = lax.optimization_barrier((grads_base, pair, up_piece[:, : sizes[-1]]))
        pairs = pairs + [swap(pair, MP, 1)]
        ups = ups + [[lax.ppermute(up_piece, AXES, route) for route in layout.up_routes()]]
    mlp_base = {name: grads_base[name] for name in ("d2", "d1")}
    heads_base = {"da": grads_base["da"]}

    counts = (0, 0, sizes[-1], 0)
    which = (groups - 1, groups - 1)
    old = steps[-2]
    last = run_step(
        tables, static, landed, counts, which, old, attention=False, terms=mlp_terms, base=mlp_base, quartered=paired
    )
    if paired:
        last, pairs, ups = lax.optimization_barrier((last, pairs, ups))
        d2, d1 = (last[name + "_k"] + swap(last[name + "_s"], ROW, 1) for name in ("d2", "d1"))
        after, d2, d1 = lax.optimization_barrier((sec, d2, d1))
    heads = run_step(
        tables, dict(static, sec=after), None, counts, which, {**old, **last}, mlp=False, terms=heads_terms, base=heads_base, quartered=paired
    )
    smalls = [done["small"] for done in steps[1:] + [last, heads]]
    biases = [done["dbias"] for done in steps[1:] + [heads]]
    steps.append({**last, **heads})
    def summed(smalls, biases):
        small = sum(smalls)[:4]
        table = sum(biases).reshape(SLOT, 4 * GROUP, SLOT).transpose(1, 0, 2).reshape(4 * GROUP, -1)
        table = jnp.dot(table, onehot.T, precision=highest)
        flat = jnp.pad(table.reshape(-1), (0, -table.size % 2048)).reshape(-1, 2048)
        return jnp.concatenate([small, flat])

    if paired:
        high, core = row // 2, row % 2
        gate = lax.optimization_barrier
        term = lambda part, step: take_at(part, (mp - 2 - step) % mp_count)

        def joined(pair, crossed):
            whole = jnp.stack([jnp.where(core == 0, pair, crossed), jnp.where(core == 0, crossed, pair)], axis=1)
            return whole.astype(F32).reshape(-1, width)

        def around(array, axis):
            return [swap(array, axis, bits) for bits in (1, 2, 3)]

        def in_pairs(array, came):
            return (array + came[0]) + (came[1] + came[2])

        def ordered(mine, other):
            return jnp.stack([jnp.where(high == 0, mine, other), jnp.where(high == 0, other, mine)])

        d2_came, d1_came = ring(take_at(d2, (mp - 1) % mp_count), MP), swap(take_at(d1, 1 - high, 1), ROW, 2)
        d2_came, d1_came, sending = gate((d2_came, d1_came, heads["da_s"]))
        da_came, pair_came = swap(sending, ROW, 1), lax.ppermute(heads["f_pair"], AXES, layout.pair_route(0))
        d2_total, d1 = d2_came + term(d2, 0), take_at(d1, high, 1) + d1_came
        d2_came, d1_came = ring(d2_total, MP), ring(take_at(d1, (mp - 1) % mp_count), MP)
        da = heads["da_k"] + da_came
        mine, other = take_at(da, high, 1), take_at(da, 1 - high, 1)
        da_came = swap(other, ROW, 2)
        pair_came, _ = gate((pair_came, other))
        placed = run_places(static, steps, pairs + [pair_came], ups + [[]], own, take, land, sizes, tokens_here)
        da_came, first_out, second_out = gate((da_came, placed["first"], placed["second"]))
        da = mine + da_came
        sending = take_at(da, (mp - 1) % mp_count)
        da_came = ring(sending, MP)
        d2_came, d1_came, smalls, biases, _ = gate((d2_came, d1_came, smalls, biases, sending))
        d2_total, d1_total = d2_came + term(d2, 1), d1_came + term(d1, 0)
        d2_came, d1_came = ring(d2_total, MP), ring(d1_total, MP)
        sums = summed(smalls, biases)
        sending = da_came + term(da, 0)
        da_came = ring(sending, MP)
        d2_came, d1_came, sums, _ = gate((d2_came, d1_came, sums, sending))
        d2, d1_total = d2_came + term(d2, 2), d1_came + term(d1, 1)
        d2_came, d1_came, sums_came = swap(d2, ROW, 2), ring(d1_total, MP), around(sums, ROW)
        sending = da_came + term(da, 1)
        da_came = ring(sending, MP)
        d2_came, d1_came, sums_came, _ = gate((d2_came, d1_came, sums_came, sending))
        d2, d1, sums = d2 + d2_came, d1_came + term(d1, 2), in_pairs(sums, sums_came)
        d2_came, d1_came, sums_came = swap(d2, ROW, 1), swap(d1, ROW, 2), around(sums, MP)
        da = da_came + term(da, 2)
        da_came = swap(da, ROW, 2)
        d2_came, d1_came, _ = gate((d2_came, d1_came, da))
        d2, d1 = joined(d2, d2_came), ordered(d1, d1_came)
        d1_came = swap(d1, ROW, 1)
        da = ordered(da, da_came)
        da_came = swap(da, ROW, 1)
        d1_came, sums_came, _ = gate((d1_came, sums_came, da))
        d1, sums = joined(d1, d1_came), in_pairs(sums, sums_came)
        da = joined(da, da_came)
        dq, do = da[: GROUP * 96].reshape(3, GROUP, 32, width), da[GROUP * 96 :]
        dq = dq.transpose(3, 1, 0, 2).reshape(attend_weight.shape[1:])
    else:

        def shared(parts):
            part = lax.psum_scatter(parts, MP, scatter_dimension=0, tiled=False)
            return lax.psum(part, ROW).astype(F32)

        da = heads["da_o"]
        dq = da[:, : GROUP * 96].reshape(4, 3, GROUP, 32, width).transpose(0, 2, 1, 3, 4).reshape(mp_count, heads_here * 96, width)
        d2, d1, do = shared(last["d2_o"]), shared(last["d1_o"]), shared(da[:, GROUP * 96 :].reshape(mp_count, heads_here * 32, width))
        dq = shared(dq).T.reshape(attend_weight.shape[1:])
        sums = lax.psum(summed(smalls, biases), (ROW, MP))
    small = sums[:4]
    table = sums[4:].reshape(-1)[: 4 * GROUP * onehot.shape[0]].reshape(4 * GROUP, -1)
    shift = small[3, :1536].reshape(4, 3, GROUP, 32)
    shift = jnp.concatenate([shift[:, 0], shift[:, 2]], axis=-1).reshape(4 * GROUP, 64)
    mine = lambda array: lax.dynamic_index_in_dim(array.reshape((mp_count, -1) + array.shape[1:]), mp, 0, keepdims=False)

    if not paired:
        plain = [(steps[group]["y_o"], steps[group + 2]["dx_o"]) for group in range(groups)]
        mains = [steps[group + 1]["h_main"] for group in range(groups)]
        made = run_patches(static, plain, mains, halo, sizes)
        everything = lax.all_gather(made["patch"], MP, axis=1, tiled=True)
        placed = low_dot(whole_patches(layout, mp, tokens_here), everything)
        first_out, second_out = placed[:batches], placed[batches:].astype(F32)

    return (
        first_out[None],
        second_out[None],
        small[1, 1024:1536][None],
        small[1, 1536:2048][None],
        dq[None],
        mine(shift)[None],
        mine(table)[None],
        do.reshape(output_weight.shape),
        small[1, 512:1024][None],
        small[2, 0:512][None],
        small[2, 512:1024][None],
        d1[None],
        mine(small[0])[None],
        d2[None],
        small[1, 0:512][None],
    )


def solution(mesh):
    return jax.shard_map(
        body,
        mesh=mesh,
        in_specs=(
            P(None, (ROW, MP), None),
            P(None, (ROW, MP), None),
            P(SECTION, None),
            P(SECTION, None),
            P(SECTION, None, MP, None),
            P(SECTION, MP, None),
            P(SECTION, MP, None),
            P(SECTION, MP, None, None),
            P(SECTION, None),
            P(SECTION, None),
            P(SECTION, None),
            P(SECTION, None, MP),
            P(SECTION, MP),
            P(SECTION, MP, None),
            P(SECTION, None),
        ),
        out_specs=(
            P(SECTION, None, (ROW, MP), None),
            P(SECTION, None, (ROW, MP), None),
            P(SECTION, None),
            P(SECTION, None),
            P(SECTION, None, MP, None),
            P(SECTION, MP, None),
            P(SECTION, MP, None),
            P(SECTION, MP, None, None),
            P(SECTION, None),
            P(SECTION, None),
            P(SECTION, None),
            P(SECTION, None, MP),
            P(SECTION, MP),
            P(SECTION, MP, None),
            P(SECTION, None),
        ),
        check_vma=False,
    )
```

```python
import functools

import jax
import jax.numpy as jnp
import numpy as np
from jax import lax
from jax.experimental import pallas as pl
from jax.experimental.pallas import tpu as pltpu
from jax.sharding import PartitionSpec as P

WIN = 7
SHIFT = 3
WCOLS = 8
WROWS = 2
TOKENS = WIN * WIN
SLOT = 64
GROUP = 4
SECTION, ROW, MP = AXES = ("section", "row", "mp")
EPS = 1e-05
BF = jnp.bfloat16
F32 = jnp.float32
NN = (((1,), (0,)), ((), ()))
NT = (((1,), (1,)), ((), ()))
TN = (((0,), (0,)), ((), ()))
VMEM_LIMIT = 56 * 1024 * 1024
highest = lax.Precision.HIGHEST


def mm(left, right, dims=NN):
    return lax.dot_general(left, right, dims, preferred_element_type=F32)


def up16(count):
    return -(-count // 16) * 16


def patch_place(row, col):
    return (col // WIN) * SLOT + row * WIN + col % WIN


class Tables:
    def __init__(self, wins):
        self.wins = wins
        self.rows = wins * SLOT
        cols = wins * WIN
        wide = range(SHIFT, cols)
        thin = range(SHIFT)
        low, high = range(SHIFT, WIN), range(SHIFT)
        pieces = [(low, wide), (high, wide), (low, thin), (high, thin)]
        self.sizes = [up16(len(a) * len(b)) for a, b in pieces]
        self.total = sum(self.sizes)
        pick = np.zeros((self.total, self.rows), np.float32)
        put = np.zeros((self.rows, self.total), np.float32)
        at = 0
        for (rows, columns), size in zip(pieces, self.sizes):
            spot = at
            for row in rows:
                for col in columns:
                    pick[spot, patch_place(row, col)] = 1
                    put[patch_place((row - SHIFT) % WIN, (col - SHIFT) % cols), spot] = 1
                    spot += 1
            at += size
        self.pick, self.put = pick, put


def pair_tables(wins):
    cols = wins * WIN
    tokens = WIN * cols
    keep = np.zeros((2, wins * SLOT, tokens), np.float32)
    take = np.zeros((2, wins * SLOT, up16(SHIFT * cols)), np.float32)
    send = np.zeros((up16(SHIFT * cols), tokens), np.float32)
    for seg in range(SHIFT):
        for col in range(cols):
            send[seg * cols + col, (2 * seg + 1) * cols + col] = 1
    for side in range(2):
        for row in range(WIN):
            for col in range(cols):
                place = patch_place(row, col)
                own = row <= SHIFT if side == 0 else row >= SHIFT
                if own:
                    seg = row if side == 0 else row - SHIFT
                    keep[side, place, 2 * seg * cols + col] = 1
                else:
                    seg = row - SHIFT - 1 if side == 0 else row
                    take[side, place, seg * cols + col] = 1
    return keep, take, send


def placing_tables(wins):
    cols, tokens, most = wins * WIN, WIN * wins * WIN, up16(SHIFT * (wins * WIN + 1))
    own = np.zeros((2, 2, wins * SLOT, tokens), np.float32)
    give = np.zeros((2, 2, wins * SLOT, most), np.float32)
    take = np.zeros((2, 2, most, tokens), np.float32)
    up = np.zeros((wins * SLOT, most), np.float32)
    land = np.zeros((2, most, tokens), np.float32)
    half = SHIFT * 2 * cols + cols

    def holder(row, col):
        token = row * 2 * cols + col
        return (0, token) if token < half else (1, token - half)

    for section in range(2):
        for side in range(2):
            given, raised = 0, 0
            for row in range(WIN):
                for col in range(cols):
                    place = patch_place(row, col)
                    real_row = row + SHIFT * section
                    real_col = (side * cols + col + SHIFT * section) % (2 * cols)
                    if real_row >= WIN:
                        up[place, raised] = 1
                        land[side, raised, holder(real_row - WIN, real_col)[1]] = 1
                        raised += 1
                        continue
                    keeper, token = holder(real_row, real_col)
                    if keeper == side:
                        own[section, side, place, token] = 1
                    else:
                        give[section, side, place, given] = 1
                        take[section, keeper, given, token] = 1
                        given += 1
    return own, give, take, up, land


class Layout:
    def __init__(self, row_count, mp_count):
        self.row_count, self.mp_count = row_count, mp_count
        self.across = mp_count // WROWS
        self.wins = WCOLS // self.across
        self.high = row_count * WROWS

    def device(self, section, window_row, place):
        window_row, place = window_row % self.high, place % self.across
        row = window_row // WROWS
        return (section * self.row_count + row) * self.mp_count + (window_row % WROWS) * self.across + place

    def route(self, source, target, up, back):
        return [
            (self.device(source, window_row, place), self.device(target, window_row - up, place - back))
            for window_row in range(self.high)
            for place in range(self.across)
        ]


    def pair_route(self, section):
        return [
            (self.device(section, window_row, side), self.device(section, window_row, 1 - side))
            for window_row in range(self.high)
            for side in range(2)
        ]

    def up_routes(self):
        return [
            [(self.device(1, window_row, side), self.device(1, window_row + 1, 0)) for window_row in range(self.high)] for side in range(2)
        ]


HALO = ((0, 0), (1, 0), (0, 1), (1, 1))


def halo_swap(layout, parts, back_only):
    result = []
    for part, by in zip(parts, HALO):
        there = layout.route(0, 1, *by)
        result.append(lax.ppermute(part, AXES, [(b, a) for a, b in there] + ([] if back_only else there)))
    return result


def halo_inside(layout, parts, back):
    result = [parts[0]]
    for part, by in zip(parts[1:], HALO[1:]):
        there = layout.route(1, 1, *by)
        result.append(lax.ppermute(part, AXES, [(b, a) for a, b in there] if back else there))
    return result


def ring(shard, axis, by=1):
    count = lax.axis_size(axis)
    return lax.ppermute(shard, axis, [(i, (i + by) % count) for i in range(count)])


def swap(shard, axis, bit):
    return lax.ppermute(shard, axis, [(i, i ^ bit) for i in range(lax.axis_size(axis))])


def natural_ring(shards, mp):
    stacked, count = jnp.stack(shards), len(shards)
    return jnp.stack([lax.dynamic_index_in_dim(stacked, (mp - j) % count, 0, keepdims=False) for j in range(count)])


def take_at(array, index, axis=0):
    return lax.dynamic_index_in_dim(array, index, axis, keepdims=False)


def head_masks(dtype):
    lane = lax.broadcasted_iota(jnp.int32, (1, GROUP * 32), 1)
    return [jnp.where(lane // 32 == h, 1.0, 0.0).astype(dtype) for h in range(GROUP)]


def spread_heads(block, masks):
    return jnp.concatenate([block * mask for mask in masks], axis=0)


def fold_heads(tall, masks):
    total = tall[:SLOT] * masks[0]
    for h in range(1, GROUP):
        total = total + tall[h * SLOT : (h + 1) * SLOT] * masks[h]
    return total


def centre(values):
    middle = jnp.mean(values, axis=-1, keepdims=True)
    centred = values - middle
    scale = lax.rsqrt(jnp.mean(centred * centred, axis=-1, keepdims=True) + EPS)
    return centred * scale, scale


KEPT = ("gp", "mid", "qkv", "prob", "x")
WEIGHTS = ("wq", "wo", "w1", "w2")
AHEAD = ("act", "n2", "a", "ctx")
TOGETHER = 2


class Refs:
    pass


class Copies:
    def __init__(self, sems):
        self.sems, self.used, self.sent = sems, 0, []

    def sem(self, count=1):
        self.used += count
        return self.used - count

    def at(self, index):
        return self.sems.at[index]

    def ship(self, b, make, wanted):
        first = self.sem(TOGETHER)
        maker = lambda b: make(b, self.at(first + b))
        pl.when(wanted())(lambda: maker(b).start())
        self.sent.append((maker, wanted))

    def finish(self, count):
        for b in range(TOGETHER):

            @pl.when(b < count)
            def _(b=b):
                for maker, wanted in self.sent:
                    pl.when(wanted())(lambda maker=maker: maker(b).wait())

        self.sent = []


def arrival(target, sem):
    return pltpu.make_async_copy(target, target, sem)


def load_weights(k, kinds, held, offsets, wanted):
    waits = {}
    for name in kinds:
        target, sem = getattr(k, name), k.copies.at(k.copies.sem())
        waits[name] = arrival(target, sem)

        def start(name=name, target=target, sem=sem):
            if held is None:
                pltpu.make_async_copy(getattr(k, name + "_whole"), target, sem).start()
                return
            flat, shards, offset = len(target.shape) == 2, 4, offsets[WEIGHTS.index(name)]
            high = target.shape[-2] // (4 * shards if flat else 4)
            for number, places in enumerate(held):
                for piece, (bits, back) in enumerate(places):
                    quarter = k.sec[1] ^ bits
                    shard = lax.rem(k.sec[2] + (shards - back), shards)
                    at = quarter * high
                    if flat:
                        at = at + shard * (4 * high)
                    rows = pl.ds(pl.multiple_of(at, high), high)
                    place = target.at[rows, :] if flat else target.at[shard, rows, :]
                    source = getattr(k, f"pieces_{number}").at[piece, pl.ds(offset, high), :]
                    pltpu.make_async_copy(source, place, sem).start()

        pl.when(wanted)(start)
    return waits


def window_rows(w):
    return slice(w * SLOT, (w + 1) * SLOT)


def wanted(k, name):
    return k.sec[0] == 0 if name in KEPT else k.sec[0] >= 0


def result(k, name, cols=None):
    def make(b, sem):
        src = getattr(k, name)
        src = src.at[0, b] if name in KEPT else src.at[b]
        dst = getattr(k, name + "_o").at[b]
        if cols is not None:
            src, dst = src.at[:, cols], dst.at[:, cols]
        return pltpu.make_async_copy(src, dst, sem)

    return make


def forward_part(k, wins, wait, b):
    x, qkv, prob, mid, gp = (getattr(k, name).at[0, b] for name in ("x", "qkv", "prob", "mid", "gp"))
    a, ctx, n2, act, y = (getattr(k, name).at[b] for name in ("a", "ctx", "n2", "act", "y"))
    ship = lambda name, cols=None: k.copies.ship(b, result(k, name, cols), lambda: wanted(k, name))

    @pl.when(k.sec[0] == 0)
    def _():
        x[...] = k.pin[b]

    if k.landed:

        @pl.when(k.sec[0] == 1)
        def _():
            joined = jnp.concatenate([k.p_main[b], k.p_row[b], k.p_col[b], k.p_cor[b]], axis=0)
            x[...] = mm(k.put[...], joined).astype(BF)

    for w in range(wins):
        rows = window_rows(w)
        hat, _ = centre(x[rows, :].astype(F32))
        a[rows, :] = (hat * k.vec[0:1, :] + k.vec[1:2, :]).astype(BF)
    ship("x")
    ship("a")
    wait("wq")
    lane = lax.broadcasted_iota(jnp.int32, (1, 512), 1)
    for part in range(3):
        cols = slice(part * 512, (part + 1) * 512)
        factor = jnp.where(lax.rem(lane + part * 512, 384) < GROUP * 32, 32 ** (-0.5), 1.0)
        pr = mm(a[...], k.wq[cols, :], NT) + k.bq[0:1, cols]
        qkv[:, cols] = (pr * factor).astype(BF)
    ship("qkv")
    wait("bias")
    wait("region")
    masks, masks_f = head_masks(BF), head_masks(F32)
    for w in range(wins):
        rows = window_rows(w)
        for g in range(4):
            query = qkv[rows, g * 384 : g * 384 + 128]
            key = qkv[rows, g * 384 + 128 : g * 384 + 256]
            value = qkv[rows, g * 384 + 256 : g * 384 + 384]
            scores = mm(key, spread_heads(query, masks), NT) + k.bias[g] + k.region[w]
            top = jnp.max(scores, axis=0, keepdims=True)
            e = jnp.exp(scores - top)
            low = (e * (1.0 / jnp.sum(e, axis=0, keepdims=True))).astype(BF)
            prob[rows, g * 256 : (g + 1) * 256] = low
            ctx[rows, g * 128 : (g + 1) * 128] = fold_heads(mm(low, value, TN), masks_f).astype(BF)
    ship("prob")
    ship("ctx")
    wait("wo")
    mid[...] = x[...].astype(F32) + (mm(ctx[...], k.wo[...]) + k.vec[2:3, :])
    ship("mid")
    for w in range(wins):
        rows = window_rows(w)
        hat, _ = centre(mid[rows, :])
        n2[rows, :] = (hat * k.vec[3:4, :] + k.vec[4:5, :]).astype(BF)
    ship("n2")
    wait("w1")
    wait("w2")
    parts, _, width = k.w1.shape
    for j in range(parts):
        cols = slice(j * width, (j + 1) * width)
        hidden = mm(n2[...], k.w1[j]) + k.b1[j : j + 1, :]
        phi = 0.5 + 0.5 * lax.erf(hidden * 0.7071067811865476)
        low = (hidden * phi).astype(BF)
        act[:, cols] = low
        gp[:, cols] = (phi + hidden * (jnp.exp(hidden * hidden * -0.5) * 0.3989422804014327)).astype(BF)
        ship("act", cols)
        ship("gp", cols)
    y[...] = (mid[...] + k.vec[5:6, :] + mm(act[...], k.w2[...])).astype(BF)
    ship("y")

    put_partner(k, 0, b, y)

    @pl.when(k.sec[0] == 0)
    def _():
        put_pieces(k, "s_", b, mm(k.pick[...], y[...]).astype(BF))

    @pl.when(k.sec[0] == 1)
    def _():
        put_neighbours(k, 0, b, y)


def put_pieces(k, first, b, joined):
    at = 0
    for name in PIECES:
        ref = getattr(k, first + name)
        ref[b] = joined[at : at + ref.shape[1]]
        at += ref.shape[1]


def put_partner(k, kind, b, result):
    if hasattr(k, "f_pair"):
        k.f_pair[kind % k.f_pair.shape[0], b] = mm(k.give[...], result[...], TN).astype(BF)


def put_neighbours(k, kind, b, result):
    if hasattr(k, "f_up"):
        k.f_up[kind, b] = mm(k.up[...], result[...], TN).astype(BF)
        return
    joined = mm(k.put[...], result[...], TN).astype(BF)
    at = 0
    for name in PIECES:
        ref = getattr(k, "h_" + name)
        ref[kind, b] = joined[at : at + ref.shape[2]]
        at += ref.shape[2]


def norm_back(grad, hat, scale, gain):
    inner = grad * gain
    return scale * (inner - jnp.mean(inner, axis=-1, keepdims=True) - hat * jnp.mean(inner * hat, axis=-1, keepdims=True))


def column_sum(values):
    return jnp.sum(values, axis=0, keepdims=True)


def backward_mlp(k, wins, wait, old, b):
    slot = 1 - k.sec[0]
    gp, mid = k.gp.at[slot, b], k.mid.at[slot, b]
    out_grad, dhs, gm, dmid = k.g.at[b], k.dh.at[b], k.gm.at[b], k.dmid.at[b]
    ship = lambda name, cols=None: k.copies.ship(b, result(k, name, cols), lambda: wanted(k, name))

    @pl.when(k.sec[0] == 0)
    def _():
        joined = jnp.concatenate([k.p_main[b], k.p_row[b], k.p_col[b], k.p_cor[b]], axis=0)
        out_grad[...] = mm(k.pick[...], joined, TN).astype(BF)

    @pl.when(k.sec[0] == 1)
    def _():
        joined = jnp.concatenate([k.c_main[b], k.c_row[b], k.c_col[b], k.c_cor[b]], axis=0)
        out_grad[...] = mm(k.put[...], joined).astype(BF)

    ship("g")
    parts, _, width = k.w1.shape
    wait("w2")
    wait("w1")
    old("gp", b)
    total = None
    for j in range(parts):
        cols = slice(j * width, (j + 1) * width)
        dh = (mm(out_grad[...], k.w2[cols, :], NT) * gp[:, cols].astype(F32)).astype(BF)
        dhs[:, cols] = dh
        k.small[0:1, cols] += column_sum(dh.astype(F32))
        ship("dh", cols)
        part = mm(dh, k.w1[j], NT)
        total = part if total is None else total + part
    k.dn[...] = total
    old("mid", b)
    sums = [0.0] * 4
    for w in range(wins):
        rows = window_rows(w)
        grad = k.dn[rows, :]
        out = out_grad[rows, :].astype(F32)
        hat, scale = centre(mid[rows, :])
        whole = out + norm_back(grad, hat, scale, k.vec[3:4, :])
        dmid[rows, :] = whole
        low = whole.astype(BF)
        gm[rows, :] = low
        for i, term in enumerate((out, low.astype(F32), grad * hat, grad)):
            sums[i] = sums[i] + column_sum(term)
    ship("gm")
    if hasattr(k, "dmid_o"):
        ship("dmid")
    k.small[1:2, 0:512] += sums[0]
    k.small[1:2, 512:1024] += sums[1]
    k.small[2:3, 0:512] += sums[2]
    k.small[2:3, 512:1024] += sums[3]


def backward_attention(k, wins, wait, old, b, reload):
    slot = 1 - k.sec[0]
    qkv, prob, x = k.qkv.at[slot, b], k.prob.at[slot, b], k.x.at[slot, b]
    gm, dmid, dqkv, dx = k.gm.at[b], k.dmid.at[b], k.dqkv.at[b], k.dx.at[b]
    ship = lambda name, cols=None: k.copies.ship(b, result(k, name, cols), lambda: wanted(k, name))
    wait("wo")
    if reload:
        old("gm", b)
    k.dctx[...] = mm(gm[...], k.wo[...], NT).astype(BF)
    old("qkv", b)
    old("prob", b)
    masks, masks_f = head_masks(BF), head_masks(F32)
    for w in range(wins):
        rows = window_rows(w)
        for g in range(4):
            at = g * 384
            query = qkv[rows, at : at + 128]
            key = qkv[rows, at + 128 : at + 256]
            value = qkv[rows, at + 256 : at + 384]
            do = spread_heads(k.dctx[rows, g * 128 : (g + 1) * 128], masks)
            low = prob[rows, g * 256 : (g + 1) * 256]
            p = low.astype(F32)
            dp = mm(value, do, NT)
            ds = (p * (dp - column_sum(p * dp))).astype(BF)
            k.dbias[:, g * 256 : (g + 1) * 256] += ds.astype(F32)
            dv = mm(low, do).astype(BF)
            dk = mm(ds, spread_heads(query, masks)).astype(BF)
            dq = (fold_heads(mm(ds, key, TN), masks_f) * 32 ** (-0.5)).astype(BF)
            dqkv[rows, at : at + 128] = dq
            dqkv[rows, at + 128 : at + 256] = dk
            dqkv[rows, at + 256 : at + 384] = dv
    ship("dqkv")
    wait("wq")
    k.small[3:4, 0:1536] += column_sum(dqkv[...].astype(F32))
    k.dn[...] = mm(dqkv[...], k.wq[...])
    old("x", b)
    if reload:
        old("dmid", b)
    sums = [0.0] * 2
    for w in range(wins):
        rows = window_rows(w)
        grad = k.dn[rows, :]
        hat, scale = centre(x[rows, :].astype(F32))
        dx[rows, :] = (dmid[rows, :] + norm_back(grad, hat, scale, k.vec[0:1, :])).astype(BF)
        sums[0] = sums[0] + column_sum(grad * hat)
        sums[1] = sums[1] + column_sum(grad)
    ship("dx")
    k.small[1:2, 1024:1536] += sums[0]
    k.small[1:2, 1536:2048] += sums[1]
    put_partner(k, 1, b, dx)
    if hasattr(k, "s_main"):

        @pl.when(k.sec[0] == 1)
        def _():
            put_pieces(k, "s_", b, mm(k.put[...], dx[...], TN).astype(BF))
            put_neighbours(k, 1, b, dx)


def loop(count, most, run):
    def once(b, carry):
        run(b)
        return carry

    if most:
        lax.fori_loop(0, count, once, 0)


def step_kernel(wins, held, offsets, counts, mlp, attention, terms, quartered, k):
    k.copies = copies = Copies(k.sems)
    ahead, back = max(counts[:2]), max(counts[2:])
    number = lambda pair: jnp.where(k.sec[0] == 0, pair[0], pair[1])
    forwards, backwards = number(counts[:2]), number(counts[2:])
    kinds = WEIGHTS if ahead else (("w2", "w1") if mlp else ()) + (("wo", "wq") if attention else ())
    loaded = backwards >= (0 if ahead else 1)
    waits = load_weights(k, kinds[:1], held, offsets, loaded)
    if ahead:
        for name in ("bias", "region"):
            copy = pltpu.make_async_copy(getattr(k, name + "_h"), getattr(k, name), copies.at(copies.sem()))
            copy.start()
            waits[name] = copy
    fetched = {}
    if back:
        reload = attention and not mlp
        for name in k.needed:
            first = copies.sem(TOGETHER)

            def fetch(b, name=name, first=first):
                target = getattr(k, name)
                target = target.at[1, b] if name in KEPT else target.at[b]
                return pltpu.make_async_copy(getattr(k, "old_" + name).at[b], target, copies.at(first + b))

            fetched[name] = fetch
            for b in range(back):
                pl.when((k.sec[0] == 0) & (b < backwards))(lambda b=b, fetch=fetch: fetch(b).start())
    waits |= load_weights(k, kinds[1:], held, offsets, loaded)
    targets = tuple(dict.fromkeys(term[3] for term in terms))
    bases = [pltpu.make_async_copy(getattr(k, name + "_b"), getattr(k, name), copies.at(copies.sem())) for name in targets]
    for copy in bases:
        copy.start()

    def all_weights():
        for copy in waits.values():
            copy.wait()

    def old(name, b):
        if name in fetched:
            pl.when(k.sec[0] == 0)(lambda: fetched[name](b).wait())

    def forward(b):
        forward_part(k, wins, lambda name: pl.when(b == 0)(waits[name].wait), b)

    loop(forwards, ahead, forward)
    if ahead:
        pl.when(forwards == 0)(all_weights)
    sent_ahead, copies.sent = copies.sent, []
    if back:
        k.small[...] = jnp.zeros_like(k.small)
        if attention:
            k.dbias[...] = jnp.zeros_like(k.dbias)
        wait = lambda b: (lambda name: None) if ahead else (lambda name: pl.when(b == 0)(waits[name].wait))

        def backward(b):
            if mlp:
                backward_mlp(k, wins, wait(b), old, b)
            if attention:
                backward_attention(k, wins, wait(b), old, b, reload)
            if terms:
                for name in dict.fromkeys(name for term in terms for name in term[:2]):
                    if name in k.needed and name not in ("gm", "dmid"):
                        old(name, b)
                for copy in bases:
                    pl.when(b == 0)(copy.wait)
                add_products(k, terms, b, False)

        loop(backwards, back, backward)
        for copy in bases:
            pl.when(backwards == 0)(copy.wait)
        leaving = [leave(k, name, quartered, copies.at(copies.sem())) for name in targets]
        for copy in leaving:
            copy.wait()
    copies.finish(backwards)
    copies.sent = sent_ahead
    copies.finish(forwards)


SMEM_SPEC = pl.BlockSpec(memory_space=pltpu.SMEM)
HBM_SPEC = pl.BlockSpec(memory_space=pl.ANY)
VMEM_SPEC = pl.BlockSpec(memory_space=pltpu.VMEM)


def shape_of(*shape, dtype=BF):
    return jax.ShapeDtypeStruct(shape, dtype)


def call(kernel, name, ins, outs, scratch, flops, moved):
    names = list(ins) + list(outs) + list(scratch)

    def wrapped(*refs):
        k = Refs()
        for key, ref in zip(names, refs):
            setattr(k, key, ref)
        kernel(k)

    results = pl.pallas_call(
        wrapped,
        grid=(1,),
        out_shape=[shape for shape, _ in outs.values()],
        in_specs=[spec for _, spec in ins.values()],
        out_specs=[spec for _, spec in outs.values()],
        scratch_shapes=list(scratch.values()),
        compiler_params=pltpu.CompilerParams(vmem_limit_bytes=VMEM_LIMIT),
        cost_estimate=pl.CostEstimate(flops=min(flops, 1), bytes_accessed=min(moved, 1), transcendentals=0),
        name=name,
    )(*[array for array, _ in ins.values()])
    return dict(zip(outs, results))


PIECES = ("main", "row", "col", "cor")


def vmem(array):
    return (array, VMEM_SPEC)


def hbm(array):
    return (array, HBM_SPEC)


def run_step(tables, static, landed, counts, groups, old, mlp=True, attention=True, terms=(), base=None, quartered=False):
    sources, held, offsets, shapes = static["weights"]
    rows, wide = tables.rows, shapes[2][0] * shapes[2][2]
    ahead, back = max(counts[:2]), max(counts[2:])
    one = lambda array, index: (array, pl.BlockSpec((TOGETHER,) + array.shape[1:], lambda i: (index, 0, 0)))
    ins = {"sec": (static["sec"], SMEM_SPEC), "put": vmem(static["put"]), "pick": vmem(static["pick"]), "vec": vmem(static["vec"])}
    if landed is not None and (ahead or mlp):
        for name, piece in zip(PIECES, landed):
            ins["p_" + name] = vmem(piece)
    kinds = WEIGHTS if ahead else (("w1", "w2") if mlp else ()) + (("wq", "wo") if attention else ())
    outs, scratch = {}, {}
    for name, shape in zip(WEIGHTS, shapes):
        if name in kinds:
            scratch[name] = pltpu.VMEM(shape, BF)
            if held is None:
                ins[name + "_whole"] = hbm(sources[WEIGHTS.index(name)])
    if held is not None:
        for number, source in enumerate(sources):
            ins[f"pieces_{number}"] = hbm(source)
    widths = {"gp": (wide, BF), "mid": (512, F32), "qkv": (1536, BF), "prob": (1024, BF), "x": (512, BF)}
    for name, (cols, dtype) in widths.items():
        if ahead or (mlp if name in ("gp", "mid") else attention):
            scratch[name] = pltpu.VMEM((2, TOGETHER, rows, cols), dtype)
    local, passed = {}, {}
    if "give" in static and (ahead or attention):
        ins["give"] = vmem(static["give"])
        many = (2, TOGETHER) if ahead else (1, back)
        outs["f_pair"] = (shape_of(*many, static["give"].shape[1], 512), VMEM_SPEC)
        if ahead:
            ins["up"] = vmem(static["up"])
            outs["f_up"] = (shape_of(2, TOGETHER, static["up"].shape[1], 512), VMEM_SPEC)
    if ahead:
        ins["pin"] = one(static["pin"], groups[0])
        ins["bq"], ins["b1"] = vmem(static["bq"]), vmem(static["b1"])
        for name in ("bias", "region"):
            ins[name + "_h"] = hbm(static[name])
            scratch[name] = pltpu.VMEM(static[name].shape, F32)
        for name, size in zip(PIECES, tables.sizes):
            outs["s_" + name] = (shape_of(TOGETHER, size, 512), VMEM_SPEC)
            if "give" not in static:
                outs["h_" + name] = (shape_of(2, TOGETHER, size, 512), VMEM_SPEC)
        for name, (cols, dtype) in widths.items():
            outs[name + "_o"] = (shape_of(TOGETHER, rows, cols, dtype=dtype), HBM_SPEC)
        local |= {"a": (512, BF), "ctx": (512, BF), "n2": (512, BF), "act": (wide, BF), "y": (512, BF)}
    if back:
        if mlp:
            for name, target in zip(PIECES, static["targets"]):
                ins["c_" + name] = one(target, groups[1])
            local |= {"g": (512, BF), "dh": (wide, BF), "gm": (512, BF)}
            (passed if attention else local)["dmid"] = (512, F32)
        else:
            passed |= {"gm": (512, BF), "dmid": (512, F32)}
        needed = (("gp", "mid") if mlp else ("gm", "dmid")) + (("qkv", "prob", "x") if attention else ())
        for name in dict.fromkeys(name for term in terms for name in term[:2]):
            if name in AHEAD:
                needed += (name,)
                passed[name] = (old[name + "_o"].shape[2], BF)
        for name in needed:
            ins["old_" + name] = hbm(old[name + "_o"])
        for name, array in (base or {}).items():
            ins[name + "_b"] = hbm(array)
            scratch[name] = pltpu.VMEM(array.shape, BF)
        outs |= leaving_shapes({name: array.shape for name, array in (base or {}).items()}, quartered)
        if attention:
            local |= {"dqkv": (1536, BF), "dx": (512, BF)}
            scratch["dctx"] = pltpu.VMEM((rows, 512), BF)
            outs["dbias"] = (shape_of(SLOT, 1024, dtype=F32), VMEM_SPEC)
        scratch["dn"] = pltpu.VMEM((rows, 512), F32)
        outs["small"] = (shape_of(8, 2048, dtype=F32), VMEM_SPEC)
    for name, (cols, dtype) in local.items():
        outs[name + "_o"] = (shape_of(TOGETHER, rows, cols, dtype=dtype), HBM_SPEC)
        scratch[name] = pltpu.VMEM((TOGETHER, rows, cols), dtype)
    for name, (cols, dtype) in passed.items():
        scratch[name] = pltpu.VMEM((TOGETHER, rows, cols), dtype)
    scratch["sems"] = pltpu.SemaphoreType.DMA((192,))
    passes = 2 * ahead + 2 * back * (mlp + attention)
    kernel = functools.partial(step_kernel, tables.wins, held, offsets, counts, mlp, attention, terms, quartered)

    def run(k):
        k.landed = landed is not None
        k.needed = needed if back else ()
        kernel(k)

    return call(run, "layer_step", ins, outs, scratch, 2 * passes * rows * TOGETHER * 3145728, 20_000_000)


def add_products(k, terms, place, fresh):
    for left, right, cut_left, name, first, rows in terms:
        l, r, t = getattr(k, left).at[place], getattr(k, right).at[place], getattr(k, name)
        parts = t.shape[0]
        for part in range(parts):
            width = (l if cut_left else r).shape[1] // parts
            cols = slice(part * width, (part + 1) * width)
            value = mm(l[:, cols], r[...], TN) if cut_left else mm(l[...], r[:, cols], TN)
            if not fresh:
                value = value + t[part, first : first + rows, :].astype(F32)
            t[part, first : first + rows, :] = value.astype(BF)


def leave(k, name, quartered, sem):
    t = getattr(k, name)
    if not quartered:
        copy = pltpu.make_async_copy(t, getattr(k, name + "_o"), sem)
        copy.start()
        return copy
    keep, send = getattr(k, name + "_k"), getattr(k, name + "_s")
    high = t.shape[1] // 4
    for core in range(2):

        @pl.when(lax.rem(k.sec[1], 2) == core)
        def _(core=core):
            for quarter in range(4):
                place = keep if quarter % 2 == core else send
                pltpu.make_async_copy(t.at[:, pl.ds(quarter * high, high), :], place.at[:, quarter // 2], sem).start()

    return arrival(t, sem)


def leaving_shapes(shapes, quartered):
    outs = {}
    for name, shape in shapes.items():
        if quartered:
            for kind in "ks":
                outs[f"{name}_{kind}"] = (shape_of(shape[0], 2, shape[1] // 4, shape[2]), HBM_SPEC)
        else:
            outs[name + "_o"] = (shape_of(*shape), HBM_SPEC)
    return outs


def weight_grad_kernel(slots, terms, based, k):
    def run(section):
        sems = iter(range(64))
        waits = {}
        for name in dict.fromkeys(name for term in terms for name in term[:2]):
            places, target, sem = slots[name][section], getattr(k, name), k.sems.at[next(sems)]
            rows = getattr(k, f"{name}_{places[0][0]}").shape[1]
            for at, (step, place) in enumerate(places):
                source = getattr(k, f"{name}_{step}").at[place]
                pltpu.make_async_copy(source, target.at[pl.ds(at * rows, rows), :], sem).start()
            waits[name] = arrival(target.at[pl.ds(0, len(places) * rows), :], sem)
            all_rows = pl.ds(0, len(places) * rows)
        if section == 0:
            for name in based:
                waits[name] = pltpu.make_async_copy(getattr(k, name + "_b"), getattr(k, name), k.sems.at[next(sems)])
                waits[name].start()
        leaving = []
        for number, term in enumerate(terms):
            fresh = term[3] not in based or section == 1
            for needed in (term[0], term[1], term[3]):
                if needed in waits:
                    waits.pop(needed).wait()
            add_products(k, (term,), all_rows, fresh)
            if all(term[3] != later[3] for later in terms[number + 1 :]):
                leaving.append(leave(k, term[3], False, k.sems.at[next(sems)]))
        for copy in leaving:
            copy.wait()

    for section in range(2):
        if slots[terms[0][0]][section]:
            pl.when(k.sec[0] == section)(functools.partial(run, section))


def run_weight_grad(static, steps, counted, terms, shapes, base):
    ins = {"sec": (static["sec"], SMEM_SPEC)}
    scratch, slots = {}, {}
    for name in dict.fromkeys(name for term in terms for name in term[:2]):
        shifts = (0, 1) if name in AHEAD else (2, 1)
        slots[name] = [[(at // TOGETHER + shift, at % TOGETHER) for at in count] for count, shift in zip(counted, shifts)]
        for step in sorted({step for places in slots[name] for step, _ in places}):
            array = steps[step][name + "_o"]
            ins[f"{name}_{step}"] = hbm(array)
        most = max(len(places) for places in slots[name])
        scratch[name] = pltpu.VMEM((most * array.shape[1], array.shape[2]), BF)
    for name, shape in shapes.items():
        scratch[name] = pltpu.VMEM(shape, BF)
        if base:
            ins[name + "_b"] = hbm(base[name])
    scratch["sems"] = pltpu.SemaphoreType.DMA((64,))
    kernel = functools.partial(weight_grad_kernel, slots, terms, tuple(base))
    done = call(kernel, "weight_grad", ins, leaving_shapes(shapes, False), scratch, 0, 0)
    return {name: done[name + "_o"] for name in shapes}


def collect(arrays):
    ins = {f"{name}_{i}": vmem(array) for name, members in arrays.items() for i, array in enumerate(members)}
    outs = {name: (shape_of(len(members), *members[0].shape), VMEM_SPEC) for name, members in arrays.items()}

    def kernel(k):
        for name, members in arrays.items():
            for i in range(len(members)):
                getattr(k, name)[i] = getattr(k, f"{name}_{i}")[...]

    return call(kernel, "collect", ins, outs, {}, 0, 4_000_000)


def run_patches(static, plain, mains, halo, sizes):
    rows = plain[0][0].shape[1]
    batches = sum(sizes)
    ins = {"sec": (static["sec"], SMEM_SPEC), "pick": vmem(static["pick"])}
    for group, (pair, main) in enumerate(zip(plain, mains)):
        ins[f"plain_0_{group}"], ins[f"plain_1_{group}"], ins[f"main_{group}"] = vmem(pair[0]), vmem(pair[1]), vmem(main)
    for name, array in zip(PIECES[1:], halo):
        ins[name] = vmem(array)
    outs = {"patch": (shape_of(2 * batches, rows, 512), VMEM_SPEC)}

    def kernel(k):
        for kind in range(2):
            for group, size in enumerate(sizes):
                for b in range(size):
                    at = kind * batches + sum(sizes[:group]) + b

                    @pl.when(k.sec[0] == 0)
                    def _(at=at, kind=kind, group=group, b=b):
                        k.patch[at] = getattr(k, f"plain_{kind}_{group}")[b]

                    @pl.when(k.sec[0] == 1)
                    def _(at=at, kind=kind, group=group, b=b):
                        parts = [getattr(k, f"main_{group}")[kind, b]] + [getattr(k, name)[group, kind, b] for name in PIECES[1:]]
                        k.patch[at] = mm(k.pick[...], jnp.concatenate(parts, axis=0), TN).astype(BF)

    return call(kernel, "patches", ins, outs, {}, 0, 0)


def run_places(static, steps, pairs, ups, own, take, land, sizes, tokens):
    batches, groups = sum(sizes), len(sizes)
    ins = {"sec": (static["sec"], SMEM_SPEC), "own": vmem(own), "take": vmem(take), "land_0": vmem(land[0]), "land_1": vmem(land[1])}
    for step, done in enumerate(steps):
        for name in ("y_o", "dx_o"):
            if name in done:
                ins[f"{name}_{step}"] = vmem(done[name])
        ins[f"pair_{step}"] = vmem(pairs[step])
        for side, array in enumerate(ups[step]):
            ins[f"up_{side}_{step}"] = vmem(array)
    outs = {"first": (shape_of(batches, tokens, 512), VMEM_SPEC), "second": (shape_of(batches, tokens, 512, dtype=F32), VMEM_SPEC)}

    def kernel(k):
        for kind, name in enumerate(("y_o", "dx_o")):
            for group, size in enumerate(sizes):
                for b in range(size):
                    at = sum(sizes[:group]) + b

                    def put(value, at=at, kind=kind):
                        if kind == 0:
                            k.first[at] = value.astype(BF)
                        else:
                            k.second[at] = value

                    def here(step, kind=kind, name=name, b=b):
                        value = mm(k.own[...], getattr(k, f"{name}_{step}")[b], TN)
                        return value + mm(k.take[...], getattr(k, f"pair_{step}")[kind % pairs[step].shape[0], b], TN)

                    @pl.when(k.sec[0] == 0)
                    def _(group=group, kind=kind, put=put, here=here):
                        put(here(group + 2 * kind))

                    @pl.when(k.sec[0] == 1)
                    def _(group=group, kind=kind, b=b, put=put, here=here):
                        value = here(group + 1)
                        for side in range(2):
                            value = value + mm(getattr(k, f"land_{side}")[...], getattr(k, f"up_{side}_{group + 1}")[kind, b], TN)
                        put(value)

    return call(kernel, "places", ins, outs, {}, 0, 0)


def table_onehot():
    code = np.full((SLOT, SLOT), -1, np.int32)
    for u in range(TOKENS):
        for t in range(TOKENS):
            code[u, t] = (t // WIN - u // WIN + WIN - 1) * (2 * WIN - 1) + t % WIN - u % WIN + WIN - 1
    side = (2 * WIN - 1) ** 2
    return (jnp.arange(side, dtype=jnp.int32)[:, None] == jnp.asarray(code.reshape(1, -1))).astype(F32)


def region_mask(layout, section):
    row, mp = lax.axis_index(ROW), lax.axis_index(MP)
    window_row = row * WROWS + mp // layout.across
    window_col = (mp % layout.across) * layout.wins + jnp.arange(layout.wins)
    place = jnp.arange(SLOT)
    row_label = jnp.where(window_row == layout.high - 1, 1 + (place // WIN >= WIN - SHIFT).astype(jnp.int32), 0)
    col_label = jnp.where(
        (window_col == WCOLS - 1)[:, None], 1 + (place % WIN >= WIN - SHIFT).astype(jnp.int32)[None], 0
    )
    labels = 3 * row_label[None] + col_label
    differs = labels[:, :, None] != labels[:, None, :]
    term = jnp.where(differs & (section == 1), -100.0, 0.0).astype(F32)
    return jnp.tile(term, (1, 1, GROUP))


def full_patches(layout, mp, tokens):
    wins = layout.wins
    place = jnp.arange(wins * SLOT)
    window, inner = place // SLOT, place % SLOT
    row = (mp // layout.across) * WIN + inner // WIN
    col = ((mp % layout.across) * wins + window) * WIN + inner % WIN
    token = jnp.where(inner < TOKENS, row * (WCOLS * WIN) + col, -1)
    return (token[:, None] == jnp.arange(tokens)[None]).astype(BF)


def whole_patches(layout, mp, tokens_here):
    token = mp * tokens_here + jnp.arange(tokens_here)
    row, col = token // (WCOLS * WIN), token % (WCOLS * WIN)
    window = col // WIN
    owner = (row // WIN) * layout.across + window // layout.wins
    place = owner * layout.wins * SLOT + (window % layout.wins) * SLOT + (row % WIN) * WIN + col % WIN
    return (place[:, None] == jnp.arange(layout.mp_count * layout.wins * SLOT)[None]).astype(BF)


def low_dot(matrix, stack):
    return jnp.einsum("pr,nrd->npd", matrix, stack, preferred_element_type=F32).astype(BF)


def body(
    layer_input,
    out_cotangent,
    norm_one_gain,
    norm_one_bias,
    attend_weight,
    attend_bias,
    position_table,
    output_weight,
    output_bias,
    norm_two_gain,
    norm_two_bias,
    expand_weight,
    expand_bias,
    reduce_weight,
    reduce_bias,
):
    row_count, mp_count = lax.axis_size(ROW), lax.axis_size(MP)
    section, mp = lax.axis_index(SECTION), lax.axis_index(MP)
    layout = Layout(row_count, mp_count)
    tables = Tables(layout.wins)
    put = jnp.asarray(tables.put, BF)
    pick = jnp.asarray(tables.pick, BF)
    batches, tokens_here, width = layer_input.shape
    heads_here = attend_weight.shape[2]
    hidden_here = expand_weight.shape[2]
    row = lax.axis_index(ROW)
    sec = jnp.stack([section, row, mp]).astype(jnp.int32)
    paired = layout.across == 2 and row_count == 4
    first = section == 0

    flat = jnp.concatenate([attend_bias[0].reshape(-1), position_table[0].reshape(-1), expand_bias[0].reshape(-1)])
    wq_rows = attend_weight[0].transpose(1, 2, 0).reshape(heads_here, 3, 32, width)
    if paired:
        quarter = lambda array: take_at(array.reshape(4, -1, width), row)
        shards = (wq_rows.transpose(1, 0, 2, 3), output_weight[0], expand_weight[0], reduce_weight[0])
        quarters = [quarter(array) for array in shards]
        offsets = np.cumsum([0] + [array.shape[0] for array in quarters])[:-1].tolist()
        here = jnp.concatenate(quarters)
        near, far = ring(here, MP), ring(here, MP, -1)
        further = ring(near, MP)
        across = lambda piece: swap(piece, ROW, 2)
        crossed = [across(here), across(near), across(far)]
        after = ring(flat, MP)
        flat_all = natural_ring([flat, after, ring(after, MP), ring(flat, MP, -1)], mp)
    else:
        wq_all = lax.all_gather(wq_rows, MP, axis=0).reshape(4, GROUP, 3, 32, width).transpose(0, 2, 1, 3, 4)
        wq_all = wq_all.reshape(4 * GROUP * 96, width)
        wo_all = lax.all_gather(output_weight[0], MP, axis=0).reshape(-1, width)
        w1_all = lax.all_gather(expand_weight[0], MP, axis=0)
        w2_all = lax.all_gather(reduce_weight[0], MP, axis=0).reshape(-1, width)
        flat_all = lax.all_gather(flat, MP, axis=0)
        whole = (wq_all, wo_all, w1_all, w2_all)
        weights = (whole, None, None, tuple(array.shape for array in whole))
    cut_one = heads_here * 64
    cut_two = cut_one + heads_here * position_table.shape[2]
    bias_all = flat_all[:, :cut_one].reshape(4, GROUP, 2, 32)
    table_all = flat_all[:, cut_one:cut_two].reshape(-1, position_table.shape[2])
    b1 = flat_all[:, cut_two:]
    bq = jnp.stack([bias_all[:, :, 0], jnp.zeros_like(bias_all[:, :, 0]), bias_all[:, :, 1]], axis=1).reshape(1, -1)
    onehot = table_onehot()
    bias = jnp.dot(table_all, onehot, precision=highest).reshape(4, GROUP, SLOT, SLOT).transpose(0, 2, 1, 3)
    bias = bias.reshape(4, SLOT, GROUP * SLOT) + jnp.where(jnp.arange(SLOT) < TOKENS, 0.0, -1e30)[None, :, None]
    vec = jnp.concatenate(
        [norm_one_gain, norm_one_bias, output_bias, norm_two_gain, norm_two_bias, reduce_bias, jnp.zeros((2, width), F32)]
    )
    region = region_mask(layout, section)

    taken = jnp.where(first, layer_input, out_cotangent)
    if paired:
        keep, take, send = pair_tables(layout.wins)
        side = mp % 2
        keep = lax.dynamic_index_in_dim(jnp.asarray(keep, BF), side, 0, keepdims=False)
        take = lax.dynamic_index_in_dim(jnp.asarray(take, BF), side, 0, keepdims=False)
        send = jnp.asarray(send, BF)
        arrived = swap(low_dot(send, taken), MP, 1)
        pin = low_dot(jnp.concatenate([keep, take], axis=1), jnp.concatenate([taken, arrived], axis=1))
        own, give, take, up, land = (jnp.asarray(table, BF) for table in placing_tables(layout.wins))
        own, give, take = (take_at(take_at(table, section), side) for table in (own, give, take))
        land = jnp.where((section == 1) & (side == 0), land, 0)
    else:
        everything = lax.all_gather(taken, MP, axis=1, tiled=True)
        pin = low_dot(full_patches(layout, mp, everything.shape[1]), everything)
    groups = -(-batches // TOGETHER)
    sizes = [min(TOGETHER, batches - TOGETHER * group) for group in range(groups)]
    pin = jnp.pad(pin, ((0, TOGETHER * groups - batches), (0, 0), (0, 0)))
    cuts = np.cumsum(tables.sizes)[:-1].tolist()
    targets = halo_inside(layout, jnp.split(low_dot(pick, pin), cuts, axis=1), False)
    if paired:
        further, pin, bias, region, bq, b1 = lax.optimization_barrier((further, pin, bias, region, bq, b1))
        arrays = [jnp.stack([here, near, crossed[0], crossed[1]]), jnp.stack([far, further, crossed[2], across(further)])]
        held = (((0, 0), (0, 1), (2, 0), (2, 1)), ((0, 3), (0, 2), (2, 3), (2, 2)))
        arrays[1], targets = lax.optimization_barrier((arrays[1], targets))
        held += tuple(tuple((bits + 1, back) for bits, back in places) for places in held)
        weights = (
            arrays + [swap(array, ROW, 1) for array in arrays],
            held,
            offsets,
            ((4 * GROUP * 96, width), (4 * GROUP * 32, width), (mp_count, width, hidden_here), (mp_count * hidden_here, width)),
        )

    static = dict(
        sec=sec, weights=weights, pin=pin, targets=targets, put=put, pick=pick, vec=vec, bq=bq, b1=b1, bias=bias, region=region
    )
    if paired:
        static |= dict(give=give, up=up)
    size_of = lambda group: sizes[group] if 0 <= group < groups else 0
    landed = None
    steps, pairs, ups = [], [], []
    mlp_terms = (("act", "g", True, "d2", 0, hidden_here), ("n2", "dh", False, "d1", 0, width))
    heads_terms = (("dqkv", "a", True, "da", 0, GROUP * 96), ("ctx", "gm", True, "da", GROUP * 96, GROUP * 32))
    terms = mlp_terms + heads_terms
    shapes = {"d2": (mp_count, hidden_here, width), "d1": (mp_count, width, hidden_here), "da": (4, GROUP * 128, width)}
    early, ready = TOGETHER * (groups - 1), max(TOGETHER * (groups - 2), 0)
    grads_base = {}
    for step in range(groups + 1):
        counts = (size_of(step), size_of(step - 1), size_of(step - 2), size_of(step - 1))
        which = (min(step, groups - 1), max(step - 1, 0))
        done = run_step(tables, static, landed, counts, which, steps[max(step - 2, 0)] if step else None)
        steps.append(done)
        sends = [done["s_" + name] for name in PIECES]
        pair, up_piece = done.get("f_pair"), done.get("f_up")
        if step == groups:
            sends = [piece[: sizes[-1]] for piece in sends]
        if paired:
            sends, pairs, ups = lax.optimization_barrier((sends, pairs, ups))
        if step == groups - 1 and ready:
            grads_base = run_weight_grad(static, steps, (range(ready), ()), terms, shapes, {})
            sends, grads_base = lax.optimization_barrier((sends, grads_base))
        landed = halo_swap(layout, sends, step == groups)
        if paired:
            if step == groups:
                break
            landed, pair, up_piece = lax.optimization_barrier((landed, pair, up_piece))
            pairs = pairs + [swap(pair, MP, 1)]
            ups = ups + [[lax.ppermute(up_piece, AXES, route) for route in layout.up_routes()] if step else []]

    if not paired:
        halo = collect({name: [done["h_" + name] for done in steps[1:]] for name in PIECES[1:]})
        halo = [halo[name] for name in PIECES[1:]]
        flat_halo = halo_inside(layout, [None] + [array.reshape((-1,) + array.shape[3:]) for array in halo], True)[1:]
        halo = [flat.reshape(array.shape) for flat, array in zip(flat_halo, halo)]

    grads_base = run_weight_grad(static, steps, (range(ready, early), range(batches)), terms, shapes, grads_base)
    landed, grads_base = lax.optimization_barrier((landed, grads_base))
    after = sec
    if paired:
        grads_base, pair, up_piece = lax.optimization_barrier((grads_base, pair, up_piece[:, : sizes[-1]]))
        pairs = pairs + [swap(pair, MP, 1)]
        ups = ups + [[lax.ppermute(up_piece, AXES, route) for route in layout.up_routes()]]
    mlp_base = {name: grads_base[name] for name in ("d2", "d1")}
    heads_base = {"da": grads_base["da"]}

    counts = (0, 0, sizes[-1], 0)
    which = (groups - 1, groups - 1)
    old = steps[-2]
    last = run_step(
        tables, static, landed, counts, which, old, attention=False, terms=mlp_terms, base=mlp_base, quartered=paired
    )
    if paired:
        last, pairs, ups = lax.optimization_barrier((last, pairs, ups))
        d2, d1 = (last[name + "_k"] + swap(last[name + "_s"], ROW, 1) for name in ("d2", "d1"))
        after, d2, d1 = lax.optimization_barrier((sec, d2, d1))
    heads = run_step(
        tables, dict(static, sec=after), None, counts, which, {**old, **last}, mlp=False, terms=heads_terms, base=heads_base, quartered=paired
    )
    smalls = [done["small"] for done in steps[1:] + [last, heads]]
    biases = [done["dbias"] for done in steps[1:] + [heads]]
    steps.append({**last, **heads})
    def summed(smalls, biases):
        small = sum(smalls)[:4]
        table = sum(biases).reshape(SLOT, 4 * GROUP, SLOT).transpose(1, 0, 2).reshape(4 * GROUP, -1)
        table = jnp.dot(table, onehot.T, precision=highest)
        flat = jnp.pad(table.reshape(-1), (0, -table.size % 2048)).reshape(-1, 2048)
        return jnp.concatenate([small, flat])

    if paired:
        high, core = row // 2, row % 2
        gate = lax.optimization_barrier
        term = lambda part, step: take_at(part, (mp - 2 - step) % mp_count)

        def joined(pair, crossed):
            whole = jnp.stack([jnp.where(core == 0, pair, crossed), jnp.where(core == 0, crossed, pair)], axis=1)
            return whole.astype(F32).reshape(-1, width)

        def around(array, axis):
            return [swap(array, axis, bits) for bits in (1, 2, 3)]

        def in_pairs(array, came):
            return (array + came[0]) + (came[1] + came[2])

        def ordered(mine, other):
            return jnp.stack([jnp.where(high == 0, mine, other), jnp.where(high == 0, other, mine)])

        d2_came, d1_came = ring(take_at(d2, (mp - 1) % mp_count), MP), swap(take_at(d1, 1 - high, 1), ROW, 2)
        d2_came, d1_came, sending = gate((d2_came, d1_came, heads["da_s"]))
        da_came, pair_came = swap(sending, ROW, 1), lax.ppermute(heads["f_pair"], AXES, layout.pair_route(0))
        d2_total, d1 = d2_came + term(d2, 0), take_at(d1, high, 1) + d1_came
        d2_came, d1_came = ring(d2_total, MP), ring(take_at(d1, (mp - 1) % mp_count), MP)
        da = heads["da_k"] + da_came
        mine, other = take_at(da, high, 1), take_at(da, 1 - high, 1)
        da_came = swap(other, ROW, 2)
        d1_came, _ = gate((d1_came, other))
        sending = d1_came + term(d1, 0)
        d1_came = ring(sending, MP)
        pair_came, _ = gate((pair_came, sending))
        placed = run_places(static, steps, pairs + [pair_came], ups + [[]], own, take, land, sizes, tokens_here)
        da_came, first_out, second_out = gate((da_came, placed["first"], placed["second"]))
        da = mine + da_came
        sending = take_at(da, (mp - 1) % mp_count)
        da_came = ring(sending, MP)
        d2_came, d1_came, smalls, biases, _ = gate((d2_came, d1_came, smalls, biases, sending))
        d2_total, d1_total = d2_came + term(d2, 1), d1_came + term(d1, 1)
        d2_came, d1_came = ring(d2_total, MP), ring(d1_total, MP)
        sums = summed(smalls, biases)
        sending = da_came + term(da, 0)
        da_came = ring(sending, MP)
        d2_came, d1_came, sums, _ = gate((d2_came, d1_came, sums, sending))
        d2, d1 = d2_came + term(d2, 2), d1_came + term(d1, 2)
        d2_came, d1_came, sums_came = swap(d2, ROW, 2), swap(d1, ROW, 2), around(sums, ROW)
        sending = da_came + term(da, 1)
        da_came = ring(sending, MP)
        d2_came, d1_came, sums_came, _ = gate((d2_came, d1_came, sums_came, sending))
        d2, d1, sums = d2 + d2_came, ordered(d1, d1_came), in_pairs(sums, sums_came)
        d2_came, d1_came, sums_came = swap(d2, ROW, 1), swap(d1, ROW, 1), around(sums, MP)
        da = da_came + term(da, 2)
        da_came = swap(da, ROW, 2)
        d2_came, d1_came, _ = gate((d2_came, d1_came, da))
        d2, d1 = joined(d2, d2_came), joined(d1, d1_came)
        da = ordered(da, da_came)
        da_came = swap(da, ROW, 1)
        sums_came, _ = gate((sums_came, da))
        sums = in_pairs(sums, sums_came)
        da = joined(da, da_came)
        dq, do = da[: GROUP * 96].reshape(3, GROUP, 32, width), da[GROUP * 96 :]
        dq = dq.transpose(3, 1, 0, 2).reshape(attend_weight.shape[1:])
    else:

        def shared(parts):
            part = lax.psum_scatter(parts, MP, scatter_dimension=0, tiled=False)
            return lax.psum(part, ROW).astype(F32)

        da = heads["da_o"]
        dq = da[:, : GROUP * 96].reshape(4, 3, GROUP, 32, width).transpose(0, 2, 1, 3, 4).reshape(mp_count, heads_here * 96, width)
        d2, d1, do = shared(last["d2_o"]), shared(last["d1_o"]), shared(da[:, GROUP * 96 :].reshape(mp_count, heads_here * 32, width))
        dq = shared(dq).T.reshape(attend_weight.shape[1:])
        sums = lax.psum(summed(smalls, biases), (ROW, MP))
    small = sums[:4]
    table = sums[4:].reshape(-1)[: 4 * GROUP * onehot.shape[0]].reshape(4 * GROUP, -1)
    shift = small[3, :1536].reshape(4, 3, GROUP, 32)
    shift = jnp.concatenate([shift[:, 0], shift[:, 2]], axis=-1).reshape(4 * GROUP, 64)
    mine = lambda array: lax.dynamic_index_in_dim(array.reshape((mp_count, -1) + array.shape[1:]), mp, 0, keepdims=False)

    if not paired:
        plain = [(steps[group]["y_o"], steps[group + 2]["dx_o"]) for group in range(groups)]
        mains = [steps[group + 1]["h_main"] for group in range(groups)]
        made = run_patches(static, plain, mains, halo, sizes)
        everything = lax.all_gather(made["patch"], MP, axis=1, tiled=True)
        placed = low_dot(whole_patches(layout, mp, tokens_here), everything)
        first_out, second_out = placed[:batches], placed[batches:].astype(F32)

    return (
        first_out[None],
        second_out[None],
        small[1, 1024:1536][None],
        small[1, 1536:2048][None],
        dq[None],
        mine(shift)[None],
        mine(table)[None],
        do.reshape(output_weight.shape),
        small[1, 512:1024][None],
        small[2, 0:512][None],
        small[2, 512:1024][None],
        d1[None],
        mine(small[0])[None],
        d2[None],
        small[1, 0:512][None],
    )


def solution(mesh):
    return jax.shard_map(
        body,
        mesh=mesh,
        in_specs=(
            P(None, (ROW, MP), None),
            P(None, (ROW, MP), None),
            P(SECTION, None),
            P(SECTION, None),
            P(SECTION, None, MP, None),
            P(SECTION, MP, None),
            P(SECTION, MP, None),
            P(SECTION, MP, None, None),
            P(SECTION, None),
            P(SECTION, None),
            P(SECTION, None),
            P(SECTION, None, MP),
            P(SECTION, MP),
            P(SECTION, MP, None),
            P(SECTION, None),
        ),
        out_specs=(
            P(SECTION, None, (ROW, MP), None),
            P(SECTION, None, (ROW, MP), None),
            P(SECTION, None),
            P(SECTION, None),
            P(SECTION, None, MP, None),
            P(SECTION, MP, None),
            P(SECTION, MP, None),
            P(SECTION, MP, None, None),
            P(SECTION, None),
            P(SECTION, None),
            P(SECTION, None),
            P(SECTION, None, MP),
            P(SECTION, MP),
            P(SECTION, MP, None),
            P(SECTION, None),
        ),
        check_vma=False,
    )
```

```python
import functools

import jax
import jax.numpy as jnp
import numpy as np
from jax import lax
from jax.experimental import pallas as pl
from jax.experimental.pallas import tpu as pltpu
from jax.sharding import PartitionSpec as P

WIN = 7
SHIFT = 3
WCOLS = 8
WROWS = 2
TOKENS = WIN * WIN
SLOT = 64
GROUP = 4
SECTION, ROW, MP = AXES = ("section", "row", "mp")
EPS = 1e-05
BF = jnp.bfloat16
F32 = jnp.float32
NN = (((1,), (0,)), ((), ()))
NT = (((1,), (1,)), ((), ()))
TN = (((0,), (0,)), ((), ()))
VMEM_LIMIT = 52 * 1024 * 1024
highest = lax.Precision.HIGHEST


def mm(left, right, dims=NN):
    return lax.dot_general(left, right, dims, preferred_element_type=F32)


def up16(count):
    return -(-count // 16) * 16


def patch_place(row, col):
    return (col // WIN) * SLOT + row * WIN + col % WIN


class Tables:
    def __init__(self, wins):
        self.wins = wins
        self.rows = wins * SLOT
        cols = wins * WIN
        wide = range(SHIFT, cols)
        thin = range(SHIFT)
        low, high = range(SHIFT, WIN), range(SHIFT)
        pieces = [(low, wide), (high, wide), (low, thin), (high, thin)]
        self.sizes = [up16(len(a) * len(b)) for a, b in pieces]
        self.total = sum(self.sizes)
        pick = np.zeros((self.total, self.rows), np.float32)
        put = np.zeros((self.rows, self.total), np.float32)
        at = 0
        for (rows, columns), size in zip(pieces, self.sizes):
            spot = at
            for row in rows:
                for col in columns:
                    pick[spot, patch_place(row, col)] = 1
                    put[patch_place((row - SHIFT) % WIN, (col - SHIFT) % cols), spot] = 1
                    spot += 1
            at += size
        self.pick, self.put = pick, put


def pair_tables(wins):
    cols = wins * WIN
    tokens = WIN * cols
    keep = np.zeros((2, wins * SLOT, tokens), np.float32)
    take = np.zeros((2, wins * SLOT, up16(SHIFT * cols)), np.float32)
    send = np.zeros((up16(SHIFT * cols), tokens), np.float32)
    for seg in range(SHIFT):
        for col in range(cols):
            send[seg * cols + col, (2 * seg + 1) * cols + col] = 1
    for side in range(2):
        for row in range(WIN):
            for col in range(cols):
                place = patch_place(row, col)
                own = row <= SHIFT if side == 0 else row >= SHIFT
                if own:
                    seg = row if side == 0 else row - SHIFT
                    keep[side, place, 2 * seg * cols + col] = 1
                else:
                    seg = row - SHIFT - 1 if side == 0 else row
                    take[side, place, seg * cols + col] = 1
    return keep, take, send


def placing_tables(wins):
    cols, tokens, most = wins * WIN, WIN * wins * WIN, up16(SHIFT * (wins * WIN + 1))
    own = np.zeros((2, 2, wins * SLOT, tokens), np.float32)
    give = np.zeros((2, 2, wins * SLOT, most), np.float32)
    take = np.zeros((2, 2, most, tokens), np.float32)
    up = np.zeros((wins * SLOT, most), np.float32)
    land = np.zeros((2, most, tokens), np.float32)
    half = SHIFT * 2 * cols + cols

    def holder(row, col):
        token = row * 2 * cols + col
        return (0, token) if token < half else (1, token - half)

    for section in range(2):
        for side in range(2):
            given, raised = 0, 0
            for row in range(WIN):
                for col in range(cols):
                    place = patch_place(row, col)
                    real_row = row + SHIFT * section
                    real_col = (side * cols + col + SHIFT * section) % (2 * cols)
                    if real_row >= WIN:
                        up[place, raised] = 1
                        land[side, raised, holder(real_row - WIN, real_col)[1]] = 1
                        raised += 1
                        continue
                    keeper, token = holder(real_row, real_col)
                    if keeper == side:
                        own[section, side, place, token] = 1
                    else:
                        give[section, side, place, given] = 1
                        take[section, keeper, given, token] = 1
                        given += 1
    return own, give, take, up, land


class Layout:
    def __init__(self, row_count, mp_count):
        self.row_count, self.mp_count = row_count, mp_count
        self.across = mp_count // WROWS
        self.wins = WCOLS // self.across
        self.high = row_count * WROWS

    def device(self, section, window_row, place):
        window_row, place = window_row % self.high, place % self.across
        row = window_row // WROWS
        return (section * self.row_count + row) * self.mp_count + (window_row % WROWS) * self.across + place

    def route(self, source, target, up, back):
        return [
            (self.device(source, window_row, place), self.device(target, window_row - up, place - back))
            for window_row in range(self.high)
            for place in range(self.across)
        ]


    def pair_route(self, section):
        return [
            (self.device(section, window_row, side), self.device(section, window_row, 1 - side))
            for window_row in range(self.high)
            for side in range(2)
        ]

    def up_routes(self):
        return [
            [(self.device(1, window_row, side), self.device(1, window_row + 1, 0)) for window_row in range(self.high)] for side in range(2)
        ]


HALO = ((0, 0), (1, 0), (0, 1), (1, 1))


def halo_swap(layout, parts, back_only):
    result = []
    for part, by in zip(parts, HALO):
        there = layout.route(0, 1, *by)
        result.append(lax.ppermute(part, AXES, [(b, a) for a, b in there] + ([] if back_only else there)))
    return result


def halo_inside(layout, parts, back):
    result = [parts[0]]
    for part, by in zip(parts[1:], HALO[1:]):
        there = layout.route(1, 1, *by)
        result.append(lax.ppermute(part, AXES, [(b, a) for a, b in there] if back else there))
    return result


def ring(shard, axis, by=1):
    count = lax.axis_size(axis)
    return lax.ppermute(shard, axis, [(i, (i + by) % count) for i in range(count)])


def swap(shard, axis, bit):
    return lax.ppermute(shard, axis, [(i, i ^ bit) for i in range(lax.axis_size(axis))])


def natural_ring(shards, mp):
    stacked, count = jnp.stack(shards), len(shards)
    return jnp.stack([lax.dynamic_index_in_dim(stacked, (mp - j) % count, 0, keepdims=False) for j in range(count)])


def take_at(array, index, axis=0):
    return lax.dynamic_index_in_dim(array, index, axis, keepdims=False)


def head_masks(dtype):
    lane = lax.broadcasted_iota(jnp.int32, (1, GROUP * 32), 1)
    return [jnp.where(lane // 32 == h, 1.0, 0.0).astype(dtype) for h in range(GROUP)]


def spread_heads(block, masks):
    return jnp.concatenate([block * mask for mask in masks], axis=0)


def fold_heads(tall, masks):
    total = tall[:SLOT] * masks[0]
    for h in range(1, GROUP):
        total = total + tall[h * SLOT : (h + 1) * SLOT] * masks[h]
    return total


def centre(values):
    middle = jnp.mean(values, axis=-1, keepdims=True)
    centred = values - middle
    scale = lax.rsqrt(jnp.mean(centred * centred, axis=-1, keepdims=True) + EPS)
    return centred * scale, scale


KEPT = ("gp", "mid", "qkv", "prob", "x")
WEIGHTS = ("wq", "wo", "w1", "w2")
AHEAD = ("act", "n2", "a", "ctx")
TOGETHER = 2


class Refs:
    pass


class Copies:
    def __init__(self, sems):
        self.sems, self.used, self.sent = sems, 0, []

    def sem(self, count=1):
        self.used += count
        return self.used - count

    def at(self, index):
        return self.sems.at[index]

    def ship(self, b, make, wanted):
        first = self.sem(TOGETHER)
        maker = lambda b: make(b, self.at(first + b))
        pl.when(wanted())(lambda: maker(b).start())
        self.sent.append((maker, wanted))

    def finish(self, count):
        for b in range(TOGETHER):

            @pl.when(b < count)
            def _(b=b):
                for maker, wanted in self.sent:
                    pl.when(wanted())(lambda maker=maker: maker(b).wait())

        self.sent = []


def arrival(target, sem):
    return pltpu.make_async_copy(target, target, sem)


def load_weights(k, kinds, held, offsets, wanted):
    waits = {}
    for name in kinds:
        target, sem = getattr(k, name), k.copies.at(k.copies.sem())
        waits[name] = arrival(target, sem)

        def start(name=name, target=target, sem=sem):
            if held is None:
                pltpu.make_async_copy(getattr(k, name + "_whole"), target, sem).start()
                return
            flat, shards, offset = len(target.shape) == 2, 4, offsets[WEIGHTS.index(name)]
            high = target.shape[-2] // (4 * shards if flat else 4)
            for number, places in enumerate(held):
                for piece, (bits, back) in enumerate(places):
                    quarter = k.sec[1] ^ bits
                    shard = lax.rem(k.sec[2] + (shards - back), shards)
                    at = quarter * high
                    if flat:
                        at = at + shard * (4 * high)
                    rows = pl.ds(pl.multiple_of(at, high), high)
                    place = target.at[rows, :] if flat else target.at[shard, rows, :]
                    source = getattr(k, f"pieces_{number}").at[piece, pl.ds(offset, high), :]
                    pltpu.make_async_copy(source, place, sem).start()

        pl.when(wanted)(start)
    return waits


def window_rows(w):
    return slice(w * SLOT, (w + 1) * SLOT)


def wanted(k, name):
    return k.sec[0] == 0 if name in KEPT else k.sec[0] >= 0


def result(k, name, cols=None):
    def make(b, sem):
        src = getattr(k, name)
        src = src.at[0, b] if name in KEPT else src.at[b]
        dst = getattr(k, name + "_o").at[b]
        if cols is not None:
            src, dst = src.at[:, cols], dst.at[:, cols]
        return pltpu.make_async_copy(src, dst, sem)

    return make


def forward_part(k, wins, wait, b):
    x, qkv, prob, mid, gp = (getattr(k, name).at[0, b] for name in ("x", "qkv", "prob", "mid", "gp"))
    a, ctx, n2, act, y = (getattr(k, name).at[b] for name in ("a", "ctx", "n2", "act", "y"))
    ship = lambda name, cols=None: k.copies.ship(b, result(k, name, cols), lambda: wanted(k, name))

    @pl.when(k.sec[0] == 0)
    def _():
        x[...] = k.pin[b]

    if k.landed:

        @pl.when(k.sec[0] == 1)
        def _():
            joined = jnp.concatenate([k.p_main[b], k.p_row[b], k.p_col[b], k.p_cor[b]], axis=0)
            x[...] = mm(k.put[...], joined).astype(BF)

    for w in range(wins):
        rows = window_rows(w)
        hat, _ = centre(x[rows, :].astype(F32))
        a[rows, :] = (hat * k.vec[0:1, :] + k.vec[1:2, :]).astype(BF)
    ship("x")
    ship("a")
    wait("wq")
    lane = lax.broadcasted_iota(jnp.int32, (1, 512), 1)
    for part in range(3):
        cols = slice(part * 512, (part + 1) * 512)
        factor = jnp.where(lax.rem(lane + part * 512, 384) < GROUP * 32, 32 ** (-0.5), 1.0)
        pr = mm(a[...], k.wq[cols, :], NT) + k.bq[0:1, cols]
        qkv[:, cols] = (pr * factor).astype(BF)
    ship("qkv")
    wait("bias")
    wait("region")
    masks, masks_f = head_masks(BF), head_masks(F32)
    for w in range(wins):
        rows = window_rows(w)
        for g in range(4):
            query = qkv[rows, g * 384 : g * 384 + 128]
            key = qkv[rows, g * 384 + 128 : g * 384 + 256]
            value = qkv[rows, g * 384 + 256 : g * 384 + 384]
            scores = mm(key, spread_heads(query, masks), NT) + k.bias[g] + k.region[w]
            top = jnp.max(scores, axis=0, keepdims=True)
            e = jnp.exp(scores - top)
            low = (e * (1.0 / jnp.sum(e, axis=0, keepdims=True))).astype(BF)
            prob[rows, g * 256 : (g + 1) * 256] = low
            ctx[rows, g * 128 : (g + 1) * 128] = fold_heads(mm(low, value, TN), masks_f).astype(BF)
    ship("prob")
    ship("ctx")
    wait("wo")
    mid[...] = x[...].astype(F32) + (mm(ctx[...], k.wo[...]) + k.vec[2:3, :])
    ship("mid")
    for w in range(wins):
        rows = window_rows(w)
        hat, _ = centre(mid[rows, :])
        n2[rows, :] = (hat * k.vec[3:4, :] + k.vec[4:5, :]).astype(BF)
    ship("n2")
    wait("w1")
    wait("w2")
    parts, _, width = k.w1.shape
    for j in range(parts):
        cols = slice(j * width, (j + 1) * width)
        hidden = mm(n2[...], k.w1[j]) + k.b1[j : j + 1, :]
        phi = 0.5 + 0.5 * lax.erf(hidden * 0.7071067811865476)
        low = (hidden * phi).astype(BF)
        act[:, cols] = low
        gp[:, cols] = (phi + hidden * (jnp.exp(hidden * hidden * -0.5) * 0.3989422804014327)).astype(BF)
        ship("act", cols)
        ship("gp", cols)
    y[...] = (mid[...] + k.vec[5:6, :] + mm(act[...], k.w2[...])).astype(BF)
    ship("y")

    put_partner(k, 0, b, y)

    @pl.when(k.sec[0] == 0)
    def _():
        put_pieces(k, "s_", b, mm(k.pick[...], y[...]).astype(BF))

    @pl.when(k.sec[0] == 1)
    def _():
        put_neighbours(k, 0, b, y)


def put_pieces(k, first, b, joined):
    at = 0
    for name in PIECES:
        ref = getattr(k, first + name)
        ref[b] = joined[at : at + ref.shape[1]]
        at += ref.shape[1]


def put_partner(k, kind, b, result):
    if hasattr(k, "f_pair"):
        k.f_pair[kind % k.f_pair.shape[0], b] = mm(k.give[...], result[...], TN).astype(BF)


def put_neighbours(k, kind, b, result):
    if hasattr(k, "f_up"):
        k.f_up[kind, b] = mm(k.up[...], result[...], TN).astype(BF)
        return
    joined = mm(k.put[...], result[...], TN).astype(BF)
    at = 0
    for name in PIECES:
        ref = getattr(k, "h_" + name)
        ref[kind, b] = joined[at : at + ref.shape[2]]
        at += ref.shape[2]


def norm_back(grad, hat, scale, gain):
    inner = grad * gain
    return scale * (inner - jnp.mean(inner, axis=-1, keepdims=True) - hat * jnp.mean(inner * hat, axis=-1, keepdims=True))


def column_sum(values):
    return jnp.sum(values, axis=0, keepdims=True)


def backward_mlp(k, wins, wait, old, b):
    slot = 1 - k.sec[0]
    gp, mid = k.gp.at[slot, b], k.mid.at[slot, b]
    out_grad, dhs, gm, dmid = k.g.at[b], k.dh.at[b], k.gm.at[b], k.dmid.at[b]
    ship = lambda name, cols=None: k.copies.ship(b, result(k, name, cols), lambda: wanted(k, name))

    @pl.when(k.sec[0] == 0)
    def _():
        joined = jnp.concatenate([k.p_main[b], k.p_row[b], k.p_col[b], k.p_cor[b]], axis=0)
        out_grad[...] = mm(k.pick[...], joined, TN).astype(BF)

    @pl.when(k.sec[0] == 1)
    def _():
        joined = jnp.concatenate([k.c_main[b], k.c_row[b], k.c_col[b], k.c_cor[b]], axis=0)
        out_grad[...] = mm(k.put[...], joined).astype(BF)

    ship("g")
    parts, _, width = k.w1.shape
    wait("w2")
    wait("w1")
    old("gp", b)
    total = None
    for j in range(parts):
        cols = slice(j * width, (j + 1) * width)
        dh = (mm(out_grad[...], k.w2[cols, :], NT) * gp[:, cols].astype(F32)).astype(BF)
        dhs[:, cols] = dh
        k.small[0:1, cols] += column_sum(dh.astype(F32))
        ship("dh", cols)
        part = mm(dh, k.w1[j], NT)
        total = part if total is None else total + part
    k.dn[...] = total
    old("mid", b)
    sums = [0.0] * 4
    for w in range(wins):
        rows = window_rows(w)
        grad = k.dn[rows, :]
        out = out_grad[rows, :].astype(F32)
        hat, scale = centre(mid[rows, :])
        whole = out + norm_back(grad, hat, scale, k.vec[3:4, :])
        dmid[rows, :] = whole
        low = whole.astype(BF)
        gm[rows, :] = low
        for i, term in enumerate((out, low.astype(F32), grad * hat, grad)):
            sums[i] = sums[i] + column_sum(term)
    ship("gm")
    if hasattr(k, "dmid_o"):
        ship("dmid")
    k.small[1:2, 0:512] += sums[0]
    k.small[1:2, 512:1024] += sums[1]
    k.small[2:3, 0:512] += sums[2]
    k.small[2:3, 512:1024] += sums[3]


def backward_attention(k, wins, wait, old, b, reload):
    slot = 1 - k.sec[0]
    qkv, prob, x = k.qkv.at[slot, b], k.prob.at[slot, b], k.x.at[slot, b]
    gm, dmid, dqkv, dx = k.gm.at[b], k.dmid.at[b], k.dqkv.at[b], k.dx.at[b]
    ship = lambda name, cols=None: k.copies.ship(b, result(k, name, cols), lambda: wanted(k, name))
    wait("wo")
    if reload:
        old("gm", b)
    k.dctx[...] = mm(gm[...], k.wo[...], NT).astype(BF)
    old("qkv", b)
    old("prob", b)
    masks, masks_f = head_masks(BF), head_masks(F32)
    for w in range(wins):
        rows = window_rows(w)
        for g in range(4):
            at = g * 384
            query = qkv[rows, at : at + 128]
            key = qkv[rows, at + 128 : at + 256]
            value = qkv[rows, at + 256 : at + 384]
            do = spread_heads(k.dctx[rows, g * 128 : (g + 1) * 128], masks)
            low = prob[rows, g * 256 : (g + 1) * 256]
            p = low.astype(F32)
            dp = mm(value, do, NT)
            ds = (p * (dp - column_sum(p * dp))).astype(BF)
            k.dbias[:, g * 256 : (g + 1) * 256] += ds.astype(F32)
            dv = mm(low, do).astype(BF)
            dk = mm(ds, spread_heads(query, masks)).astype(BF)
            dq = (fold_heads(mm(ds, key, TN), masks_f) * 32 ** (-0.5)).astype(BF)
            dqkv[rows, at : at + 128] = dq
            dqkv[rows, at + 128 : at + 256] = dk
            dqkv[rows, at + 256 : at + 384] = dv
    ship("dqkv")
    wait("wq")
    k.small[3:4, 0:1536] += column_sum(dqkv[...].astype(F32))
    k.dn[...] = mm(dqkv[...], k.wq[...])
    old("x", b)
    if reload:
        old("dmid", b)
    sums = [0.0] * 2
    for w in range(wins):
        rows = window_rows(w)
        grad = k.dn[rows, :]
        hat, scale = centre(x[rows, :].astype(F32))
        dx[rows, :] = (dmid[rows, :] + norm_back(grad, hat, scale, k.vec[0:1, :])).astype(BF)
        sums[0] = sums[0] + column_sum(grad * hat)
        sums[1] = sums[1] + column_sum(grad)
    ship("dx")
    k.small[1:2, 1024:1536] += sums[0]
    k.small[1:2, 1536:2048] += sums[1]
    put_partner(k, 1, b, dx)
    if hasattr(k, "s_main"):

        @pl.when(k.sec[0] == 1)
        def _():
            put_pieces(k, "s_", b, mm(k.put[...], dx[...], TN).astype(BF))
            put_neighbours(k, 1, b, dx)


def loop(count, most, run):
    def once(b, carry):
        run(b)
        return carry

    if most:
        lax.fori_loop(0, count, once, 0)


def step_kernel(wins, held, offsets, counts, mlp, attention, terms, quartered, k):
    k.copies = copies = Copies(k.sems)
    ahead, back = max(counts[:2]), max(counts[2:])
    number = lambda pair: jnp.where(k.sec[0] == 0, pair[0], pair[1])
    forwards, backwards = number(counts[:2]), number(counts[2:])
    kinds = WEIGHTS if ahead else (("w2", "w1") if mlp else ()) + (("wo", "wq") if attention else ())
    loaded = backwards >= (0 if ahead else 1)
    waits = load_weights(k, kinds[:1], held, offsets, loaded)
    if ahead:
        for name in ("bias", "region"):
            copy = pltpu.make_async_copy(getattr(k, name + "_h"), getattr(k, name), copies.at(copies.sem()))
            copy.start()
            waits[name] = copy
    fetched = {}
    if back:
        reload = attention and not mlp
        for name in k.needed:
            first = copies.sem(TOGETHER)

            def fetch(b, name=name, first=first):
                target = getattr(k, name)
                target = target.at[1, b] if name in KEPT else target.at[b]
                return pltpu.make_async_copy(getattr(k, "old_" + name).at[b], target, copies.at(first + b))

            fetched[name] = fetch
            for b in range(back):
                pl.when((k.sec[0] == 0) & (b < backwards))(lambda b=b, fetch=fetch: fetch(b).start())
    waits |= load_weights(k, kinds[1:], held, offsets, loaded)
    targets = tuple(dict.fromkeys(term[3] for term in terms))
    bases = [pltpu.make_async_copy(getattr(k, name + "_b"), getattr(k, name), copies.at(copies.sem())) for name in targets]
    for copy in bases:
        copy.start()

    def all_weights():
        for copy in waits.values():
            copy.wait()

    def old(name, b):
        if name in fetched:
            pl.when(k.sec[0] == 0)(lambda: fetched[name](b).wait())

    def forward(b):
        forward_part(k, wins, lambda name: pl.when(b == 0)(waits[name].wait), b)

    loop(forwards, ahead, forward)
    if ahead:
        pl.when(forwards == 0)(all_weights)
    sent_ahead, copies.sent = copies.sent, []
    if back:
        k.small[...] = jnp.zeros_like(k.small)
        if attention:
            k.dbias[...] = jnp.zeros_like(k.dbias)
        wait = lambda b: (lambda name: None) if ahead else (lambda name: pl.when(b == 0)(waits[name].wait))

        def backward(b):
            if mlp:
                backward_mlp(k, wins, wait(b), old, b)
            if attention:
                backward_attention(k, wins, wait(b), old, b, reload)
            if terms:
                for name in dict.fromkeys(name for term in terms for name in term[:2]):
                    if name in k.needed and name not in ("gm", "dmid"):
                        old(name, b)
                for copy in bases:
                    pl.when(b == 0)(copy.wait)
                add_products(k, terms, b, False)

        loop(backwards, back, backward)
        for copy in bases:
            pl.when(backwards == 0)(copy.wait)
        leaving = [leave(k, name, quartered, copies.at(copies.sem())) for name in targets]
        for copy in leaving:
            copy.wait()
    copies.finish(backwards)
    copies.sent = sent_ahead
    copies.finish(forwards)


SMEM_SPEC = pl.BlockSpec(memory_space=pltpu.SMEM)
HBM_SPEC = pl.BlockSpec(memory_space=pl.ANY)
VMEM_SPEC = pl.BlockSpec(memory_space=pltpu.VMEM)


def shape_of(*shape, dtype=BF):
    return jax.ShapeDtypeStruct(shape, dtype)


def call(kernel, name, ins, outs, scratch, flops, moved):
    names = list(ins) + list(outs) + list(scratch)

    def wrapped(*refs):
        k = Refs()
        for key, ref in zip(names, refs):
            setattr(k, key, ref)
        kernel(k)

    results = pl.pallas_call(
        wrapped,
        grid=(1,),
        out_shape=[shape for shape, _ in outs.values()],
        in_specs=[spec for _, spec in ins.values()],
        out_specs=[spec for _, spec in outs.values()],
        scratch_shapes=list(scratch.values()),
        compiler_params=pltpu.CompilerParams(vmem_limit_bytes=VMEM_LIMIT),
        cost_estimate=pl.CostEstimate(flops=min(flops, 1), bytes_accessed=min(moved, 1), transcendentals=0),
        name=name,
    )(*[array for array, _ in ins.values()])
    return dict(zip(outs, results))


PIECES = ("main", "row", "col", "cor")


def vmem(array):
    return (array, VMEM_SPEC)


def hbm(array):
    return (array, HBM_SPEC)


def run_step(tables, static, landed, counts, groups, old, mlp=True, attention=True, terms=(), base=None, quartered=False):
    sources, held, offsets, shapes = static["weights"]
    rows, wide = tables.rows, shapes[2][0] * shapes[2][2]
    ahead, back = max(counts[:2]), max(counts[2:])
    one = lambda array, index: (array, pl.BlockSpec((TOGETHER,) + array.shape[1:], lambda i: (index, 0, 0)))
    ins = {"sec": (static["sec"], SMEM_SPEC), "put": vmem(static["put"]), "pick": vmem(static["pick"]), "vec": vmem(static["vec"])}
    if landed is not None and (ahead or mlp):
        for name, piece in zip(PIECES, landed):
            ins["p_" + name] = vmem(piece)
    kinds = WEIGHTS if ahead else (("w1", "w2") if mlp else ()) + (("wq", "wo") if attention else ())
    outs, scratch = {}, {}
    for name, shape in zip(WEIGHTS, shapes):
        if name in kinds:
            scratch[name] = pltpu.VMEM(shape, BF)
            if held is None:
                ins[name + "_whole"] = hbm(sources[WEIGHTS.index(name)])
    if held is not None:
        for number, source in enumerate(sources):
            ins[f"pieces_{number}"] = hbm(source)
    widths = {"gp": (wide, BF), "mid": (512, F32), "qkv": (1536, BF), "prob": (1024, BF), "x": (512, BF)}
    for name, (cols, dtype) in widths.items():
        if ahead or (mlp if name in ("gp", "mid") else attention):
            scratch[name] = pltpu.VMEM((2, TOGETHER, rows, cols), dtype)
    local, passed = {}, {}
    if "give" in static and (ahead or attention):
        ins["give"] = vmem(static["give"])
        many = (2, TOGETHER) if ahead else (1, back)
        outs["f_pair"] = (shape_of(*many, static["give"].shape[1], 512), VMEM_SPEC)
        if ahead:
            ins["up"] = vmem(static["up"])
            outs["f_up"] = (shape_of(2, TOGETHER, static["up"].shape[1], 512), VMEM_SPEC)
    if ahead:
        ins["pin"] = one(static["pin"], groups[0])
        ins["bq"], ins["b1"] = vmem(static["bq"]), vmem(static["b1"])
        for name in ("bias", "region"):
            ins[name + "_h"] = hbm(static[name])
            scratch[name] = pltpu.VMEM(static[name].shape, F32)
        for name, size in zip(PIECES, tables.sizes):
            outs["s_" + name] = (shape_of(TOGETHER, size, 512), VMEM_SPEC)
            if "give" not in static:
                outs["h_" + name] = (shape_of(2, TOGETHER, size, 512), VMEM_SPEC)
        for name, (cols, dtype) in widths.items():
            outs[name + "_o"] = (shape_of(TOGETHER, rows, cols, dtype=dtype), HBM_SPEC)
        local |= {"a": (512, BF), "ctx": (512, BF), "n2": (512, BF), "act": (wide, BF), "y": (512, BF)}
    if back:
        if mlp:
            for name, target in zip(PIECES, static["targets"]):
                ins["c_" + name] = one(target, groups[1])
            local |= {"g": (512, BF), "dh": (wide, BF), "gm": (512, BF)}
            (passed if attention else local)["dmid"] = (512, F32)
        else:
            passed |= {"gm": (512, BF), "dmid": (512, F32)}
        needed = (("gp", "mid") if mlp else ("gm", "dmid")) + (("qkv", "prob", "x") if attention else ())
        for name in dict.fromkeys(name for term in terms for name in term[:2]):
            if name in AHEAD:
                needed += (name,)
                passed[name] = (old[name + "_o"].shape[2], BF)
        for name in needed:
            ins["old_" + name] = hbm(old[name + "_o"])
        for name, array in (base or {}).items():
            ins[name + "_b"] = hbm(array)
            scratch[name] = pltpu.VMEM(array.shape, BF)
        outs |= leaving_shapes({name: array.shape for name, array in (base or {}).items()}, quartered)
        if attention:
            local |= {"dqkv": (1536, BF), "dx": (512, BF)}
            scratch["dctx"] = pltpu.VMEM((rows, 512), BF)
            outs["dbias"] = (shape_of(SLOT, 1024, dtype=F32), VMEM_SPEC)
        scratch["dn"] = pltpu.VMEM((rows, 512), F32)
        outs["small"] = (shape_of(8, 2048, dtype=F32), VMEM_SPEC)
    for name, (cols, dtype) in local.items():
        outs[name + "_o"] = (shape_of(TOGETHER, rows, cols, dtype=dtype), HBM_SPEC)
        scratch[name] = pltpu.VMEM((TOGETHER, rows, cols), dtype)
    for name, (cols, dtype) in passed.items():
        scratch[name] = pltpu.VMEM((TOGETHER, rows, cols), dtype)
    scratch["sems"] = pltpu.SemaphoreType.DMA((192,))
    passes = 2 * ahead + 2 * back * (mlp + attention)
    kernel = functools.partial(step_kernel, tables.wins, held, offsets, counts, mlp, attention, terms, quartered)

    def run(k):
        k.landed = landed is not None
        k.needed = needed if back else ()
        kernel(k)

    return call(run, "layer_step", ins, outs, scratch, 2 * passes * rows * TOGETHER * 3145728, 20_000_000)


def add_products(k, terms, place, fresh):
    for left, right, cut_left, name, first, rows in terms:
        l, r, t = getattr(k, left).at[place], getattr(k, right).at[place], getattr(k, name)
        parts = t.shape[0]
        for part in range(parts):
            width = (l if cut_left else r).shape[1] // parts
            cols = slice(part * width, (part + 1) * width)
            value = mm(l[:, cols], r[...], TN) if cut_left else mm(l[...], r[:, cols], TN)
            if not fresh:
                value = value + t[part, first : first + rows, :].astype(F32)
            t[part, first : first + rows, :] = value.astype(BF)


def leave(k, name, quartered, sem):
    t = getattr(k, name)
    if not quartered:
        copy = pltpu.make_async_copy(t, getattr(k, name + "_o"), sem)
        copy.start()
        return copy
    keep, send = getattr(k, name + "_k"), getattr(k, name + "_s")
    high = t.shape[1] // 4
    for core in range(2):

        @pl.when(lax.rem(k.sec[1], 2) == core)
        def _(core=core):
            for quarter in range(4):
                place = keep if quarter % 2 == core else send
                pltpu.make_async_copy(t.at[:, pl.ds(quarter * high, high), :], place.at[:, quarter // 2], sem).start()

    return arrival(t, sem)


def leaving_shapes(shapes, quartered):
    outs = {}
    for name, shape in shapes.items():
        if quartered:
            for kind in "ks":
                outs[f"{name}_{kind}"] = (shape_of(shape[0], 2, shape[1] // 4, shape[2]), HBM_SPEC)
        else:
            outs[name + "_o"] = (shape_of(*shape), HBM_SPEC)
    return outs


def weight_grad_kernel(slots, terms, based, k):
    def run(section):
        sems = iter(range(64))
        waits = {}
        for name in dict.fromkeys(name for term in terms for name in term[:2]):
            places, target, sem = slots[name][section], getattr(k, name), k.sems.at[next(sems)]
            rows = getattr(k, f"{name}_{places[0][0]}").shape[1]
            for at, (step, place) in enumerate(places):
                source = getattr(k, f"{name}_{step}").at[place]
                pltpu.make_async_copy(source, target.at[pl.ds(at * rows, rows), :], sem).start()
            waits[name] = arrival(target.at[pl.ds(0, len(places) * rows), :], sem)
            all_rows = pl.ds(0, len(places) * rows)
        if section == 0:
            for name in based:
                waits[name] = pltpu.make_async_copy(getattr(k, name + "_b"), getattr(k, name), k.sems.at[next(sems)])
                waits[name].start()
        leaving = []
        for number, term in enumerate(terms):
            fresh = term[3] not in based or section == 1
            for needed in (term[0], term[1], term[3]):
                if needed in waits:
                    waits.pop(needed).wait()
            add_products(k, (term,), all_rows, fresh)
            if all(term[3] != later[3] for later in terms[number + 1 :]):
                leaving.append(leave(k, term[3], False, k.sems.at[next(sems)]))
        for copy in leaving:
            copy.wait()

    for section in range(2):
        if slots[terms[0][0]][section]:
            pl.when(k.sec[0] == section)(functools.partial(run, section))


def run_weight_grad(static, steps, counted, terms, shapes, base):
    ins = {"sec": (static["sec"], SMEM_SPEC)}
    scratch, slots = {}, {}
    for name in dict.fromkeys(name for term in terms for name in term[:2]):
        shifts = (0, 1) if name in AHEAD else (2, 1)
        slots[name] = [[(at // TOGETHER + shift, at % TOGETHER) for at in count] for count, shift in zip(counted, shifts)]
        for step in sorted({step for places in slots[name] for step, _ in places}):
            array = steps[step][name + "_o"]
            ins[f"{name}_{step}"] = hbm(array)
        most = max(len(places) for places in slots[name])
        scratch[name] = pltpu.VMEM((most * array.shape[1], array.shape[2]), BF)
    for name, shape in shapes.items():
        scratch[name] = pltpu.VMEM(shape, BF)
        if base:
            ins[name + "_b"] = hbm(base[name])
    scratch["sems"] = pltpu.SemaphoreType.DMA((64,))
    kernel = functools.partial(weight_grad_kernel, slots, terms, tuple(base))
    done = call(kernel, "weight_grad", ins, leaving_shapes(shapes, False), scratch, 0, 0)
    return {name: done[name + "_o"] for name in shapes}


def collect(arrays):
    ins = {f"{name}_{i}": vmem(array) for name, members in arrays.items() for i, array in enumerate(members)}
    outs = {name: (shape_of(len(members), *members[0].shape), VMEM_SPEC) for name, members in arrays.items()}

    def kernel(k):
        for name, members in arrays.items():
            for i in range(len(members)):
                getattr(k, name)[i] = getattr(k, f"{name}_{i}")[...]

    return call(kernel, "collect", ins, outs, {}, 0, 4_000_000)


def run_patches(static, plain, mains, halo, sizes):
    rows = plain[0][0].shape[1]
    batches = sum(sizes)
    ins = {"sec": (static["sec"], SMEM_SPEC), "pick": vmem(static["pick"])}
    for group, (pair, main) in enumerate(zip(plain, mains)):
        ins[f"plain_0_{group}"], ins[f"plain_1_{group}"], ins[f"main_{group}"] = vmem(pair[0]), vmem(pair[1]), vmem(main)
    for name, array in zip(PIECES[1:], halo):
        ins[name] = vmem(array)
    outs = {"patch": (shape_of(2 * batches, rows, 512), VMEM_SPEC)}

    def kernel(k):
        for kind in range(2):
            for group, size in enumerate(sizes):
                for b in range(size):
                    at = kind * batches + sum(sizes[:group]) + b

                    @pl.when(k.sec[0] == 0)
                    def _(at=at, kind=kind, group=group, b=b):
                        k.patch[at] = getattr(k, f"plain_{kind}_{group}")[b]

                    @pl.when(k.sec[0] == 1)
                    def _(at=at, kind=kind, group=group, b=b):
                        parts = [getattr(k, f"main_{group}")[kind, b]] + [getattr(k, name)[group, kind, b] for name in PIECES[1:]]
                        k.patch[at] = mm(k.pick[...], jnp.concatenate(parts, axis=0), TN).astype(BF)

    return call(kernel, "patches", ins, outs, {}, 0, 0)


def run_places(static, steps, pairs, ups, own, take, land, sizes, tokens):
    batches, groups = sum(sizes), len(sizes)
    ins = {"sec": (static["sec"], SMEM_SPEC), "own": vmem(own), "take": vmem(take), "land_0": vmem(land[0]), "land_1": vmem(land[1])}
    for step, done in enumerate(steps):
        for name in ("y_o", "dx_o"):
            if name in done:
                ins[f"{name}_{step}"] = vmem(done[name])
        ins[f"pair_{step}"] = vmem(pairs[step])
        for side, array in enumerate(ups[step]):
            ins[f"up_{side}_{step}"] = vmem(array)
    outs = {"first": (shape_of(batches, tokens, 512), VMEM_SPEC), "second": (shape_of(batches, tokens, 512, dtype=F32), VMEM_SPEC)}

    def kernel(k):
        for kind, name in enumerate(("y_o", "dx_o")):
            for group, size in enumerate(sizes):
                for b in range(size):
                    at = sum(sizes[:group]) + b

                    def put(value, at=at, kind=kind):
                        if kind == 0:
                            k.first[at] = value.astype(BF)
                        else:
                            k.second[at] = value

                    def here(step, kind=kind, name=name, b=b):
                        value = mm(k.own[...], getattr(k, f"{name}_{step}")[b], TN)
                        return value + mm(k.take[...], getattr(k, f"pair_{step}")[kind % pairs[step].shape[0], b], TN)

                    @pl.when(k.sec[0] == 0)
                    def _(group=group, kind=kind, put=put, here=here):
                        put(here(group + 2 * kind))

                    @pl.when(k.sec[0] == 1)
                    def _(group=group, kind=kind, b=b, put=put, here=here):
                        value = here(group + 1)
                        for side in range(2):
                            value = value + mm(getattr(k, f"land_{side}")[...], getattr(k, f"up_{side}_{group + 1}")[kind, b], TN)
                        put(value)

    return call(kernel, "places", ins, outs, {}, 0, 0)


def table_onehot():
    code = np.full((SLOT, SLOT), -1, np.int32)
    for u in range(TOKENS):
        for t in range(TOKENS):
            code[u, t] = (t // WIN - u // WIN + WIN - 1) * (2 * WIN - 1) + t % WIN - u % WIN + WIN - 1
    side = (2 * WIN - 1) ** 2
    return (jnp.arange(side, dtype=jnp.int32)[:, None] == jnp.asarray(code.reshape(1, -1))).astype(F32)


def region_mask(layout, section):
    row, mp = lax.axis_index(ROW), lax.axis_index(MP)
    window_row = row * WROWS + mp // layout.across
    window_col = (mp % layout.across) * layout.wins + jnp.arange(layout.wins)
    place = jnp.arange(SLOT)
    row_label = jnp.where(window_row == layout.high - 1, 1 + (place // WIN >= WIN - SHIFT).astype(jnp.int32), 0)
    col_label = jnp.where(
        (window_col == WCOLS - 1)[:, None], 1 + (place % WIN >= WIN - SHIFT).astype(jnp.int32)[None], 0
    )
    labels = 3 * row_label[None] + col_label
    differs = labels[:, :, None] != labels[:, None, :]
    term = jnp.where(differs & (section == 1), -100.0, 0.0).astype(F32)
    return jnp.tile(term, (1, 1, GROUP))


def full_patches(layout, mp, tokens):
    wins = layout.wins
    place = jnp.arange(wins * SLOT)
    window, inner = place // SLOT, place % SLOT
    row = (mp // layout.across) * WIN + inner // WIN
    col = ((mp % layout.across) * wins + window) * WIN + inner % WIN
    token = jnp.where(inner < TOKENS, row * (WCOLS * WIN) + col, -1)
    return (token[:, None] == jnp.arange(tokens)[None]).astype(BF)


def whole_patches(layout, mp, tokens_here):
    token = mp * tokens_here + jnp.arange(tokens_here)
    row, col = token // (WCOLS * WIN), token % (WCOLS * WIN)
    window = col // WIN
    owner = (row // WIN) * layout.across + window // layout.wins
    place = owner * layout.wins * SLOT + (window % layout.wins) * SLOT + (row % WIN) * WIN + col % WIN
    return (place[:, None] == jnp.arange(layout.mp_count * layout.wins * SLOT)[None]).astype(BF)


def low_dot(matrix, stack):
    return jnp.einsum("pr,nrd->npd", matrix, stack, preferred_element_type=F32).astype(BF)


def body(
    layer_input,
    out_cotangent,
    norm_one_gain,
    norm_one_bias,
    attend_weight,
    attend_bias,
    position_table,
    output_weight,
    output_bias,
    norm_two_gain,
    norm_two_bias,
    expand_weight,
    expand_bias,
    reduce_weight,
    reduce_bias,
):
    row_count, mp_count = lax.axis_size(ROW), lax.axis_size(MP)
    section, mp = lax.axis_index(SECTION), lax.axis_index(MP)
    layout = Layout(row_count, mp_count)
    tables = Tables(layout.wins)
    put = jnp.asarray(tables.put, BF)
    pick = jnp.asarray(tables.pick, BF)
    batches, tokens_here, width = layer_input.shape
    heads_here = attend_weight.shape[2]
    hidden_here = expand_weight.shape[2]
    row = lax.axis_index(ROW)
    sec = jnp.stack([section, row, mp]).astype(jnp.int32)
    paired = layout.across == 2 and row_count == 4
    first = section == 0

    flat = jnp.concatenate([attend_bias[0].reshape(-1), position_table[0].reshape(-1), expand_bias[0].reshape(-1)])
    wq_rows = attend_weight[0].transpose(1, 2, 0).reshape(heads_here, 3, 32, width)
    if paired:
        quarter = lambda array: take_at(array.reshape(4, -1, width), row)
        shards = (wq_rows.transpose(1, 0, 2, 3), output_weight[0], expand_weight[0], reduce_weight[0])
        quarters = [quarter(array) for array in shards]
        offsets = np.cumsum([0] + [array.shape[0] for array in quarters])[:-1].tolist()
        here = jnp.concatenate(quarters)
        near, far = ring(here, MP), ring(here, MP, -1)
        further = ring(near, MP)
        across = lambda piece: swap(piece, ROW, 2)
        crossed = [across(here), across(near), across(far)]
        after = ring(flat, MP)
        flat_all = natural_ring([flat, after, ring(after, MP), ring(flat, MP, -1)], mp)
    else:
        wq_all = lax.all_gather(wq_rows, MP, axis=0).reshape(4, GROUP, 3, 32, width).transpose(0, 2, 1, 3, 4)
        wq_all = wq_all.reshape(4 * GROUP * 96, width)
        wo_all = lax.all_gather(output_weight[0], MP, axis=0).reshape(-1, width)
        w1_all = lax.all_gather(expand_weight[0], MP, axis=0)
        w2_all = lax.all_gather(reduce_weight[0], MP, axis=0).reshape(-1, width)
        flat_all = lax.all_gather(flat, MP, axis=0)
        whole = (wq_all, wo_all, w1_all, w2_all)
        weights = (whole, None, None, tuple(array.shape for array in whole))
    cut_one = heads_here * 64
    cut_two = cut_one + heads_here * position_table.shape[2]
    bias_all = flat_all[:, :cut_one].reshape(4, GROUP, 2, 32)
    table_all = flat_all[:, cut_one:cut_two].reshape(-1, position_table.shape[2])
    b1 = flat_all[:, cut_two:]
    bq = jnp.stack([bias_all[:, :, 0], jnp.zeros_like(bias_all[:, :, 0]), bias_all[:, :, 1]], axis=1).reshape(1, -1)
    onehot = table_onehot()
    bias = jnp.dot(table_all, onehot, precision=highest).reshape(4, GROUP, SLOT, SLOT).transpose(0, 2, 1, 3)
    bias = bias.reshape(4, SLOT, GROUP * SLOT) + jnp.where(jnp.arange(SLOT) < TOKENS, 0.0, -1e30)[None, :, None]
    vec = jnp.concatenate(
        [norm_one_gain, norm_one_bias, output_bias, norm_two_gain, norm_two_bias, reduce_bias, jnp.zeros((2, width), F32)]
    )
    region = region_mask(layout, section)

    taken = jnp.where(first, layer_input, out_cotangent)
    if paired:
        keep, take, send = pair_tables(layout.wins)
        side = mp % 2
        keep = lax.dynamic_index_in_dim(jnp.asarray(keep, BF), side, 0, keepdims=False)
        take = lax.dynamic_index_in_dim(jnp.asarray(take, BF), side, 0, keepdims=False)
        send = jnp.asarray(send, BF)
        arrived = swap(low_dot(send, taken), MP, 1)
        pin = low_dot(jnp.concatenate([keep, take], axis=1), jnp.concatenate([taken, arrived], axis=1))
        own, give, take, up, land = (jnp.asarray(table, BF) for table in placing_tables(layout.wins))
        own, give, take = (take_at(take_at(table, section), side) for table in (own, give, take))
        land = jnp.where((section == 1) & (side == 0), land, 0)
    else:
        everything = lax.all_gather(taken, MP, axis=1, tiled=True)
        pin = low_dot(full_patches(layout, mp, everything.shape[1]), everything)
    groups = -(-batches // TOGETHER)
    sizes = [min(TOGETHER, batches - TOGETHER * group) for group in range(groups)]
    pin = jnp.pad(pin, ((0, TOGETHER * groups - batches), (0, 0), (0, 0)))
    cuts = np.cumsum(tables.sizes)[:-1].tolist()
    targets = halo_inside(layout, jnp.split(low_dot(pick, pin), cuts, axis=1), False)
    if paired:
        further, pin, bias, region, bq, b1 = lax.optimization_barrier((further, pin, bias, region, bq, b1))
        arrays = [jnp.stack([here, near, crossed[0], crossed[1]]), jnp.stack([far, further, crossed[2], across(further)])]
        held = (((0, 0), (0, 1), (2, 0), (2, 1)), ((0, 3), (0, 2), (2, 3), (2, 2)))
        arrays[1], targets = lax.optimization_barrier((arrays[1], targets))
        held += tuple(tuple((bits + 1, back) for bits, back in places) for places in held)
        weights = (
            arrays + [swap(array, ROW, 1) for array in arrays],
            held,
            offsets,
            ((4 * GROUP * 96, width), (4 * GROUP * 32, width), (mp_count, width, hidden_here), (mp_count * hidden_here, width)),
        )

    static = dict(
        sec=sec, weights=weights, pin=pin, targets=targets, put=put, pick=pick, vec=vec, bq=bq, b1=b1, bias=bias, region=region
    )
    if paired:
        static |= dict(give=give, up=up)
    size_of = lambda group: sizes[group] if 0 <= group < groups else 0
    landed = None
    steps, pairs, ups = [], [], []
    mlp_terms = (("act", "g", True, "d2", 0, hidden_here), ("n2", "dh", False, "d1", 0, width))
    heads_terms = (("dqkv", "a", True, "da", 0, GROUP * 96), ("ctx", "gm", True, "da", GROUP * 96, GROUP * 32))
    terms = mlp_terms + heads_terms
    shapes = {"d2": (mp_count, hidden_here, width), "d1": (mp_count, width, hidden_here), "da": (4, GROUP * 128, width)}
    early, ready = TOGETHER * (groups - 1), max(TOGETHER * (groups - 2), 0)
    grads_base = {}
    for step in range(groups + 1):
        counts = (size_of(step), size_of(step - 1), size_of(step - 2), size_of(step - 1))
        which = (min(step, groups - 1), max(step - 1, 0))
        done = run_step(tables, static, landed, counts, which, steps[max(step - 2, 0)] if step else None)
        steps.append(done)
        sends = [done["s_" + name] for name in PIECES]
        pair, up_piece = done.get("f_pair"), done.get("f_up")
        if step == groups:
            sends = [piece[: sizes[-1]] for piece in sends]
        if paired:
            sends, pairs, ups = lax.optimization_barrier((sends, pairs, ups))
        if step == groups - 1 and ready:
            grads_base = run_weight_grad(static, steps, (range(ready), ()), terms, shapes, {})
            sends, grads_base = lax.optimization_barrier((sends, grads_base))
        landed = halo_swap(layout, sends, step == groups)
        if paired:
            if step == groups:
                break
            landed, pair, up_piece = lax.optimization_barrier((landed, pair, up_piece))
            pairs = pairs + [swap(pair, MP, 1)]
            ups = ups + [[lax.ppermute(up_piece, AXES, route) for route in layout.up_routes()] if step else []]

    if not paired:
        halo = collect({name: [done["h_" + name] for done in steps[1:]] for name in PIECES[1:]})
        halo = [halo[name] for name in PIECES[1:]]
        flat_halo = halo_inside(layout, [None] + [array.reshape((-1,) + array.shape[3:]) for array in halo], True)[1:]
        halo = [flat.reshape(array.shape) for flat, array in zip(flat_halo, halo)]

    grads_base = run_weight_grad(static, steps, (range(ready, early), range(batches)), terms, shapes, grads_base)
    landed, grads_base = lax.optimization_barrier((landed, grads_base))
    after = sec
    if paired:
        grads_base, pair, up_piece = lax.optimization_barrier((grads_base, pair, up_piece[:, : sizes[-1]]))
        pairs = pairs + [swap(pair, MP, 1)]
        ups = ups + [[lax.ppermute(up_piece, AXES, route) for route in layout.up_routes()]]
    mlp_base = {name: grads_base[name] for name in ("d2", "d1")}
    heads_base = {"da": grads_base["da"]}

    counts = (0, 0, sizes[-1], 0)
    which = (groups - 1, groups - 1)
    old = steps[-2]
    last = run_step(
        tables, static, landed, counts, which, old, attention=False, terms=mlp_terms, base=mlp_base, quartered=paired
    )
    if paired:
        last, pairs, ups = lax.optimization_barrier((last, pairs, ups))
        d2, d1 = (last[name + "_k"] + swap(last[name + "_s"], ROW, 1) for name in ("d2", "d1"))
        after, d2, d1 = lax.optimization_barrier((sec, d2, d1))
    heads = run_step(
        tables, dict(static, sec=after), None, counts, which, {**old, **last}, mlp=False, terms=heads_terms, base=heads_base, quartered=paired
    )
    smalls = [done["small"] for done in steps[1:] + [last, heads]]
    biases = [done["dbias"] for done in steps[1:] + [heads]]
    steps.append({**last, **heads})
    def summed(smalls, biases):
        small = sum(smalls)[:4]
        table = sum(biases).reshape(SLOT, 4 * GROUP, SLOT).transpose(1, 0, 2).reshape(4 * GROUP, -1)
        table = jnp.dot(table, onehot.T, precision=highest)
        flat = jnp.pad(table.reshape(-1), (0, -table.size % 2048)).reshape(-1, 2048)
        return jnp.concatenate([small, flat])

    if paired:
        high, core = row // 2, row % 2
        gate = lax.optimization_barrier
        term = lambda part, step: take_at(part, (mp - 2 - step) % mp_count)

        def joined(pair, crossed):
            whole = jnp.stack([jnp.where(core == 0, pair, crossed), jnp.where(core == 0, crossed, pair)], axis=1)
            return whole.astype(F32).reshape(-1, width)

        def around(array, axis):
            return [swap(array, axis, bits) for bits in (1, 2, 3)]

        def in_pairs(array, came):
            return (array + came[0]) + (came[1] + came[2])

        def ordered(mine, other):
            return jnp.stack([jnp.where(high == 0, mine, other), jnp.where(high == 0, other, mine)])

        d2_came, d1_came = ring(take_at(d2, (mp - 1) % mp_count), MP), swap(take_at(d1, 1 - high, 1), ROW, 2)
        d2_came, d1_came, sending = gate((d2_came, d1_came, heads["da_s"]))
        da_came, pair_came = swap(sending, ROW, 1), lax.ppermute(heads["f_pair"], AXES, layout.pair_route(0))
        d2_total, d1 = d2_came + term(d2, 0), take_at(d1, high, 1) + d1_came
        d2_came, d1_came = ring(d2_total, MP), ring(take_at(d1, (mp - 1) % mp_count), MP)
        da = heads["da_k"] + da_came
        mine, other = take_at(da, high, 1), take_at(da, 1 - high, 1)
        da_came = swap(other, ROW, 2)
        d1_came, _ = gate((d1_came, other))
        sending = d1_came + term(d1, 0)
        d1_came = ring(sending, MP)
        pair_came, _ = gate((pair_came, sending))
        placed = run_places(static, steps, pairs + [pair_came], ups + [[]], own, take, land, sizes, tokens_here)
        da_came, first_out, second_out = gate((da_came, placed["first"], placed["second"]))
        da = mine + da_came
        sending = take_at(da, (mp - 1) % mp_count)
        da_came = ring(sending, MP)
        d2_came, d1_came, smalls, biases, _ = gate((d2_came, d1_came, smalls, biases, sending))
        d2_total, d1_total = d2_came + term(d2, 1), d1_came + term(d1, 1)
        d2_came, d1_came = ring(d2_total, MP), ring(d1_total, MP)
        sums = summed(smalls, biases)
        sending = da_came + term(da, 0)
        da_came = ring(sending, MP)
        d2_came, d1_came, sums, _ = gate((d2_came, d1_came, sums, sending))
        d2, d1 = d2_came + term(d2, 2), d1_came + term(d1, 2)
        d2_came, d1_came, sums_came = swap(d2, ROW, 2), swap(d1, ROW, 2), around(sums, ROW)
        sending = da_came + term(da, 1)
        da_came = ring(sending, MP)
        d2_came, d1_came, sums_came, _ = gate((d2_came, d1_came, sums_came, sending))
        d2, d1, sums = d2 + d2_came, ordered(d1, d1_came), in_pairs(sums, sums_came)
        d2_came, d1_came, sums_came = swap(d2, ROW, 1), swap(d1, ROW, 1), around(sums, MP)
        da = da_came + term(da, 2)
        da_came = swap(da, ROW, 2)
        d2_came, d1_came, _ = gate((d2_came, d1_came, da))
        d2, d1 = joined(d2, d2_came), joined(d1, d1_came)
        da = ordered(da, da_came)
        da_came = swap(da, ROW, 1)
        sums_came, _ = gate((sums_came, da))
        sums = in_pairs(sums, sums_came)
        da = joined(da, da_came)
        dq, do = da[: GROUP * 96].reshape(3, GROUP, 32, width), da[GROUP * 96 :]
        dq = dq.transpose(3, 1, 0, 2).reshape(attend_weight.shape[1:])
    else:

        def shared(parts):
            part = lax.psum_scatter(parts, MP, scatter_dimension=0, tiled=False)
            return lax.psum(part, ROW).astype(F32)

        da = heads["da_o"]
        dq = da[:, : GROUP * 96].reshape(4, 3, GROUP, 32, width).transpose(0, 2, 1, 3, 4).reshape(mp_count, heads_here * 96, width)
        d2, d1, do = shared(last["d2_o"]), shared(last["d1_o"]), shared(da[:, GROUP * 96 :].reshape(mp_count, heads_here * 32, width))
        dq = shared(dq).T.reshape(attend_weight.shape[1:])
        sums = lax.psum(summed(smalls, biases), (ROW, MP))
    small = sums[:4]
    table = sums[4:].reshape(-1)[: 4 * GROUP * onehot.shape[0]].reshape(4 * GROUP, -1)
    shift = small[3, :1536].reshape(4, 3, GROUP, 32)
    shift = jnp.concatenate([shift[:, 0], shift[:, 2]], axis=-1).reshape(4 * GROUP, 64)
    mine = lambda array: lax.dynamic_index_in_dim(array.reshape((mp_count, -1) + array.shape[1:]), mp, 0, keepdims=False)

    if not paired:
        plain = [(steps[group]["y_o"], steps[group + 2]["dx_o"]) for group in range(groups)]
        mains = [steps[group + 1]["h_main"] for group in range(groups)]
        made = run_patches(static, plain, mains, halo, sizes)
        everything = lax.all_gather(made["patch"], MP, axis=1, tiled=True)
        placed = low_dot(whole_patches(layout, mp, tokens_here), everything)
        first_out, second_out = placed[:batches], placed[batches:].astype(F32)

    return (
        first_out[None],
        second_out[None],
        small[1, 1024:1536][None],
        small[1, 1536:2048][None],
        dq[None],
        mine(shift)[None],
        mine(table)[None],
        do.reshape(output_weight.shape),
        small[1, 512:1024][None],
        small[2, 0:512][None],
        small[2, 512:1024][None],
        d1[None],
        mine(small[0])[None],
        d2[None],
        small[1, 0:512][None],
    )


def solution(mesh):
    return jax.shard_map(
        body,
        mesh=mesh,
        in_specs=(
            P(None, (ROW, MP), None),
            P(None, (ROW, MP), None),
            P(SECTION, None),
            P(SECTION, None),
            P(SECTION, None, MP, None),
            P(SECTION, MP, None),
            P(SECTION, MP, None),
            P(SECTION, MP, None, None),
            P(SECTION, None),
            P(SECTION, None),
            P(SECTION, None),
            P(SECTION, None, MP),
            P(SECTION, MP),
            P(SECTION, MP, None),
            P(SECTION, None),
        ),
        out_specs=(
            P(SECTION, None, (ROW, MP), None),
            P(SECTION, None, (ROW, MP), None),
            P(SECTION, None),
            P(SECTION, None),
            P(SECTION, None, MP, None),
            P(SECTION, MP, None),
            P(SECTION, MP, None),
            P(SECTION, MP, None, None),
            P(SECTION, None),
            P(SECTION, None),
            P(SECTION, None),
            P(SECTION, None, MP),
            P(SECTION, MP),
            P(SECTION, MP, None),
            P(SECTION, None),
        ),
        check_vma=False,
    )
```
